256 devices in a mesh: dp: 128 (over y, x, z), rep: 2 (over core).
Axes of the slice: x: 4, y: 4, z: 8, core: 2. Of those that a mesh axis runs over, the one named last changes fastest.
Arguments:
- dense_feats: bfloat16 [65536, 256], P(('dp', 'rep')), may hold values from -6 to 6
- bottom_weight: bfloat16 [256, 128], replicated, may hold values from -0.375 to 0.375
- top_weight: bfloat16 [479, 1024], replicated, may hold values from -0.25 to 0.25
- out_weight: bfloat16 [1024], replicated, may hold values from -0.1875 to 0.1875
- hot_table: bfloat16 [4096, 128], replicated, may hold values from -1.796875 to 1.796875
- cold_table: bfloat16 [524288, 128], P('dp'), may hold values from -1.796875 to 1.796875
- hot_index: int32 [65536, 13], P(('dp', 'rep')), may hold values from 0 to 4095
- cold_owner: int32 [65536, 13], P(('dp', 'rep')), may hold values from 0 to 127, all different within a row; in each aligned block of 256 rows (0 to 255, 256 to 511, ...) at most 52 rows name the same one
- cold_row: int32 [65536, 13], P(('dp', 'rep')), may hold values from 0 to 4095
- clicks: int32 [65536], P(('dp', 'rep')), may hold values from 0 to 1
Outputs:
- hot_grad: float32 [4096, 128], replicated
- cold_grad: float32 [524288, 128], P('dp')
- top_grad: float32 [479, 1024], replicated
The draws below stay inside these ranges and needn't reach their ends.
Inputs may be any that keep to these rules, and one draw needn't show every extreme that they name: `cold_owner`: each sample names 13 different owners. Among the samples of one device no owner is named by more than 52 samples, and on some device some owner is named by exactly 52.
All inputs are finite; a program needn't handle non-finite values.
Results may differ from the reference program's by a relative error of at most 0.0061.
Values may be sent and summed in bfloat16 or wider, within the bound.
A program may use at most 64 MiB of HBM per device.

```python
import math
import jax
import jax.numpy as jnp
import numpy as np
from jax import lax

E = 128
HID = 1024
BOT_IN = 256
FH = 13
FC = 13
HOT = 4096
ROWS_DEV = 4096
B_DEV = 256
NI = 479
CAP = 52
SAMPLES = 65536
COLD = 524288
N_DP = 128


def draw_clicks(key, part):
    key = jax.random.fold_in(key, 7)
    level_key, pick_key = jax.random.split(key)
    blocks = SAMPLES // B_DEV
    level = jax.random.randint(level_key, (blocks, 1), 0, 9)
    picks = jax.random.randint(pick_key, (blocks, B_DEV), 0, 8)
    return (picks < level).astype(jnp.int32).reshape(SAMPLES)


def plant(values, rng, smallest, largest):
    dims = values.shape
    index_at = [jax.random.randint(jax.random.fold_in(rng, axis), (), 0, dims[axis]) for axis in range(len(dims))]
    values = values.at[tuple(index_at)].set(smallest)
    longest = dims.index(max(dims))
    index_at[longest] = (index_at[longest] + 1) % dims[longest]
    return values.at[tuple(index_at)].set(largest)


def steps_of(key, shape, cuts, least, high):
    level, own = 1.0, jax.random.fold_in(key, 6)
    for position, shards_of in cuts:
        draws = jnp.exp(jax.random.uniform(jax.random.fold_in(own, position), (shards_of,), jnp.float32, least / len(cuts), high / len(cuts)))
        level = level * jnp.repeat(draws, shape[position] // shards_of).reshape([-1 if axis == position else 1 for axis in range(len(shape))])
    return level


def cumulative_ranks(count, lean):
    weights = [(1 << 20) // math.isqrt(rank ** lean) + 1 for rank in range(1, count + 1)]
    deviation = 1 + sum(weights) // (1 << 30)
    return np.cumsum(np.array([max(1, weight // deviation) for weight in weights]))


def skewed_ids(rng, extent, amount, skew):
    table = cumulative_ranks(amount, skew)
    pick = jax.random.randint(jax.random.fold_in(rng, 1), extent, 0, int(table[amount - 1]))
    standing = jnp.searchsorted(jnp.asarray(table, jnp.int32), pick, side="right")
    return jax.random.permutation(jax.random.fold_in(rng, 2), amount)[standing].astype(jnp.int32)


def deal_out(rng, own, number, rows, number_of, top, bound, slope):
    sequence = jax.random.permutation(rng, number_of)
    heavy_load, usual = load_shares(number_of, rows * top, bound, slope, True), load_shares(number_of, rows * top, bound, slope, False)
    places = jnp.arange(number_of)

    def named(sizes, rotation):
        used = int((sizes > 0).sum())
        fixed = max(1, used // 4)
        passed = fixed + (places - fixed + rotation * (used - fixed)) % max(1, number_of - fixed)
        return jnp.zeros((number_of,), jnp.int32).at[sequence[jnp.where(places < fixed, places, passed)]].set(jnp.asarray(sizes, jnp.int32))

    sizes = jnp.where(number % 4 == 0, named(heavy_load, number // 4), named(usual, number - number // 4 - 1))
    mixed = jax.random.permutation(jax.random.fold_in(own, 3), number_of)
    giver, sink = mixed[0:number_of // 2 * 2:2], mixed[1:number_of // 2 * 2:2]
    margin = jnp.minimum(sizes[giver] - 1, bound - sizes[sink]) // 2
    margin = jnp.where((giver == sequence[0]) | (sink == sequence[0]) | (sizes[sink] == 0), 0, jnp.maximum(margin, 0))
    passed = jax.random.randint(jax.random.fold_in(own, 4), (number_of // 2,), 0, 1 << 20) % (margin + 1)
    sizes = sizes.at[giver].add(-passed).at[sink].add(passed)
    items = jnp.searchsorted(jnp.cumsum(sizes), jnp.arange(rows * top), side="right").astype(jnp.int32)
    listing = items.reshape(top, rows).T
    listing = listing[jax.random.permutation(jax.random.fold_in(own, 1), rows)]
    rotation = jax.random.randint(jax.random.fold_in(own, 2), (rows, 1), 0, top)
    return jnp.take_along_axis(listing, (jnp.arange(top)[None, :] + rotation) % top, axis=1)


def load_shares(amount, total, bound, skew, full):
    loads = [(1 << 20) // math.isqrt(grade ** skew) + 1 for grade in range(1, amount + 1)]
    largest = bound if full else min(bound, max(-(-total // amount), total * loads[0] // sum(loads)))
    least = 1 if total - largest >= amount - 1 else 0
    holding, spare = [largest] + [least] * (amount - 1), total - largest - least * (amount - 1)
    while spare > 0:
        candidates = [i for i in range(1, amount) if holding[i] < largest] or [i for i in range(1, amount) if holding[i] < bound]
        mass, budget = sum([loads[i] for i in candidates]), spare
        for i in candidates:
            more = min(bound - holding[i], max(1, budget * loads[i] // mass), spare)
            holding[i] = holding[i] + more
            spare = spare - more
    return np.array(holding)


def bell_draw(rng, dims, width, bound, pieces=(), dtype=jnp.bfloat16):
    factor_of = steps_of(rng, dims, pieces, -0.22, 0.18) if pieces else 1.0
    result = jax.random.normal(rng, dims, jnp.float32) * width * factor_of
    return jnp.minimum(jnp.maximum(result, -bound), bound).astype(dtype)


def setup_inputs(seed: int = 0) -> dict:
    streams_of = jax.random.split(jax.random.key(seed), 11)
    dense_feats = bell_draw(streams_of[0], (SAMPLES, BOT_IN), 1.0, 6.0, ((0, 256),))
    bottom_weight = bell_draw(streams_of[1], (BOT_IN, E), BOT_IN ** -0.5, 0.375)
    top_weight = bell_draw(streams_of[2], (NI, HID), NI ** -0.5, 0.25)
    out_weight = bell_draw(streams_of[3], (HID,), HID ** -0.5, 0.1875)
    hot_table = bell_draw(streams_of[4], (HOT, E), 0.3, 1.796875)
    cold_table = bell_draw(streams_of[5], (COLD, E), 0.3, 1.796875, ((0, 128),))
    hot_index = plant(skewed_ids(streams_of[6], (SAMPLES, FH), HOT, 1), jax.random.fold_in(streams_of[6], 3), 0, HOT - 1).astype(jnp.int32)
    cold_owner_keys = jax.random.split(jax.random.fold_in(streams_of[7], 1), SAMPLES // B_DEV)
    cold_owner_turns = jax.random.permutation(jax.random.fold_in(streams_of[7], 3), SAMPLES // B_DEV)
    cold_owner = jax.vmap(lambda own, number: deal_out(jax.random.fold_in(streams_of[7], 2), own, number, B_DEV, N_DP, FC, CAP, 2))(cold_owner_keys, cold_owner_turns).reshape((SAMPLES, FC))
    cold_row = plant(jax.random.randint(streams_of[8], (SAMPLES, FC), 0, ROWS_DEV), jax.random.fold_in(streams_of[8], 1), 0, ROWS_DEV - 1).astype(jnp.int32)
    clicks = draw_clicks(jax.random.fold_in(streams_of[10], 71), 0)
    return dict(dense_feats=dense_feats, bottom_weight=bottom_weight, top_weight=top_weight, out_weight=out_weight, hot_table=hot_table, cold_table=cold_table, hot_index=hot_index, cold_owner=cold_owner, cold_row=cold_row, clicks=clicks)


def pair_tables(fields):
    lower_row, lower_col = np.tril_indices(fields, -1)
    picked = lower_row * fields + lower_col
    spread = np.zeros((picked.shape[0], fields * fields), np.float32)
    spread[np.arange(picked.shape[0]), picked] = 1.0
    spread[np.arange(picked.shape[0]), lower_col * fields + lower_row] = 1.0
    return (picked, spread)

def gelu_tanh(values):
    return jax.nn.gelu(values, approximate=True)

def reference(dense_feats, bottom_weight, top_weight, out_weight, hot_table, cold_table, hot_index, cold_owner, cold_row, clicks):
    fields = 1 + FH + FC
    picked, spread = pair_tables(fields)
    spread_table = jnp.asarray(spread).astype(jnp.bfloat16)
    blocks = SAMPLES // B_DEV
    global_row = (cold_owner * ROWS_DEV + cold_row).astype(jnp.int32)
    dense_blocks = dense_feats.reshape(blocks, B_DEV, BOT_IN)
    hot_blocks = hot_index.reshape(blocks, B_DEV, FH)
    cold_blocks = global_row.reshape(blocks, B_DEV, FC)
    click_blocks = clicks.reshape(blocks, B_DEV)

    def accumulate(totals, sample_block):
        hot_total, cold_total, top_total = totals
        dense_rows, hot_ids, cold_ids, click_rows = sample_block
        bottom = jnp.maximum(jnp.dot(dense_rows, bottom_weight, preferred_element_type=jnp.float32), 0.0).astype(jnp.bfloat16)
        stacked = jnp.concatenate([bottom[:, None, :], hot_table[hot_ids], cold_table[cold_ids]], axis=1)
        stack_wide = stacked.astype(jnp.float32)
        pair_dots = jnp.einsum('bie,bje->bij', stack_wide, stack_wide, precision=lax.Precision.HIGHEST)
        lower_pairs = pair_dots.reshape(pair_dots.shape[0], fields * fields)[:, picked].astype(jnp.bfloat16)
        interact = jnp.concatenate([bottom, lower_pairs], axis=1)
        hidden_pre = jnp.dot(interact, top_weight, preferred_element_type=jnp.float32)
        activated, act_back = jax.vjp(gelu_tanh, hidden_pre)
        hidden = activated.astype(jnp.bfloat16)
        logits = jnp.dot(hidden, out_weight, preferred_element_type=jnp.float32)
        errors = jax.nn.sigmoid(logits) - click_rows.astype(jnp.float32)
        grad_pre, = act_back(errors[:, None] * out_weight.astype(jnp.float32)[None, :])
        grad_pre = grad_pre.astype(jnp.bfloat16)
        top_total = top_total + lax.dot_general(interact, grad_pre, (((0,), (0,)), ((), ())), preferred_element_type=jnp.float32)
        grad_inter = lax.dot_general(grad_pre, top_weight, (((1,), (1,)), ((), ())), preferred_element_type=jnp.float32)
        grad_pairs = grad_inter[:, E:].astype(jnp.bfloat16)
        symmetric = jnp.dot(grad_pairs, spread_table, preferred_element_type=jnp.float32).reshape(-1, fields, fields)
        grad_stack = jnp.einsum('bij,bje->bie', symmetric, stack_wide, precision=lax.Precision.HIGHEST)
        hot_total = hot_total.at[hot_ids.reshape(-1)].add(grad_stack[:, 1:1 + FH].reshape(-1, E))
        cold_terms = lax.optimization_barrier(grad_stack[:, 1 + FH:].astype(jnp.bfloat16))
        cold_total = cold_total.at[cold_ids.reshape(-1)].add(cold_terms.astype(jnp.float32).reshape(-1, E))
        return ((hot_total, cold_total, top_total), None)
    start = (jnp.zeros((HOT, E), jnp.float32), jnp.zeros((COLD, E), jnp.float32), jnp.zeros((NI, HID), jnp.float32))
    (hot_grad, cold_grad, top_grad), _ = lax.scan(accumulate, start, (dense_blocks, hot_blocks, cold_blocks, click_blocks))
    return (hot_grad, cold_grad, top_grad)
```

```python
import functools

import jax
import jax.numpy as jnp
import numpy as np
from jax import lax
from jax.experimental import pallas as pl
from jax.experimental.pallas import tpu as pltpu
from jax.sharding import PartitionSpec as P

FH = 13
MESH = pl.DeviceIdType.MESH
NX, NY, NZ = 4, 4, 8
VMEM_LIMIT = 48 * 1024 * 1024
F32 = jnp.float32
BF16 = jnp.bfloat16


def pair_tables(fields):
    lower_row, lower_col = np.tril_indices(fields, -1)
    picked = lower_row * fields + lower_col
    spread = np.zeros((picked.shape[0], fields * fields), np.float32)
    spread[np.arange(picked.shape[0]), picked] = 1.0
    spread[np.arange(picked.shape[0]), lower_col * fields + lower_row] = 1.0
    return (picked, spread)


def gelu_tanh(values):
    return jax.nn.gelu(values, approximate=True)


def place():
    me = lax.axis_index("dp")
    core = lax.axis_index("rep")
    z = lax.rem(me, NZ)
    x = lax.rem(lax.div(me, NZ), NX)
    y = lax.div(me, NZ * NX)
    return x, y, z, core


def peer(x, y, z, core):
    return (y * (NX * NZ) + x * NZ + z, core)


def rows_at(start, size):
    return pl.ds(pl.multiple_of(start, 16), size)


def reduce_kernel(in_ref, out_ref, core_buf, half, buf1, sum1, buf2, sum2, buf3, send_sem, recv_sem):
    x, y, z, core = place()
    partner = peer(x, y, z, 1 - core)
    xs = [peer(lax.rem(x + d, NX), y, z, core) for d in range(1, NX)]
    ys = [peer(x, lax.rem(y + d, NY), z, core) for d in range(1, NY)]
    zs = [peer(x, y, lax.rem(z + d, NZ), core) for d in range(1, NZ)]
    barrier = pltpu.get_barrier_semaphore()
    everyone = [partner] + xs + ys + zs
    for other in everyone:
        pl.semaphore_signal(barrier, inc=1, device_id=other, device_id_type=MESH)
    pl.semaphore_wait(barrier, len(everyone))

    count = [0]

    def send(src, dst, device):
        index = count[0]
        count[0] += 1
        copy = pltpu.make_async_remote_copy(
            src_ref=src, dst_ref=dst, send_sem=send_sem.at[index], recv_sem=recv_sem.at[index],
            device_id=device, device_id_type=MESH,
        )
        copy.start()
        return copy

    def finish(copies):
        for copy in copies:
            copy.wait()

    finish([send(in_ref.at[rows_at((1 - core) * 4096, 4096)], core_buf, partner)])

    @pl.loop(0, 16)
    def _(step):
        here = rows_at(step * 256, 256)
        mine = in_ref[rows_at(core * 4096 + step * 256, 256), :]
        half[here, :] = (mine.astype(F32) + core_buf[here, :].astype(F32)).astype(BF16)

    copies = []
    for d in range(1, 4):
        copies.append(send(half.at[rows_at(lax.rem(x + d, NX) * 512, 512)], buf1.at[0, d - 1], xs[d - 1]))
        copies.append(send(half.at[rows_at(2048 + lax.rem(y + d, NY) * 512, 512)], buf1.at[1, d - 1], ys[d - 1]))
    finish(copies)
    for which, own in ((0, x), (1, y)):

        @pl.loop(0, 4)
        def _(step):
            here = rows_at(step * 128, 128)
            total = half[rows_at(which * 2048 + own * 512 + step * 128, 128), :].astype(F32)
            for d in range(3):
                total += buf1[which, d, here, :].astype(F32)
            sum1[which, here, :] = total.astype(BF16)

    copies = []
    for d in range(1, 4):
        copies.append(send(sum1.at[0, rows_at(lax.rem(y + d, NY) * 128, 128)], buf2.at[0, d - 1], ys[d - 1]))
        copies.append(send(sum1.at[1, rows_at(lax.rem(x + d, NX) * 128, 128)], buf2.at[1, d - 1], xs[d - 1]))
    finish(copies)
    for which, own in ((0, y), (1, x)):
        total = sum1[which, rows_at(own * 128, 128), :].astype(F32)
        for d in range(3):
            total += buf2[which, d].astype(F32)
        sum2[which] = total.astype(BF16)

    copies = []
    for d in range(1, 8):
        for which in range(2):
            copies.append(send(sum2.at[which, rows_at(lax.rem(z + d, NZ) * 16, 16)], buf3.at[which, d - 1], zs[d - 1]))
    finish(copies)
    first = (x * 512 + y * 128, 2048 + y * 512 + x * 128)
    for which in range(2):
        total = sum2[which, rows_at(z * 16, 16), :].astype(F32)
        for d in range(7):
            total += buf3[which, d].astype(F32)
        out_ref[rows_at(core * 4096 + first[which] + z * 16, 16), :] = total.astype(BF16)

    copies = []
    for d in range(1, 8):
        for which in range(2):
            block = out_ref.at[rows_at(core * 4096 + first[which] + z * 16, 16)]
            copies.append(send(block, block, zs[d - 1]))
    finish(copies)
    copies = []
    for d in range(1, 4):
        block = out_ref.at[rows_at(core * 4096 + first[0], 128)]
        copies.append(send(block, block, ys[d - 1]))
        block = out_ref.at[rows_at(core * 4096 + first[1], 128)]
        copies.append(send(block, block, xs[d - 1]))
    finish(copies)
    copies = []
    for d in range(1, 4):
        block = out_ref.at[rows_at(core * 4096 + x * 512, 512)]
        copies.append(send(block, block, xs[d - 1]))
        block = out_ref.at[rows_at(core * 4096 + 2048 + y * 512, 512)]
        copies.append(send(block, block, ys[d - 1]))
    finish(copies)
    block = out_ref.at[rows_at(core * 4096, 4096)]
    finish([send(block, block, partner)])


def reduce_all(values):
    return pl.pallas_call(
        reduce_kernel,
        out_shape=jax.ShapeDtypeStruct((8192, 128), BF16),
        in_specs=[pl.BlockSpec(memory_space=pltpu.VMEM)],
        out_specs=pl.BlockSpec(memory_space=pltpu.VMEM),
        scratch_shapes=[
            pltpu.VMEM((4096, 128), BF16),
            pltpu.VMEM((4096, 128), BF16),
            pltpu.VMEM((2, 3, 512, 128), BF16),
            pltpu.VMEM((2, 512, 128), BF16),
            pltpu.VMEM((2, 3, 128, 128), BF16),
            pltpu.VMEM((2, 128, 128), BF16),
            pltpu.VMEM((2, 7, 16, 128), BF16),
            pltpu.SemaphoreType.DMA((54,)),
            pltpu.SemaphoreType.DMA((54,)),
        ],
        compiler_params=pltpu.CompilerParams(
            collective_id=0, has_side_effects=True, vmem_limit_bytes=VMEM_LIMIT
        ),
        name="reduce_all",
    )(values)


def pair_sum_kernel(in_ref, out_ref, held, got, send_sem, recv_sem):
    x, y, z, core = place()
    partner = peer(x, y, z, 1 - core)
    barrier = pltpu.get_barrier_semaphore()
    pl.semaphore_signal(barrier, inc=1, device_id=partner, device_id_type=MESH)
    pl.semaphore_wait(barrier, 1)
    copies = []
    for part in range(4):
        here = pl.ds(part * 1024, 1024)
        held[here, :] = in_ref[here, :].astype(BF16)
        copy = pltpu.make_async_remote_copy(
            src_ref=held.at[here], dst_ref=got.at[here], send_sem=send_sem.at[part],
            recv_sem=recv_sem.at[part], device_id=partner, device_id_type=MESH,
        )
        copy.start()
        copies.append(copy)
    for part in range(4):
        here = pl.ds(part * 1024, 1024)
        copies[part].wait()
        out_ref[here, :] = held[here, :].astype(F32) + got[here, :].astype(F32)


def pair_sum(values):
    return pl.pallas_call(
        pair_sum_kernel,
        out_shape=jax.ShapeDtypeStruct((4096, 128), F32),
        in_specs=[pl.BlockSpec(memory_space=pltpu.VMEM)],
        out_specs=pl.BlockSpec(memory_space=pltpu.VMEM),
        scratch_shapes=[
            pltpu.VMEM((4096, 128), BF16),
            pltpu.VMEM((4096, 128), BF16),
            pltpu.SemaphoreType.DMA((4,)),
            pltpu.SemaphoreType.DMA((4,)),
        ],
        compiler_params=pltpu.CompilerParams(
            collective_id=1, has_side_effects=True, vmem_limit_bytes=VMEM_LIMIT
        ),
        name="pair_sum",
    )(values)


def body(
    dense_feats,
    bottom_weight,
    top_weight,
    out_weight,
    hot_table,
    cold_table,
    hot_index,
    cold_owner,
    cold_row,
    clicks,
):
    owners = lax.axis_size("dp")
    samples, cold_fields = cold_owner.shape
    width = hot_table.shape[1]
    capacity = min(samples, max(2, (2 * samples * cold_fields + owners - 1) // owners))
    fields = 1 + hot_index.shape[1] + cold_fields
    picked, spread = pair_tables(fields)
    spread_table = jnp.asarray(spread).astype(jnp.bfloat16)
    flat_owner = cold_owner.reshape(-1)
    onehot = (flat_owner[:, None] == jnp.arange(owners, dtype=jnp.int32)[None, :]).astype(jnp.int32)
    position = jnp.sum(jnp.cumsum(onehot, axis=0) * onehot, axis=1) - 1
    slot_index = flat_owner * capacity + position
    requests = jnp.zeros((owners * capacity,), jnp.int32).at[slot_index].set(cold_row.reshape(-1))
    requests = requests.reshape(owners, capacity)
    wanted = lax.all_to_all(requests, "dp", split_axis=0, concat_axis=0, tiled=True)
    found_rows = jnp.take(cold_table, wanted, axis=0)
    sent_back = lax.all_to_all(found_rows, "dp", split_axis=0, concat_axis=0, tiled=True)
    cold_vectors = jnp.take(
        sent_back.reshape(owners * capacity, width), slot_index, axis=0
    ).reshape(samples, cold_fields, width)
    hot_vectors = jnp.take(hot_table, hot_index, axis=0)
    bottom = jnp.maximum(
        jnp.dot(dense_feats, bottom_weight, preferred_element_type=jnp.float32), 0.0
    ).astype(jnp.bfloat16)
    stacked = jnp.concatenate([bottom[:, None, :], hot_vectors, cold_vectors], axis=1)
    pair_dots = jnp.einsum("bie,bje->bij", stacked, stacked, preferred_element_type=jnp.float32)
    lower_pairs = pair_dots.reshape(samples, fields * fields)[:, picked].astype(jnp.bfloat16)
    interact = jnp.concatenate([bottom, lower_pairs], axis=1)
    hidden_pre = jnp.dot(interact, top_weight, preferred_element_type=jnp.float32)
    activated, act_back = jax.vjp(gelu_tanh, hidden_pre)
    hidden = activated.astype(jnp.bfloat16)
    logits = jnp.dot(hidden, out_weight, preferred_element_type=jnp.float32)
    errors = jax.nn.sigmoid(logits) - clicks.astype(jnp.float32)
    (grad_pre,) = act_back(errors[:, None] * out_weight.astype(jnp.float32)[None, :])
    grad_pre = grad_pre.astype(jnp.bfloat16)
    top_term = lax.dot_general(
        interact, grad_pre, (((0,), (0,)), ((), ())), preferred_element_type=jnp.float32
    )
    grad_inter = lax.dot_general(
        grad_pre, top_weight, (((1,), (1,)), ((), ())), preferred_element_type=jnp.float32
    )
    grad_pairs = grad_inter[:, width:].astype(jnp.bfloat16)
    symmetric = jnp.dot(grad_pairs, spread_table, preferred_element_type=jnp.float32).reshape(
        samples, fields, fields
    )
    grad_stack = jnp.einsum(
        "bij,bje->bie", symmetric.astype(jnp.bfloat16), stacked, preferred_element_type=jnp.float32
    )
    cold_terms = grad_stack[:, 1 + FH :].astype(jnp.bfloat16).reshape(samples * cold_fields, width)
    outgoing = jnp.zeros((owners * capacity, width), jnp.bfloat16).at[slot_index].set(cold_terms)
    returned = lax.all_to_all(
        outgoing.reshape(owners, capacity, width), "dp", split_axis=0, concat_axis=0, tiled=True
    )
    local_hot = (
        jnp.zeros(hot_table.shape, jnp.float32)
        .at[hot_index.reshape(-1)]
        .add(grad_stack[:, 1 : 1 + FH].reshape(-1, width))
    )
    top_rows = top_term.astype(BF16).reshape(479, 8, 128).transpose(1, 0, 2).reshape(8 * 479, 128)
    summed = reduce_all(
        jnp.concatenate([local_hot.astype(BF16), top_rows, jnp.zeros((4096 - 8 * 479, 128), BF16)], axis=0)
    )
    hot_grad = summed[:4096].astype(F32)
    top_grad = summed[4096 : 4096 + 8 * 479].reshape(8, 479, 128).transpose(1, 0, 2).reshape(479, 1024).astype(F32)
    local_cold = (
        jnp.zeros((cold_table.shape[0], width), jnp.float32)
        .at[wanted.reshape(-1)]
        .add(returned.reshape(owners * capacity, width).astype(jnp.float32))
    )
    cold_grad = pair_sum(local_cold)
    return (hot_grad, cold_grad, top_grad)


def solution(mesh):
    return jax.shard_map(
        body,
        mesh=mesh,
        in_specs=(
            P(("dp", "rep"), None),
            P(),
            P(),
            P(),
            P(),
            P("dp", None),
            P(("dp", "rep"), None),
            P(("dp", "rep"), None),
            P(("dp", "rep"), None),
            P(("dp", "rep")),
        ),
        out_specs=(P(), P("dp", None), P()),
        check_vma=False,
    )
```

```python
import jax
import jax.numpy as jnp
import numpy as np
from jax import lax
from jax.experimental import pallas as pl
from jax.experimental.pallas import tpu as pltpu
from jax.sharding import PartitionSpec as P

MESH = pl.DeviceIdType.MESH
NX, NY, NZ = 4, 4, 8
VMEM_LIMIT = 48 * 1024 * 1024
F32 = jnp.float32
BF16 = jnp.bfloat16
CAP = 52
STRIDE = 56


def place():
    me = lax.axis_index("dp")
    core = lax.axis_index("rep")
    z = lax.rem(me, NZ)
    x = lax.rem(lax.div(me, NZ), NX)
    y = lax.div(me, NZ * NX)
    return x, y, z, core


def peer(x, y, z, core):
    return (y * (NX * NZ) + x * NZ + z, core)


def rows_at(start, size):
    return pl.ds(pl.multiple_of(start, 16), size)


def reduce_kernel(in_ref, out_ref, core_buf, half, buf1, sum1, buf2, sum2, buf3, send_sem, recv_sem):
    x, y, z, core = place()
    partner = peer(x, y, z, 1 - core)
    xs = [peer(lax.rem(x + d, NX), y, z, core) for d in range(1, NX)]
    ys = [peer(x, lax.rem(y + d, NY), z, core) for d in range(1, NY)]
    zs = [peer(x, y, lax.rem(z + d, NZ), core) for d in range(1, NZ)]
    barrier = pltpu.get_barrier_semaphore()
    everyone = [partner] + xs + ys + zs
    for other in everyone:
        pl.semaphore_signal(barrier, inc=1, device_id=other, device_id_type=MESH)
    pl.semaphore_wait(barrier, len(everyone))

    count = [0]

    def send(src, dst, device):
        index = count[0]
        count[0] += 1
        copy = pltpu.make_async_remote_copy(
            src_ref=src, dst_ref=dst, send_sem=send_sem.at[index], recv_sem=recv_sem.at[index],
            device_id=device, device_id_type=MESH,
        )
        copy.start()
        return copy

    def finish(copies):
        for copy in copies:
            copy.wait()

    finish([send(in_ref.at[rows_at((1 - core) * 4096, 4096)], core_buf, partner)])

    @pl.loop(0, 16)
    def _(step):
        here = rows_at(step * 256, 256)
        mine = in_ref[rows_at(core * 4096 + step * 256, 256), :]
        half[here, :] = (mine.astype(F32) + core_buf[here, :].astype(F32)).astype(BF16)

    copies = []
    for d in range(1, 4):
        copies.append(send(half.at[rows_at(lax.rem(x + d, NX) * 512, 512)], buf1.at[0, d - 1], xs[d - 1]))
        copies.append(send(half.at[rows_at(2048 + lax.rem(y + d, NY) * 512, 512)], buf1.at[1, d - 1], ys[d - 1]))
    finish(copies)
    for which, own in ((0, x), (1, y)):

        @pl.loop(0, 4)
        def _(step):
            here = rows_at(step * 128, 128)
            total = half[rows_at(which * 2048 + own * 512 + step * 128, 128), :].astype(F32)
            for d in range(3):
                total += buf1[which, d, here, :].astype(F32)
            sum1[which, here, :] = total

    copies = []
    for d in range(1, 4):
        copies.append(send(sum1.at[0, rows_at(lax.rem(y + d, NY) * 128, 128)], buf2.at[0, d - 1], ys[d - 1]))
        copies.append(send(sum1.at[1, rows_at(lax.rem(x + d, NX) * 128, 128)], buf2.at[1, d - 1], xs[d - 1]))
    finish(copies)
    for which, own in ((0, y), (1, x)):
        total = sum1[which, rows_at(own * 128, 128), :]
        for d in range(3):
            total += buf2[which, d]
        sum2[which] = total

    copies = []
    for d in range(1, 8):
        for which in range(2):
            copies.append(send(sum2.at[which, rows_at(lax.rem(z + d, NZ) * 16, 16)], buf3.at[which, d - 1], zs[d - 1]))
    finish(copies)
    first = (x * 512 + y * 128, 2048 + y * 512 + x * 128)
    for which in range(2):
        total = sum2[which, rows_at(z * 16, 16), :]
        for d in range(7):
            total += buf3[which, d]
        out_ref[rows_at(core * 4096 + first[which] + z * 16, 16), :] = total.astype(BF16)

    copies = []
    for d in range(1, 8):
        for which in range(2):
            block = out_ref.at[rows_at(core * 4096 + first[which] + z * 16, 16)]
            copies.append(send(block, block, zs[d - 1]))
    finish(copies)
    copies = []
    for d in range(1, 4):
        block = out_ref.at[rows_at(core * 4096 + first[0], 128)]
        copies.append(send(block, block, ys[d - 1]))
        block = out_ref.at[rows_at(core * 4096 + first[1], 128)]
        copies.append(send(block, block, xs[d - 1]))
    finish(copies)
    copies = []
    for d in range(1, 4):
        block = out_ref.at[rows_at(core * 4096 + x * 512, 512)]
        copies.append(send(block, block, xs[d - 1]))
        block = out_ref.at[rows_at(core * 4096 + 2048 + y * 512, 512)]
        copies.append(send(block, block, ys[d - 1]))
    finish(copies)
    block = out_ref.at[rows_at(core * 4096, 4096)]
    finish([send(block, block, partner)])


def reduce_all(values):
    return pl.pallas_call(
        reduce_kernel,
        out_shape=jax.ShapeDtypeStruct((8192, 128), BF16),
        in_specs=[pl.BlockSpec(memory_space=pltpu.VMEM)],
        out_specs=pl.BlockSpec(memory_space=pltpu.VMEM),
        scratch_shapes=[
            pltpu.VMEM((4096, 128), BF16),
            pltpu.VMEM((4096, 128), BF16),
            pltpu.VMEM((2, 3, 512, 128), BF16),
            pltpu.VMEM((2, 512, 128), F32),
            pltpu.VMEM((2, 3, 128, 128), F32),
            pltpu.VMEM((2, 128, 128), F32),
            pltpu.VMEM((2, 7, 16, 128), F32),
            pltpu.SemaphoreType.DMA((54,)),
            pltpu.SemaphoreType.DMA((54,)),
        ],
        compiler_params=pltpu.CompilerParams(
            collective_id=0, has_side_effects=True, vmem_limit_bytes=VMEM_LIMIT
        ),
        name="reduce_all",
    )(values)


def pair_sum_kernel(in_ref, out_ref, held, got, send_sem, recv_sem):
    x, y, z, core = place()
    partner = peer(x, y, z, 1 - core)
    barrier = pltpu.get_barrier_semaphore()
    pl.semaphore_signal(barrier, inc=1, device_id=partner, device_id_type=MESH)
    pl.semaphore_wait(barrier, 1)
    copies = []
    for part in range(4):
        here = pl.ds(part * 1024, 1024)
        held[here, :] = in_ref[here, :].astype(BF16)
        copy = pltpu.make_async_remote_copy(
            src_ref=held.at[here], dst_ref=got.at[here], send_sem=send_sem.at[part],
            recv_sem=recv_sem.at[part], device_id=partner, device_id_type=MESH,
        )
        copy.start()
        copies.append(copy)
    for part in range(4):
        here = pl.ds(part * 1024, 1024)
        copies[part].wait()
        out_ref[here, :] = held[here, :].astype(F32) + got[here, :].astype(F32)


def pair_sum(values):
    return pl.pallas_call(
        pair_sum_kernel,
        out_shape=jax.ShapeDtypeStruct((4096, 128), F32),
        in_specs=[pl.BlockSpec(memory_space=pltpu.VMEM)],
        out_specs=pl.BlockSpec(memory_space=pltpu.VMEM),
        scratch_shapes=[
            pltpu.VMEM((4096, 128), BF16),
            pltpu.VMEM((4096, 128), BF16),
            pltpu.SemaphoreType.DMA((4,)),
            pltpu.SemaphoreType.DMA((4,)),
        ],
        compiler_params=pltpu.CompilerParams(
            collective_id=1, has_side_effects=True, vmem_limit_bytes=VMEM_LIMIT
        ),
        name="pair_sum",
    )(values)


def params():
    return pltpu.CompilerParams(vmem_limit_bytes=VMEM_LIMIT)


def iota(shape, dimension):
    return lax.broadcasted_iota(jnp.int32, shape, dimension)


def build_kernel(owner_ref, row_ref, query_ref, slot_ref, rank, rows, table):
    x, y, z, _ = place()
    owner = owner_ref[...]
    dz = (lax.bitwise_and(owner, 7) - z + 8) & 7
    dx = (lax.bitwise_and(lax.shift_right_logical(owner, 3), 3) - x + 4) & 3
    dy = (lax.shift_right_logical(owner, 5) - y + 4) & 3
    relative = dz * 16 + dy * 4 + dx
    row = row_ref[...].astype(F32)
    owner = owner.astype(F32)
    lane = iota((256, 128), 1)
    named = jnp.zeros((256, 128), F32)
    wanted = jnp.zeros((256, 128), F32)
    for f in range(13):
        here = relative[:, f : f + 1] == lane
        named = jnp.where(here, 1.0, named)
        wanted = jnp.where(here, row[:, f : f + 1], wanted)
    before = jnp.where(iota((256, 256), 1) < iota((256, 256), 0), 1.0, 0.0).astype(BF16)
    count = jnp.dot(before, named.astype(BF16), preferred_element_type=F32)
    slots = jnp.zeros((256, 128), F32)
    for f in range(13):
        here = relative[:, f : f + 1] == lane
        mine = jnp.sum(jnp.where(here, count, 0.0), axis=1, keepdims=True)
        slots = jnp.where(lane == f, owner[:, f : f + 1] * STRIDE + mine, slots)
    slot_ref[...] = slots.T[0:16, :].astype(jnp.int32)
    rank[...] = jnp.where(named > 0.0, count, -1.0)
    rows[...] = wanted
    table[...] = jnp.zeros((128, 128), F32)

    for p in range(CAP):
        chosen = jnp.where(rank[...] == float(p), rows[...], 0.0)
        table[p : p + 1, :] = jnp.sum(chosen, axis=0, keepdims=True)

    query_ref[...] = table[...].T.astype(jnp.int32).reshape(8, 16, 128)


def build_requests(cold_owner, cold_row):
    return pl.pallas_call(
        build_kernel,
        out_shape=(
            jax.ShapeDtypeStruct((8, 16, 128), jnp.int32),
            jax.ShapeDtypeStruct((16, 256), jnp.int32),
        ),
        scratch_shapes=[pltpu.VMEM((256, 128), F32), pltpu.VMEM((256, 128), F32), pltpu.VMEM((128, 128), F32)],
        compiler_params=params(),
        name="build_requests",
    )(cold_owner, cold_row)


def request_kernel(query_ref, out_ref, middle, turned, send_sem, recv_sem):
    x, y, z, core = place()
    plane = [(dx, dy) for dy in range(4) for dx in range(4)]
    zs = [peer(x, y, lax.rem(z + d, NZ), core) for d in range(1, NZ)]
    xys = [peer(lax.rem(x + dx, NX), lax.rem(y + dy, NY), z, core) for dx, dy in plane[1:]]
    barrier = pltpu.get_barrier_semaphore()
    for other in zs + xys:
        pl.semaphore_signal(barrier, inc=1, device_id=other, device_id_type=MESH)
    pl.semaphore_wait(barrier, len(zs) + len(xys))
    copies = []
    for d in range(1, 8):
        copy = pltpu.make_async_remote_copy(
            src_ref=query_ref.at[d], dst_ref=middle.at[d], send_sem=send_sem.at[d], recv_sem=recv_sem.at[d],
            device_id=zs[d - 1], device_id_type=MESH,
        )
        copy.start()
        copies.append(copy)
    middle[0] = query_ref[0]
    for copy in copies:
        copy.wait()
    for d in range(8):
        for k in range(16):
            turned[k, d : d + 1, :] = middle[d, k : k + 1, :]
    copies = []
    for k in range(1, 16):
        copy = pltpu.make_async_remote_copy(
            src_ref=turned.at[k], dst_ref=out_ref.at[k], send_sem=send_sem.at[7 + k], recv_sem=recv_sem.at[7 + k],
            device_id=xys[k - 1], device_id_type=MESH,
        )
        copy.start()
        copies.append(copy)
    out_ref[0] = turned[0]
    for copy in copies:
        copy.wait()


def exchange_requests(query):
    return pl.pallas_call(
        request_kernel,
        out_shape=jax.ShapeDtypeStruct((16, 8, 128), jnp.int32),
        in_specs=[pl.BlockSpec(memory_space=pltpu.VMEM)],
        out_specs=pl.BlockSpec(memory_space=pltpu.VMEM),
        scratch_shapes=[
            pltpu.VMEM((8, 16, 128), jnp.int32),
            pltpu.VMEM((16, 8, 128), jnp.int32),
            pltpu.SemaphoreType.DMA((23,)),
            pltpu.SemaphoreType.DMA((23,)),
        ],
        compiler_params=pltpu.CompilerParams(collective_id=2, has_side_effects=True, vmem_limit_bytes=VMEM_LIMIT),
        name="exchange_requests",
    )(query)


def source_of(r, x, y, z):
    dz, dx, dy = lax.rem(r, 8), lax.rem(lax.div(r, 8), 4), lax.div(r, 32)
    return lax.rem(y - dy + 4, 4) * 32 + lax.rem(x - dx + 4, 4) * 8 + lax.rem(z - dz + 8, 8)


def widen(wide, ref, rows):
    @pl.loop(0, rows // 256)
    def _(step):
        here = pl.ds(pl.multiple_of(step * 256, 256), 256)
        wide[here, :] = ref[here, :].astype(F32)


def lookup_kernel(want_ref, table_ref, out_ref, wide, tile):
    x, y, z, _ = place()
    widen(wide, table_ref, 4096)

    @pl.loop(0, 128)
    def _(r):
        for p in range(CAP):
            tile[p : p + 1, :] = wide[pl.ds(want_ref[r, p], 1), :]
        out_ref[source_of(r, x, y, z)] = tile[0:CAP, :].astype(BF16)


def lookup_rows(want, table):
    return pl.pallas_call(
        lookup_kernel,
        out_shape=jax.ShapeDtypeStruct((128, CAP, 128), BF16),
        in_specs=[pl.BlockSpec(memory_space=pltpu.SMEM), pl.BlockSpec(memory_space=pltpu.VMEM)],
        out_specs=pl.BlockSpec(memory_space=pltpu.VMEM),
        scratch_shapes=[pltpu.VMEM((4096, 128), F32), pltpu.VMEM((64, 128), F32)],
        compiler_params=params(),
        name="lookup_rows",
    )(want, table)


def near_kernel(index_ref, table_ref, dense_ref, weight_ref, out_ref, bottom_ref, wide, held):
    widen(wide, table_ref, 4096)
    bottom = jnp.maximum(jnp.dot(dense_ref[...], weight_ref[...], preferred_element_type=F32), 0.0)
    bottom_ref[...] = bottom.astype(BF16)
    held[...] = bottom

    @pl.loop(0, 32)
    def _(g):
        out_rows = []
        start = pl.multiple_of(g * 8, 8)
        out_ref[g, 0:16, :] = jnp.concatenate(
            [held[pl.ds(start, 8), :]]
            + [wide[pl.ds(index_ref[0, g * 8 + k], 1), :] for k in range(8)], axis=0
        ).astype(BF16)
        for f in range(1, 13, 2):
            rows = [wide[pl.ds(index_ref[f + k // 8, g * 8 + k % 8], 1), :] for k in range(16)]
            out_ref[g, 8 + f * 8 : 24 + f * 8, :] = jnp.concatenate(rows, axis=0).astype(BF16)


def near_rows(hot_index, hot_table, dense, weight):
    vmem = pl.BlockSpec(memory_space=pltpu.VMEM)
    return pl.pallas_call(
        near_kernel,
        out_shape=(jax.ShapeDtypeStruct((32, 112, 128), BF16), jax.ShapeDtypeStruct((256, 128), BF16)),
        in_specs=[pl.BlockSpec(memory_space=pltpu.SMEM), vmem, vmem, vmem],
        out_specs=(vmem, vmem),
        scratch_shapes=[pltpu.VMEM((4096, 128), F32), pltpu.VMEM((256, 128), F32)],
        compiler_params=params(),
        name="near_rows",
    )(hot_index, hot_table, dense, weight)


def main_kernel(
    slot_ref, got_ref, near_ref, bottom_ref, weight0_ref, weight_ref, out_weight_ref, click_ref,
    sent_ref, hot_ref, low_ref, grad_ref,
    wide, stack, far, pairs, hidden, slope, terms,
):
    @pl.loop(0, 128)
    def _(d):
        wide[pl.ds(pl.multiple_of(d * STRIDE, 8), CAP), :] = got_ref[d].astype(F32)

    far[104:144, :] = jnp.zeros((40, 128), F32)
    same = (iota((256, 256), 0) & 7) == (iota((256, 256), 1) & 7)
    fold = jnp.where((iota((256, 128), 0) >> 3) == (iota((256, 128), 1) & 31), 1.0, 0.0).astype(BF16)
    unfold = jnp.where((iota((128, 256), 1) >> 3) == (iota((128, 256), 0) & 31), 1.0, 0.0).astype(BF16)
    quarter = iota((8, 128), 1) >> 5
    zero8 = jnp.zeros((8, 128), F32)

    @pl.loop(0, 32)
    def _(g):
        for f in range(13):
            for k in range(8):
                far[f * 8 + k : f * 8 + k + 1, :] = wide[pl.ds(slot_ref[f, g * 8 + k], 1), :]
        stack[g, 0:112, :] = near_ref[g]
        stack[g, 112:256, :] = far[...].astype(BF16)
        group = stack[g]
        dots = lax.dot_general(group, group, (((1,), (1,)), ((), ())), preferred_element_type=F32)
        dots = jnp.where(same, dots, 0.0).astype(BF16)
        folded = jnp.dot(dots, fold, preferred_element_type=F32)
        for b in range(7):
            block = zero8
            for q in range(4):
                i = 4 * b + q
                block = jnp.where(quarter == q, folded[i * 8 : i * 8 + 8, :], block)
            pairs[pl.ds(pl.multiple_of(g * 8, 8), 8), b * 128 : b * 128 + 128] = block

    for b in range(7):
        i = 4 * b + (iota((256, 128), 1) >> 5)
        j = iota((256, 128), 1) & 31
        low_ref[:, b * 128 : b * 128 + 128] = jnp.where(i > j, pairs[:, b * 128 : b * 128 + 128], 0.0).astype(BF16)

    total = jnp.zeros((256, 128), F32)
    for n in range(4):
        here = slice(n * 256, n * 256 + 256)
        hidden[:, here] = jnp.dot(bottom_ref[...], weight0_ref[:, here], preferred_element_type=F32) + jnp.dot(
            low_ref[...], weight_ref[:, here], preferred_element_type=F32
        )
    for n in range(8):
        here = slice(n * 128, n * 128 + 128)
        v = hidden[:, here]
        c = 0.7978845608028654
        square = v * v
        t = jnp.tanh(c * v * (1.0 + 0.044715 * square))
        weight = out_weight_ref[:, here].astype(F32)
        act = (0.5 * v * (1.0 + t)).astype(BF16).astype(F32)
        total = total + act * weight
        slope[:, here] = weight * (0.5 * (1.0 + t) + 0.5 * c * v * (1.0 - t * t) * (1.0 + 0.134145 * square))
    logits = jnp.sum(total, axis=1, keepdims=True)
    errors = 1.0 / (1.0 + jnp.exp(-logits)) - click_ref[...].astype(F32)
    grad_ref[...] = (slope[...] * errors).astype(BF16)
    for b in range(7):
        here = slice(b * 128, b * 128 + 128)
        pairs[:, here] = lax.dot_general(
            grad_ref[...], weight_ref[here, :], (((1,), (1,)), ((), ())), preferred_element_type=F32
        )

    @pl.loop(0, 7)
    def _(step):
        wide[pl.ds(pl.multiple_of(step * 1024, 1024), 1024), :] = jnp.zeros((1024, 128), F32)

    @pl.loop(0, 32)
    def _(g):
        rows = []
        for b in range(7):
            block = pairs[pl.ds(pl.multiple_of(g * 8, 8), 8), b * 128 : b * 128 + 128]
            for q in range(4):
                rows.append(jnp.where(quarter == q, block, 0.0))
        rows += [zero8] * 4
        spread = jnp.dot(jnp.concatenate(rows, axis=0).astype(BF16), unfold, preferred_element_type=F32)
        spread = jnp.where(same, spread, 0.0).astype(BF16)
        result = jnp.dot(spread, stack[g], preferred_element_type=F32)
        hot_ref[g] = result[0:128, :].astype(BF16)
        terms[...] = result
        for f in range(13):
            for k in range(8):
                row = 112 + f * 8 + k
                wide[pl.ds(slot_ref[f, g * 8 + k], 1), :] = terms[row : row + 1, :]

    @pl.loop(0, 128)
    def _(d):
        sent_ref[d] = wide[pl.ds(pl.multiple_of(d * STRIDE, 8), CAP), :].astype(BF16)


def main_part(slot, got, near, bottom, weight0, weight, out_weight, clicks):
    vmem = pl.BlockSpec(memory_space=pltpu.VMEM)
    return pl.pallas_call(
        main_kernel,
        out_shape=(
            jax.ShapeDtypeStruct((128, CAP, 128), BF16),
            jax.ShapeDtypeStruct((32, 128, 128), BF16),
            jax.ShapeDtypeStruct((256, 896), BF16),
            jax.ShapeDtypeStruct((256, 1024), BF16),
        ),
        in_specs=[pl.BlockSpec(memory_space=pltpu.SMEM)] + [vmem] * 7,
        out_specs=(vmem,) * 4,
        scratch_shapes=[
            pltpu.VMEM((128 * STRIDE, 128), F32),
            pltpu.VMEM((32, 256, 128), BF16),
            pltpu.VMEM((144, 128), F32),
            pltpu.VMEM((256, 896), F32),
            pltpu.VMEM((256, 1024), F32),
            pltpu.VMEM((256, 1024), F32),
            pltpu.VMEM((256, 128), F32),
        ],
        compiler_params=params(),
        name="main_part",
    )(slot, got, near, bottom, weight0, weight, out_weight, clicks)


def hot_kernel(index_ref, column_ref, value_ref, bottom_ref, low_ref, grad_ref, out_ref, halves, top):
    for g in range(32):
        high = column_ref[:, g : g + 1] >> 11
        value = value_ref[g].astype(F32)
        halves[g * 128 : g * 128 + 128, 0:128] = jnp.where(high == 0, value, 0.0).astype(BF16)
        halves[g * 128 : g * 128 + 128, 128:256] = jnp.where(high == 1, value, 0.0).astype(BF16)

    @pl.loop(0, 8)
    def _(m):
        start = pl.multiple_of(m * 256, 256)
        total = jnp.zeros((256, 256), F32)
        for n in range(4):
            index = jnp.broadcast_to(index_ref[:, n * 1024 : n * 1024 + 1024], (256, 1024)) & 2047
            hits = jnp.where(index == iota((256, 1024), 0) + m * 256, 1.0, 0.0).astype(BF16)
            total = total + jnp.dot(hits, halves[n * 1024 : n * 1024 + 1024, :], preferred_element_type=F32)
        out_ref[pl.ds(start, 256), :] = total[:, 0:128].astype(BF16)
        out_ref[pl.ds(start + 2048, 256), :] = total[:, 128:256].astype(BF16)

    top[472:480, :] = jnp.zeros((8, 1024), F32)
    top[0:128, :] = lax.dot_general(
        bottom_ref[...], grad_ref[...], (((0,), (0,)), ((), ())), preferred_element_type=F32
    )
    for b in range(7):
        part = lax.dot_general(
            low_ref[:, b * 128 : b * 128 + 128], grad_ref[...], (((0,), (0,)), ((), ())), preferred_element_type=F32
        )
        for q in range(4):
            i = 4 * b + q
            if 0 < i < 27:
                at = 128 + i * (i - 1) // 2
                top[at : at + i, :] = part[q * 32 : q * 32 + i, :]
    for n in range(8):
        out_ref[4096 + n * 480 : 4576 + n * 480, :] = top[:, n * 128 : n * 128 + 128].astype(BF16)
    out_ref[7936:8192, :] = jnp.zeros((256, 128), BF16)


def hot_and_top(index, column, value, bottom, low, grad):
    return pl.pallas_call(
        hot_kernel,
        out_shape=jax.ShapeDtypeStruct((8192, 128), BF16),
        scratch_shapes=[pltpu.VMEM((4096, 256), BF16), pltpu.VMEM((480, 1024), F32)],
        compiler_params=params(),
        name="hot_and_top",
    )(index, column, value, bottom, low, grad)


def cold_kernel(index_ref, column_ref, value_ref, out_ref, halves):
    x, y, z, _ = place()
    pad = jnp.zeros((64 - CAP, 128), F32)
    for r in range(128):
        high = column_ref[0:64, r : r + 1] >> 11
        value = jnp.concatenate([value_ref[source_of(r, x, y, z)].astype(F32), pad], axis=0)
        halves[r * 64 : r * 64 + 64, 0:128] = jnp.where(high == 0, value, 0.0).astype(BF16)
        halves[r * 64 : r * 64 + 64, 128:256] = jnp.where(high == 1, value, 0.0).astype(BF16)

    @pl.loop(0, 8)
    def _(m):
        start = pl.multiple_of(m * 256, 256)
        total = jnp.zeros((256, 256), F32)
        for n in range(8):
            index = jnp.broadcast_to(index_ref[:, n * 1024 : n * 1024 + 1024], (256, 1024)) & 2047
            hits = jnp.where(index == iota((256, 1024), 0) + m * 256, 1.0, 0.0).astype(BF16)
            total = total + jnp.dot(hits, halves[n * 1024 : n * 1024 + 1024, :], preferred_element_type=F32)
        out_ref[pl.ds(start, 256), :] = total[:, 0:128]
        out_ref[pl.ds(start + 2048, 256), :] = total[:, 128:256]


def cold_sums(index, column, value):
    return pl.pallas_call(
        cold_kernel,
        out_shape=jax.ShapeDtypeStruct((4096, 128), F32),
        scratch_shapes=[pltpu.VMEM((8192, 256), BF16)],
        compiler_params=params(),
        name="cold_sums",
    )(index, column, value)


def format_kernel(in_ref, hot_ref, top_ref):
    hot_ref[...] = in_ref[0:4096, :].astype(F32)
    for n in range(8):
        top_ref[:, n * 128 : n * 128 + 128] = in_ref[4096 + n * 480 : 4576 + n * 480, :].astype(F32)[0:479, :]


def format_sums(values):
    return pl.pallas_call(
        format_kernel,
        out_shape=(jax.ShapeDtypeStruct((4096, 128), F32), jax.ShapeDtypeStruct((479, 1024), F32)),
        compiler_params=params(),
        name="format_sums",
    )(values)


def weight_rows():
    rows = np.full((896,), 479, np.int32)
    for i in range(27):
        for j in range(27):
            if i != j:
                a, b = max(i, j), min(i, j)
                rows[i * 32 + j] = 128 + a * (a - 1) // 2 + b
    return rows


def body(
    dense_feats,
    bottom_weight,
    top_weight,
    out_weight,
    hot_table,
    cold_table,
    hot_index,
    cold_owner,
    cold_row,
    clicks,
):
    query, slot = build_requests(cold_owner, cold_row)
    wanted = exchange_requests(query).reshape(128, 128)
    found_rows = lookup_rows(wanted, cold_table)
    got = lax.all_to_all(found_rows, "dp", split_axis=0, concat_axis=0, tiled=True)
    hot_fields = hot_index.T
    near, bottom = near_rows(hot_fields, hot_table, dense_feats, bottom_weight)
    weight = jnp.concatenate([top_weight, jnp.zeros((1, 1024), BF16)], axis=0)[weight_rows()]
    outgoing, hot_terms, low, grad = main_part(
        slot, got, near, bottom, top_weight[:128], weight, out_weight.reshape(1, 1024), clicks.reshape(256, 1)
    )
    returned = lax.all_to_all(outgoing, "dp", split_axis=0, concat_axis=0, tiled=True)
    hot_groups = jnp.pad(hot_fields.reshape(13, 32, 8).transpose(1, 0, 2), ((0, 0), (1, 2), (0, 0)), constant_values=-1)
    hot_groups = hot_groups.reshape(32, 128)
    sums = hot_and_top(hot_groups.reshape(1, 4096), hot_groups.T, hot_terms, bottom, low, grad)
    hot_grad, top_grad = format_sums(reduce_all(sums))
    local_cold = cold_sums(wanted[:, :64].reshape(1, 8192), wanted.T, returned)
    cold_grad = pair_sum(local_cold)
    return (hot_grad, cold_grad, top_grad)


def solution(mesh):
    return jax.shard_map(
        body,
        mesh=mesh,
        in_specs=(
            P(("dp", "rep"), None),
            P(),
            P(),
            P(),
            P(),
            P("dp", None),
            P(("dp", "rep"), None),
            P(("dp", "rep"), None),
            P(("dp", "rep"), None),
            P(("dp", "rep")),
        ),
        out_specs=(P(), P("dp", None), P()),
        check_vma=False,
    )
```

```python
import jax
import jax.numpy as jnp
from jax import lax
from jax.experimental import pallas as pl
from jax.experimental.pallas import tpu as pltpu
from jax.sharding import PartitionSpec as P

MESH = pl.DeviceIdType.MESH
NX, NY, NZ = 4, 4, 8
VMEM_LIMIT = 48 * 1024 * 1024
F32 = jnp.float32
BF16 = jnp.bfloat16
CAP = 52
STRIDE = 56
EARLY = 48
UNROLL = 4


def place():
    me = lax.axis_index("dp")
    core = lax.axis_index("rep")
    z = lax.rem(me, NZ)
    x = lax.rem(lax.div(me, NZ), NX)
    y = lax.div(me, NZ * NX)
    return x, y, z, core


def peer(x, y, z, core):
    return (y * (NX * NZ) + x * NZ + z, core)


def rows_at(start, size):
    return pl.ds(pl.multiple_of(start, 16), size)


def reduce_kernel(in_ref, out_ref, core_buf, half, buf1, sum1, buf2, sum2, buf3, send_sem, recv_sem):
    x, y, z, core = place()
    partner = peer(x, y, z, 1 - core)
    xs = [peer(lax.rem(x + d, NX), y, z, core) for d in range(1, NX)]
    ys = [peer(x, lax.rem(y + d, NY), z, core) for d in range(1, NY)]
    zs = [peer(x, y, lax.rem(z + d, NZ), core) for d in range(1, NZ)]
    barrier = pltpu.get_barrier_semaphore()
    everyone = [partner] + xs + ys + zs
    for other in everyone:
        pl.semaphore_signal(barrier, inc=1, device_id=other, device_id_type=MESH)
    pl.semaphore_wait(barrier, len(everyone))

    started = []

    def send(src, dst, device):
        index = len(started)
        copy = pltpu.make_async_remote_copy(
            src_ref=src, dst_ref=dst, send_sem=send_sem.at[index], recv_sem=recv_sem.at[index],
            device_id=device, device_id_type=MESH,
        )
        copy.start()
        started.append(copy)
        return copy

    mine, other = core * 4096, (1 - core) * 4096
    own = (x, y)
    plan = [(which, d) for d in (1, 2, 3, 0) for which in (0, 1)]
    starts = [which * 2048 + lax.rem(own[which] + d, 4) * 512 for which, d in plan]
    over = [send(in_ref.at[rows_at(other + start, 512)], core_buf.at[rows_at(start, 512)], partner) for start in starts]
    first = {}
    for (which, d), start, copy in zip(plan, starts, over):
        copy.wait_recv()
        if d:

            @pl.loop(0, 2)
            def _(step):
                here = rows_at(start + step * 256, 256)
                value = in_ref[rows_at(mine + start + step * 256, 256), :].astype(F32)
                half[here, :] = (value + core_buf[here, :].astype(F32)).astype(BF16)

            first[which, d] = send(
                half.at[rows_at(start, 512)], buf1.at[which, d - 1], (xs, ys)[which][d - 1]
            )
    second = {}
    for which in range(2):
        for d in range(1, 4):
            first[which, d].wait_recv()
        for d in (1, 2, 3, 0):
            piece = lax.rem(own[1 - which] + d, 4) * 128
            here = rows_at(piece, 128)
            start = which * 2048 + own[which] * 512 + piece
            total = in_ref[rows_at(mine + start, 128), :].astype(F32) + core_buf[rows_at(start, 128), :].astype(F32)
            for e in range(3):
                total += buf1[which, e, here, :].astype(F32)
            if d:
                sum1[which, here, :] = total.astype(BF16)
                second[which, d] = send(sum1.at[which, here], buf2.at[which, d - 1], (ys, xs)[which][d - 1])
            else:
                sum2[:, which] = total.reshape(8, 16, 128)
    for which in range(2):
        for d in range(1, 4):
            second[which, d].wait_recv()
        sum2[:, which] = sum2[:, which] + (
            buf2[which, 0].astype(F32) + buf2[which, 1].astype(F32) + buf2[which, 2].astype(F32)
        ).reshape(8, 16, 128)
    third = [send(sum2.at[lax.rem(z + d, 8)], buf3.at[d - 1], zs[d - 1]) for d in range(1, 8)]
    for copy in third:
        copy.wait_recv()
    total = sum2[z]
    for d in range(7):
        total += buf3[d]
    base = (mine + x * 512 + y * 128, mine + 2048 + y * 512 + x * 128)
    back = {}
    for which in range(2):
        block = out_ref.at[rows_at(base[which] + z * 16, 16)]
        out_ref[rows_at(base[which] + z * 16, 16), :] = total[which].astype(BF16)
        for d in range(1, 8):
            back[which, d] = send(block, block, zs[d - 1])
    wide = {}
    for which in range(2):
        for d in range(1, 8):
            back[which, d].wait_recv()
        block = out_ref.at[rows_at(base[which], 128)]
        for d in range(1, 4):
            wide[which, d] = send(block, block, (ys, xs)[which][d - 1])
    last, across = {}, []
    for which in range(2):
        for d in range(1, 4):
            wide[which, d].wait_recv()
        block = out_ref.at[rows_at(mine + which * 2048 + own[which] * 512, 512)]
        for d in range(1, 4):
            last[which, d] = send(block, block, (xs, ys)[which][d - 1])
        across.append(send(block, block, partner))
    for d in range(1, 4):
        for which in range(2):
            last[which, d].wait_recv()
            block = out_ref.at[rows_at(mine + which * 2048 + lax.rem(own[which] + 4 - d, 4) * 512, 512)]
            across.append(send(block, block, partner))
    for copy in across:
        copy.wait_recv()
    for copy in started:
        copy.wait_send()


def reduce_all(values):
    return pl.pallas_call(
        reduce_kernel,
        out_shape=jax.ShapeDtypeStruct((8192, 128), BF16),
        in_specs=[pl.BlockSpec(memory_space=pltpu.VMEM)],
        out_specs=pl.BlockSpec(memory_space=pltpu.VMEM),
        scratch_shapes=[
            pltpu.VMEM((4096, 128), BF16),
            pltpu.VMEM((4096, 128), BF16),
            pltpu.VMEM((2, 3, 512, 128), BF16),
            pltpu.VMEM((2, 512, 128), BF16),
            pltpu.VMEM((2, 3, 128, 128), BF16),
            pltpu.VMEM((8, 2, 16, 128), F32),
            pltpu.VMEM((7, 2, 16, 128), F32),
            pltpu.SemaphoreType.DMA((61,)),
            pltpu.SemaphoreType.DMA((61,)),
        ],
        compiler_params=pltpu.CompilerParams(
            collective_id=0, has_side_effects=True, vmem_limit_bytes=VMEM_LIMIT
        ),
        name="reduce_all",
    )(values)


def pair_sum_kernel(in_ref, out_ref, got, send_sem, recv_sem):
    x, y, z, core = place()
    partner = peer(x, y, z, 1 - core)
    barrier = pltpu.get_barrier_semaphore()
    pl.semaphore_signal(barrier, inc=1, device_id=partner, device_id_type=MESH)
    pl.semaphore_wait(barrier, 1)
    copies = []
    for part in range(4):
        here = pl.ds(part * 1024, 1024)
        copy = pltpu.make_async_remote_copy(
            src_ref=in_ref.at[here], dst_ref=got.at[here], send_sem=send_sem.at[part],
            recv_sem=recv_sem.at[part], device_id=partner, device_id_type=MESH,
        )
        copy.start()
        copies.append(copy)
    for part in range(4):
        here = pl.ds(part * 1024, 1024)
        copies[part].wait()
        out_ref[here, :] = in_ref[here, :].astype(F32) + got[here, :].astype(F32)


def pair_sum(values):
    return pl.pallas_call(
        pair_sum_kernel,
        out_shape=jax.ShapeDtypeStruct((4096, 128), F32),
        in_specs=[pl.BlockSpec(memory_space=pltpu.VMEM)],
        out_specs=pl.BlockSpec(memory_space=pltpu.VMEM),
        scratch_shapes=[
            pltpu.VMEM((4096, 128), BF16),
            pltpu.SemaphoreType.DMA((4,)),
            pltpu.SemaphoreType.DMA((4,)),
        ],
        compiler_params=pltpu.CompilerParams(
            collective_id=1, has_side_effects=True, vmem_limit_bytes=VMEM_LIMIT
        ),
        name="pair_sum",
    )(values)


def params():
    return pltpu.CompilerParams(vmem_limit_bytes=VMEM_LIMIT)


def iota(shape, dimension):
    return lax.broadcasted_iota(jnp.int32, shape, dimension)


def build_kernel(owner_ref, row_ref, query_ref, slot_ref, place_ref, rank, rows, table):
    x, y, z, _ = place()
    fill = jnp.zeros((115, 256), F32)
    owner = jnp.concatenate([owner_ref[...].astype(F32), fill], axis=0).T.astype(jnp.int32)
    row = jnp.concatenate([row_ref[...].astype(F32), fill], axis=0).T
    dz = (lax.bitwise_and(owner, 7) - z + 8) & 7
    dx = (lax.bitwise_and(lax.shift_right_logical(owner, 3), 3) - x + 4) & 3
    dy = (lax.shift_right_logical(owner, 5) - y + 4) & 3
    relative = dz * 16 + dy * 4 + dx
    owner = owner.astype(F32)
    lane = iota((256, 128), 1)
    named = jnp.zeros((256, 128), F32)
    wanted = jnp.zeros((256, 128), F32)
    for f in range(13):
        here = relative[:, f : f + 1] == lane
        named = jnp.where(here, 1.0, named)
        wanted = jnp.where(here, row[:, f : f + 1], wanted)
    before = jnp.where(iota((256, 256), 1) < iota((256, 256), 0), 1.0, 0.0).astype(BF16)
    count = jnp.dot(before, named.astype(BF16), preferred_element_type=F32)
    back_x = (4 - dx) & 3
    block = ((((4 - dy) & 3) * 4 + back_x) * 8 + ((8 - dz) & 7)) * 64
    block, late = block.astype(F32), (4 * back_x).astype(F32)
    slots = jnp.zeros((256, 128), F32)
    places = jnp.zeros((256, 128), F32)
    for f in range(13):
        here = relative[:, f : f + 1] == lane
        mine = jnp.sum(jnp.where(here, count, 0.0), axis=1, keepdims=True)
        slots = jnp.where(lane == f, owner[:, f : f + 1] * STRIDE + mine, slots)
        inside = jnp.where(mine < float(EARLY), mine, mine + late[:, f : f + 1])
        places = jnp.where(lane == f, block[:, f : f + 1] + inside, places)
    slot_ref[...] = slots.T[0:16, :].astype(jnp.int32)
    place_ref[...] = places.T[0:16, :].astype(jnp.int32)
    rank[...] = jnp.where(named > 0.0, count, -1.0)
    rows[...] = wanted
    table[...] = jnp.zeros((128, 128), F32)

    for p in range(CAP):
        chosen = jnp.where(rank[...] == float(p), rows[...], 0.0)
        table[p : p + 1, :] = jnp.sum(chosen, axis=0, keepdims=True)

    query_ref[...] = table[...].T.astype(jnp.int32).reshape(8, 16, 128)


def build_requests(cold_owner, cold_row):
    return pl.pallas_call(
        build_kernel,
        out_shape=(
            jax.ShapeDtypeStruct((8, 16, 128), jnp.int32),
            jax.ShapeDtypeStruct((16, 256), jnp.int32),
            jax.ShapeDtypeStruct((16, 256), jnp.int32),
        ),
        scratch_shapes=[pltpu.VMEM((256, 128), F32), pltpu.VMEM((256, 128), F32), pltpu.VMEM((128, 128), F32)],
        compiler_params=params(),
        name="build_requests",
    )(cold_owner, cold_row)


def source_of(r, x, y, z):
    dz, dx, dy = lax.rem(r, 8), lax.rem(lax.div(r, 8), 4), lax.div(r, 32)
    return lax.rem(y - dy + 4, 4) * 32 + lax.rem(x - dx + 4, 4) * 8 + lax.rem(z - dz + 8, 8)


def widen(wide, ref, rows):
    @pl.loop(0, rows // 256)
    def _(step):
        here = pl.ds(pl.multiple_of(step * 256, 256), 256)
        wide[here, :] = ref[here, :].astype(F32)


def front_kernel(
    query_ref, table_ref, index_ref, hot_table_ref, dense_ref, weight_ref, top_ref,
    want_ref, got_ref, near_ref, bottom_ref, square_ref,
    tall, middle, turned, wanted, wide, wide_hot, held, chosen, passing, send_sem, recv_sem, local_sem,
):
    x, y, z, core = place()
    plane = [(dx, dy) for dy in range(4) for dx in range(4)]
    zs = [peer(x, y, lax.rem(z + d, NZ), core) for d in range(1, NZ)]
    xys = [peer(lax.rem(x + dx, NX), lax.rem(y + dy, NY), z, core) for dx, dy in plane[1:]]
    barrier = pltpu.get_barrier_semaphore()
    for other in zs + xys:
        pl.semaphore_signal(barrier, inc=1, device_id=other, device_id_type=MESH)
    widen(wide, table_ref, 4096)
    pl.semaphore_wait(barrier, len(zs) + len(xys))

    started = []

    def send(src, dst, device):
        index = len(started)
        copy = pltpu.make_async_remote_copy(
            src_ref=src, dst_ref=dst, send_sem=send_sem.at[index], recv_sem=recv_sem.at[index],
            device_id=device, device_id_type=MESH,
        )
        copy.start()
        started.append(copy)
        return copy

    copies = [send(query_ref.at[d], middle.at[d], zs[d - 1]) for d in range(1, 8)]
    middle[0] = query_ref[0]
    for copy in copies:
        copy.wait_recv()
    for d in range(8):
        for k in range(16):
            turned[k, d : d + 1, :] = middle[d, k : k + 1, :]
    copies = [send(turned.at[k], want_ref.at[k], xys[k - 1]) for k in range(1, 16)]
    want_ref[0] = turned[0]
    for copy in copies:
        copy.wait_recv()
    copy = pltpu.make_async_copy(want_ref, wanted, local_sem)
    copy.start()
    copy.wait()

    order = (2, 1, 3, 0)
    along = {}
    copies = []

    def collect(dy):
        @pl.loop(0, 8)
        def _(d):
            back = lax.rem(8 - d, 8)
            for tile in range(13):
                rows = []
                for e in range(16):
                    dx, p = (tile // 3, tile % 3 * 16 + e) if tile < 12 else (e // 4, EARLY + e % 4)
                    k = (4 - dy) % 4 * 4 + (4 - dx) % 4
                    rows.append(wide[pl.ds(wanted[k, back, p], 1), :])
                chosen[dy, d, tile * 16 : tile * 16 + 16, :] = jnp.concatenate(rows, axis=0).astype(BF16)

        for d in range(1, 8):
            along[dy, d] = send(chosen.at[dy, d], passing.at[dy, d], zs[d - 1])
        passing[dy, 0] = chosen[dy, 0]

    def pass_on(dy):
        for d in range(1, 8):
            along[dy, d].wait_recv()
        for dx in range(4):
            early = passing.at[dy, :, pl.ds(dx * EARLY, EARLY)]
            late = passing.at[dy, :, pl.ds(4 * EARLY, 16)]
            k = dy * 4 + dx
            if k:
                copies.append(send(early, got_ref.at[k, :, pl.ds(0, EARLY)], xys[k - 1]))
                copies.append(send(late, got_ref.at[k, :, pl.ds(EARLY, 16)], xys[k - 1]))
            else:
                got_ref[0, :, 0:EARLY, :] = passing[0, :, 0:EARLY, :]
                got_ref[0, :, EARLY:64, :] = passing[0, :, 4 * EARLY : 4 * EARLY + 16, :]

    collect(order[0])
    collect(order[1])
    widen(wide_hot, hot_table_ref, 4096)
    bottom = jnp.maximum(jnp.dot(dense_ref[...], weight_ref[...], preferred_element_type=F32), 0.0)
    bottom_ref[...] = bottom.astype(BF16)
    held[...] = bottom

    @pl.loop(0, 32)
    def _(g):
        near_ref[g, 0:16, :] = jnp.concatenate(
            [held[pl.ds(pl.multiple_of(g * 8, 8), 8), :]]
            + [wide_hot[pl.ds(index_ref[0, g * 8 + k], 1), :] for k in range(8)], axis=0
        ).astype(BF16)
        for f in range(1, 13, 2):
            rows = [wide_hot[pl.ds(index_ref[f + k // 8, g * 8 + k % 8], 1), :] for k in range(16)]
            near_ref[g, 8 + f * 8 : 24 + f * 8, :] = jnp.concatenate(rows, axis=0).astype(BF16)

    pass_on(order[0])
    collect(order[2])
    pass_on(order[1])
    collect(order[3])
    tall[464:512, :] = jnp.zeros((48, 1024), BF16)
    tall[0:479, :] = top_ref[...]

    @pl.loop(0, 7)
    def _(b):
        i = 4 * b + (iota((128, 512), 0) >> 5)
        j = iota((128, 512), 0) & 31
        high, low = jnp.maximum(i, j), jnp.minimum(i, j)
        source = 128 + ((high * (high - 1)) >> 1) + low
        source = jnp.where((high == low) | (high > 26), -1, source)
        pick = jnp.where(source == iota((128, 512), 1), 1.0, 0.0).astype(BF16)
        square_ref[pl.ds(pl.multiple_of(b * 128, 128), 128), :] = jnp.dot(
            pick, tall[...], preferred_element_type=F32
        ).astype(BF16)

    pass_on(order[2])
    pass_on(order[3])
    for copy in copies:
        copy.wait_recv()
    for copy in started:
        copy.wait_send()


def front_part(query, table, hot_index, hot_table, dense, weight, top):
    vmem = pl.BlockSpec(memory_space=pltpu.VMEM)
    return pl.pallas_call(
        front_kernel,
        out_shape=(
            jax.ShapeDtypeStruct((16, 8, 128), jnp.int32),
            jax.ShapeDtypeStruct((16, 8, 64, 128), BF16),
            jax.ShapeDtypeStruct((32, 112, 128), BF16),
            jax.ShapeDtypeStruct((256, 128), BF16),
            jax.ShapeDtypeStruct((896, 1024), BF16),
        ),
        in_specs=[vmem, vmem, pl.BlockSpec(memory_space=pltpu.SMEM), vmem, vmem, vmem, vmem],
        out_specs=(vmem,) * 5,
        scratch_shapes=[
            pltpu.VMEM((512, 1024), BF16),
            pltpu.VMEM((8, 16, 128), jnp.int32),
            pltpu.VMEM((16, 8, 128), jnp.int32),
            pltpu.SMEM((16, 8, 128), jnp.int32),
            pltpu.VMEM((4096, 128), F32),
            pltpu.VMEM((4096, 128), F32),
            pltpu.VMEM((256, 128), F32),
            pltpu.VMEM((4, 8, 208, 128), BF16),
            pltpu.VMEM((4, 8, 208, 128), BF16),
            pltpu.SemaphoreType.DMA((80,)),
            pltpu.SemaphoreType.DMA((80,)),
            pltpu.SemaphoreType.DMA,
        ],
        compiler_params=pltpu.CompilerParams(collective_id=2, has_side_effects=True, vmem_limit_bytes=VMEM_LIMIT),
        name="front_part",
    )(query, table, hot_index, hot_table, dense, weight, top)


def main_kernel(
    slot_ref, place_ref, got_ref, near_ref, bottom_ref, weight0_ref, weight_ref, out_weight_ref, click_ref,
    sent_ref, hot_ref, low_ref, grad_ref,
    wide, stack, far, pairs, hidden, slope, terms,
):
    widen(wide, got_ref, 8192)
    for e in range(UNROLL):
        far[e, 104:144, :] = jnp.zeros((40, 128), F32)
    same = (iota((256, 256), 0) & 7) == (iota((256, 256), 1) & 7)
    fold = jnp.where((iota((256, 128), 0) >> 3) == (iota((256, 128), 1) & 31), 1.0, 0.0).astype(BF16)
    unfold = jnp.where((iota((128, 256), 1) >> 3) == (iota((128, 256), 0) & 31), 1.0, 0.0).astype(BF16)
    quarter = iota((8, 128), 1) >> 5
    zero8 = jnp.zeros((8, 128), F32)

    @pl.loop(0, 32 // UNROLL)
    def _(step):
        groups = [step * UNROLL + e for e in range(UNROLL)]
        for e, g in enumerate(groups):
            for f in range(13):
                for k in range(8):
                    far[e, f * 8 + k : f * 8 + k + 1, :] = wide[pl.ds(place_ref[f, g * 8 + k], 1), :]
        values = [jnp.concatenate([near_ref[g], far[e].astype(BF16)], axis=0) for e, g in enumerate(groups)]
        dots = [
            lax.dot_general(value, value, (((1,), (1,)), ((), ())), preferred_element_type=F32) for value in values
        ]
        dots = [jnp.where(same, dot, 0.0).astype(BF16) for dot in dots]
        folds = [jnp.dot(dot, fold, preferred_element_type=F32) for dot in dots]
        for e, g in enumerate(groups):
            stack[g] = values[e]
            for b in range(7):
                block = zero8
                for q in range(4):
                    i = 4 * b + q
                    block = jnp.where(quarter == q, folds[e][i * 8 : i * 8 + 8, :], block)
                pairs[pl.ds(pl.multiple_of(g * 8, 8), 8), b * 128 : b * 128 + 128] = block

    for b in range(7):
        i = 4 * b + (iota((256, 128), 1) >> 5)
        j = iota((256, 128), 1) & 31
        low_ref[:, b * 128 : b * 128 + 128] = jnp.where(i > j, pairs[:, b * 128 : b * 128 + 128], 0.0).astype(BF16)

    total = jnp.zeros((256, 128), F32)
    for n in range(4):
        here = slice(n * 256, n * 256 + 256)
        hidden[:, here] = jnp.dot(bottom_ref[...], weight0_ref[0:128, here], preferred_element_type=F32) + jnp.dot(
            low_ref[...], weight_ref[:, here], preferred_element_type=F32
        )
    for n in range(8):
        here = slice(n * 128, n * 128 + 128)
        v = hidden[:, here]
        c = 0.7978845608028654
        square = v * v
        t = jnp.tanh(c * v * (1.0 + 0.044715 * square))
        weight = out_weight_ref[:, here].astype(F32)
        act = (0.5 * v * (1.0 + t)).astype(BF16).astype(F32)
        total = total + act * weight
        slope[:, here] = weight * (0.5 * (1.0 + t) + 0.5 * c * v * (1.0 - t * t) * (1.0 + 0.134145 * square))
    logits = jnp.sum(total, axis=1, keepdims=True)
    clicks = jnp.broadcast_to(click_ref[...].astype(F32), (128, 256)).T[:, 0:1]
    errors = 1.0 / (1.0 + jnp.exp(-logits)) - clicks
    grad_ref[...] = (slope[...] * errors).astype(BF16)
    for b in range(7):
        here = slice(b * 128, b * 128 + 128)
        pairs[:, here] = lax.dot_general(
            grad_ref[...], weight_ref[here, :], (((1,), (1,)), ((), ())), preferred_element_type=F32
        )

    @pl.loop(0, 7)
    def _(step):
        wide[pl.ds(pl.multiple_of(step * 1024, 1024), 1024), :] = jnp.zeros((1024, 128), F32)

    @pl.loop(0, 32 // UNROLL)
    def _(step):
        groups = [step * UNROLL + e for e in range(UNROLL)]
        spreads = []
        for g in groups:
            rows = []
            for b in range(7):
                block = pairs[pl.ds(pl.multiple_of(g * 8, 8), 8), b * 128 : b * 128 + 128]
                for q in range(4):
                    rows.append(jnp.where(quarter == q, block, 0.0))
            rows += [zero8] * 4
            spreads.append(jnp.concatenate(rows, axis=0).astype(BF16))
        spreads = [jnp.dot(spread, unfold, preferred_element_type=F32) for spread in spreads]
        spreads = [jnp.where(same, spread, 0.0).astype(BF16) for spread in spreads]
        results = [jnp.dot(spread, stack[g], preferred_element_type=F32) for spread, g in zip(spreads, groups)]
        for e, g in enumerate(groups):
            for f in range(13):
                hot_ref[f, pl.ds(pl.multiple_of(g * 8, 8), 8), :] = results[e][8 + f * 8 : 16 + f * 8, :]
            terms[e] = results[e][112:216, :]
        for e, g in enumerate(groups):
            for f in range(13):
                for k in range(8):
                    row = f * 8 + k
                    wide[pl.ds(slot_ref[f, g * 8 + k], 1), :] = terms[e, row : row + 1, :]

    @pl.loop(0, 16)
    def _(step):
        for e in range(8):
            d = step * 8 + e
            sent_ref[d] = wide[pl.ds(pl.multiple_of(d * STRIDE, 8), CAP), :].astype(BF16)


def main_part(slot, places, got, near, bottom, weight0, weight, out_weight, clicks):
    vmem = pl.BlockSpec(memory_space=pltpu.VMEM)
    return pl.pallas_call(
        main_kernel,
        out_shape=(
            jax.ShapeDtypeStruct((128, CAP, 128), BF16),
            jax.ShapeDtypeStruct((13, 256, 128), F32),
            jax.ShapeDtypeStruct((256, 896), BF16),
            jax.ShapeDtypeStruct((256, 1024), BF16),
        ),
        in_specs=[pl.BlockSpec(memory_space=pltpu.SMEM)] * 2 + [vmem] * 7,
        out_specs=(vmem,) * 4,
        scratch_shapes=[
            pltpu.VMEM((8192, 128), F32),
            pltpu.VMEM((32, 256, 128), BF16),
            pltpu.VMEM((UNROLL, 144, 128), F32),
            pltpu.VMEM((256, 896), F32),
            pltpu.VMEM((256, 1024), F32),
            pltpu.VMEM((256, 1024), F32),
            pltpu.VMEM((UNROLL, 104, 128), F32),
        ],
        compiler_params=params(),
        name="main_part",
    )(slot, places, got, near, bottom, weight0, weight, out_weight, clicks)


def hot_kernel(row_ref, value_ref, bottom_ref, low_ref, grad_ref, out_ref, halves, top):
    columns = jnp.concatenate([(row_ref[...] >> 11).astype(F32), jnp.zeros((115, 256), F32)], axis=0).T
    for f in range(13):
        high = columns[:, f : f + 1]
        value = value_ref[f]
        halves[f * 256 : f * 256 + 256, 0:128] = jnp.where(high == 0.0, value, 0.0).astype(BF16)
        halves[f * 256 : f * 256 + 256, 128:256] = jnp.where(high == 0.0, 0.0, value).astype(BF16)

    @pl.loop(0, 8)
    def _(m):
        start = pl.multiple_of(m * 256, 256)
        wanted = iota((256, 256), 0) + m * 256
        hits = [
            jnp.where((jnp.broadcast_to(row_ref[f : f + 1, :], (256, 256)) & 2047) == wanted, 1.0, 0.0).astype(BF16)
            for f in range(13)
        ]
        total = jnp.dot(jnp.concatenate(hits, axis=1), halves[...], preferred_element_type=F32)
        out_ref[pl.ds(start, 256), :] = total[:, 0:128].astype(BF16)
        out_ref[pl.ds(start + 2048, 256), :] = total[:, 128:256].astype(BF16)

    top[472:480, :] = jnp.zeros((8, 1024), F32)
    top[0:128, :] = lax.dot_general(
        bottom_ref[...], grad_ref[...], (((0,), (0,)), ((), ())), preferred_element_type=F32
    )
    for b in range(7):
        part = lax.dot_general(
            low_ref[:, b * 128 : b * 128 + 128], grad_ref[...], (((0,), (0,)), ((), ())), preferred_element_type=F32
        )
        for q in range(4):
            i = 4 * b + q
            if 0 < i < 27:
                at = 128 + i * (i - 1) // 2
                top[at : at + i, :] = part[q * 32 : q * 32 + i, :]
    for n in range(8):
        out_ref[4096 + n * 480 : 4576 + n * 480, :] = top[:, n * 128 : n * 128 + 128].astype(BF16)
    out_ref[7936:8192, :] = jnp.zeros((256, 128), BF16)


def hot_and_top(row, value, bottom, low, grad):
    return pl.pallas_call(
        hot_kernel,
        out_shape=jax.ShapeDtypeStruct((8192, 128), BF16),
        scratch_shapes=[pltpu.VMEM((3328, 256), BF16), pltpu.VMEM((480, 1024), F32)],
        compiler_params=params(),
        name="hot_and_top",
    )(row, value, bottom, low, grad)


def cold_kernel(want_ref, value_ref, out_ref, halves, joined):
    x, y, z, _ = place()
    pad = jnp.zeros((64 - CAP, 128), F32)
    even, odd = want_ref[pl.ds(0, 64, stride=2), :], want_ref[pl.ds(1, 64, stride=2), :]
    joined[...] = jnp.where(iota((64, 128), 1) < 64, even, pltpu.roll(odd, 64, 1)) & 2047
    columns = (want_ref[...] >> 11).astype(F32).T
    for r in range(128):
        high = columns[0:64, r : r + 1]
        value = jnp.concatenate([value_ref[source_of(r, x, y, z)].astype(F32), pad], axis=0)
        halves[r * 64 : r * 64 + 64, 0:128] = jnp.where(high == 0.0, value, 0.0).astype(BF16)
        halves[r * 64 : r * 64 + 64, 128:256] = jnp.where(high == 0.0, 0.0, value).astype(BF16)

    @pl.loop(0, 8)
    def _(m):
        start = pl.multiple_of(m * 256, 256)
        wanted = iota((256, 128), 0) + m * 256
        total = jnp.zeros((256, 256), F32)
        for n in range(4):
            hits = [
                jnp.where(jnp.broadcast_to(joined[t : t + 1, :], (256, 128)) == wanted, 1.0, 0.0).astype(BF16)
                for t in range(n * 16, n * 16 + 16)
            ]
            total = total + jnp.dot(
                jnp.concatenate(hits, axis=1), halves[n * 2048 : n * 2048 + 2048, :], preferred_element_type=F32
            )
        out_ref[pl.ds(start, 256), :] = total[:, 0:128].astype(BF16)
        out_ref[pl.ds(start + 2048, 256), :] = total[:, 128:256].astype(BF16)


def cold_sums(want, value):
    return pl.pallas_call(
        cold_kernel,
        out_shape=jax.ShapeDtypeStruct((4096, 128), BF16),
        scratch_shapes=[pltpu.VMEM((8192, 256), BF16), pltpu.VMEM((64, 128), jnp.int32)],
        compiler_params=params(),
        name="cold_sums",
    )(want, value)


def format_kernel(in_ref, hot_ref, top_ref):
    hot_ref[...] = in_ref[0:4096, :].astype(F32)
    for n in range(8):
        top_ref[:, n * 128 : n * 128 + 128] = in_ref[4096 + n * 480 : 4576 + n * 480, :].astype(F32)[0:479, :]


def format_sums(values):
    return pl.pallas_call(
        format_kernel,
        out_shape=(jax.ShapeDtypeStruct((4096, 128), F32), jax.ShapeDtypeStruct((479, 1024), F32)),
        compiler_params=params(),
        name="format_sums",
    )(values)


def body(
    dense_feats,
    bottom_weight,
    top_weight,
    out_weight,
    hot_table,
    cold_table,
    hot_index,
    cold_owner,
    cold_row,
    clicks,
):
    query, slot, places = build_requests(cold_owner.T, cold_row.T)
    hot_fields = hot_index.T
    wanted, got, near, bottom, weight = front_part(
        query, cold_table, hot_fields, hot_table, dense_feats, bottom_weight, top_weight
    )
    wanted = wanted.reshape(128, 128)
    outgoing, hot_terms, low, grad = main_part(
        slot, places, got.reshape(8192, 128), near, bottom, top_weight, weight, out_weight.reshape(1, 1024), clicks.reshape(1, 256)
    )
    returned = lax.all_to_all(outgoing, "dp", split_axis=0, concat_axis=0, tiled=True)
    sums = hot_and_top(hot_fields, hot_terms, bottom, low, grad)
    hot_grad, top_grad = format_sums(reduce_all(sums))
    local_cold = cold_sums(wanted, returned)
    cold_grad = pair_sum(local_cold)
    return (hot_grad, cold_grad, top_grad)


def solution(mesh):
    return jax.shard_map(
        body,
        mesh=mesh,
        in_specs=(
            P(("dp", "rep"), None),
            P(),
            P(),
            P(),
            P(),
            P("dp", None),
            P(("dp", "rep"), None),
            P(("dp", "rep"), None),
            P(("dp", "rep"), None),
            P(("dp", "rep")),
        ),
        out_specs=(P(), P("dp", None), P()),
        check_vma=False,
    )
```

```python
import jax
import jax.numpy as jnp
from jax import lax
from jax.experimental import pallas as pl
from jax.experimental.pallas import tpu as pltpu
from jax.sharding import PartitionSpec as P

MESH = pl.DeviceIdType.MESH
NX, NY, NZ = 4, 4, 8
VMEM_LIMIT = 48 * 1024 * 1024
F32 = jnp.float32
BF16 = jnp.bfloat16
CAP = 52
EARLY = 48
UNROLL = 4


def place():
    me = lax.axis_index("dp")
    core = lax.axis_index("rep")
    z = lax.rem(me, NZ)
    x = lax.rem(lax.div(me, NZ), NX)
    y = lax.div(me, NZ * NX)
    return x, y, z, core


def peer(x, y, z, core):
    return (y * (NX * NZ) + x * NZ + z, core)


def rows_at(start, size):
    return pl.ds(pl.multiple_of(start, 16), size)


def params():
    return pltpu.CompilerParams(vmem_limit_bytes=VMEM_LIMIT)


def iota(shape, dimension):
    return lax.broadcasted_iota(jnp.int32, shape, dimension)


def build_kernel(owner_ref, row_ref, query_ref, slot_ref, place_ref, rank, rows, table):
    x, y, z, _ = place()
    fill = jnp.zeros((115, 256), F32)
    owner = jnp.concatenate([owner_ref[...].astype(F32), fill], axis=0).T.astype(jnp.int32)
    row = jnp.concatenate([row_ref[...].astype(F32), fill], axis=0).T
    dz = (lax.bitwise_and(owner, 7) - z + 8) & 7
    dx = (lax.bitwise_and(lax.shift_right_logical(owner, 3), 3) - x + 4) & 3
    dy = (lax.shift_right_logical(owner, 5) - y + 4) & 3
    relative = dz * 16 + dy * 4 + dx
    lane = iota((256, 128), 1)
    named = jnp.zeros((256, 128), F32)
    wanted = jnp.zeros((256, 128), F32)
    for f in range(13):
        here = relative[:, f : f + 1] == lane
        named = jnp.where(here, 1.0, named)
        wanted = jnp.where(here, row[:, f : f + 1], wanted)
    before = jnp.where(iota((256, 256), 1) < iota((256, 256), 0), 1.0, 0.0).astype(BF16)
    count = jnp.dot(before, named.astype(BF16), preferred_element_type=F32)
    back_x = (4 - dx) & 3
    block = ((((4 - dy) & 3) * 4 + back_x) * 8 + ((8 - dz) & 7)) * 64
    block, late = block.astype(F32), (4 * back_x).astype(F32)
    base = ((dy * 8 + dz) * 208).astype(F32)
    ahead = dx.astype(F32)
    slots = jnp.zeros((256, 128), F32)
    places = jnp.zeros((256, 128), F32)
    for f in range(13):
        here = relative[:, f : f + 1] == lane
        mine = jnp.sum(jnp.where(here, count, 0.0), axis=1, keepdims=True)
        past = mine - float(EARLY)
        over = ahead[:, f : f + 1]
        spot = jnp.where(past < 0.0, over * float(EARLY) + mine, 4.0 * EARLY + 4.0 * over + past)
        slots = jnp.where(lane == f, base[:, f : f + 1] + spot, slots)
        inside = jnp.where(mine < float(EARLY), mine, mine + late[:, f : f + 1])
        places = jnp.where(lane == f, block[:, f : f + 1] + inside, places)
    slot_ref[...] = slots.T[0:16, :].astype(jnp.int32)
    place_ref[...] = places.T[0:16, :].astype(jnp.int32)
    rank[...] = jnp.where(named > 0.0, count, -1.0)
    rows[...] = wanted
    table[...] = jnp.zeros((128, 128), F32)

    for p in range(CAP):
        chosen = jnp.sum(jnp.where(rank[...] == float(p), rows[...], 0.0), axis=0, keepdims=True)
        if p < EARLY:
            table[p : p + 1, :] = chosen
        else:
            for e in range(4):
                at = EARLY + e * 4 + p - EARLY
                table[at : at + 1, :] = jnp.where((iota((1, 128), 1) & 3) == e, chosen, -1.0)

    query_ref[...] = table[...].T.astype(jnp.int32).reshape(8, 16, 128)


def build_requests(cold_owner, cold_row):
    return pl.pallas_call(
        build_kernel,
        out_shape=(
            jax.ShapeDtypeStruct((8, 16, 128), jnp.int32),
            jax.ShapeDtypeStruct((16, 256), jnp.int32),
            jax.ShapeDtypeStruct((16, 256), jnp.int32),
        ),
        scratch_shapes=[pltpu.VMEM((256, 128), F32), pltpu.VMEM((256, 128), F32), pltpu.VMEM((128, 128), F32)],
        compiler_params=params(),
        name="build_requests",
    )(cold_owner, cold_row)


def widen(wide, ref, rows):
    @pl.loop(0, rows // 256)
    def _(step):
        here = pl.ds(pl.multiple_of(step * 256, 256), 256)
        wide[here, :] = ref[here, :].astype(F32)


def front_kernel(
    query_ref, table_far, index_far, hot_table_far, dense_far, weight_far, top_far,
    want_ref, got_ref, near_ref, bottom_ref, square_ref,
    table_ref, index_ref, hot_table_ref, dense_ref, weight_ref, top_ref, tall, middle, turned, wanted, wide, wide_hot, held, chosen, passing, send_sem, recv_sem, local_sem,
):
    x, y, z, core = place()
    plane = [(dx, dy) for dy in range(4) for dx in range(4)]
    zs = [peer(x, y, lax.rem(z + d, NZ), core) for d in range(1, NZ)]
    xys = [peer(lax.rem(x + dx, NX), lax.rem(y + dy, NY), z, core) for dx, dy in plane[1:]]
    barrier = pltpu.get_barrier_semaphore()
    for other in zs + xys:
        pl.semaphore_signal(barrier, inc=1, device_id=other, device_id_type=MESH)
    fetched = (
        (table_far, table_ref), (index_far, index_ref), (hot_table_far, hot_table_ref),
        (dense_far, dense_ref), (weight_far, weight_ref), (top_far, top_ref),
    )
    fetches = [pltpu.make_async_copy(src, dst, local_sem.at[1 + n]) for n, (src, dst) in enumerate(fetched)]
    for fetch in fetches:
        fetch.start()
    pl.semaphore_wait(barrier, len(zs) + len(xys))

    started = []

    def send(src, dst, device):
        index = len(started)
        copy = pltpu.make_async_remote_copy(
            src_ref=src, dst_ref=dst, send_sem=send_sem.at[index], recv_sem=recv_sem.at[index],
            device_id=device, device_id_type=MESH,
        )
        copy.start()
        started.append(copy)
        return copy

    copies = [send(query_ref.at[d], middle.at[d], zs[d - 1]) for d in range(1, 8)]
    middle[0] = query_ref[0]
    fetches[0].wait()
    widen(wide, table_ref, 4096)
    for copy in copies:
        copy.wait_recv()
    for d in range(8):
        for k in range(16):
            turned[k, d : d + 1, :] = middle[d, k : k + 1, :]
    copies = [send(turned.at[k], want_ref.at[k], xys[k - 1]) for k in range(1, 16)]
    want_ref[0] = turned[0]
    for copy in copies:
        copy.wait_recv()
    copy = pltpu.make_async_copy(want_ref, wanted, local_sem.at[0])
    copy.start()
    copy.wait()

    order = (2, 1, 3, 0)
    along = {}
    copies = []

    def collect(dy):
        @pl.loop(0, 8)
        def _(d):
            back = lax.rem(8 - d, 8)
            for tile in range(13):
                rows = []
                for e in range(16):
                    dx, p = (tile // 3, tile % 3 * 16 + e) if tile < 12 else (e // 4, EARLY + (4 - e // 4) % 4 * 4 + e % 4)
                    k = (4 - dy) % 4 * 4 + (4 - dx) % 4
                    rows.append(wide[pl.ds(wanted[k, back, p], 1), :])
                chosen[dy, d, tile * 16 : tile * 16 + 16, :] = jnp.concatenate(rows, axis=0).astype(BF16)

        for d in range(1, 8):
            along[dy, d] = send(chosen.at[dy, d], passing.at[dy, d], zs[d - 1])
        passing[dy, 0] = chosen[dy, 0]

    def pass_on(dy):
        for d in range(1, 8):
            along[dy, d].wait_recv()
        for dx in range(4):
            early = passing.at[dy, :, pl.ds(dx * EARLY, EARLY)]
            late = passing.at[dy, :, pl.ds(4 * EARLY, 16)]
            k = dy * 4 + dx
            if k:
                copies.append(send(early, got_ref.at[k, :, pl.ds(0, EARLY)], xys[k - 1]))
                copies.append(send(late, got_ref.at[k, :, pl.ds(EARLY, 16)], xys[k - 1]))
            else:
                got_ref[0, :, 0:EARLY, :] = passing[0, :, 0:EARLY, :]
                got_ref[0, :, EARLY:64, :] = passing[0, :, 4 * EARLY : 4 * EARLY + 16, :]

    collect(order[0])
    collect(order[1])
    for fetch in fetches[1:]:
        fetch.wait()
    widen(wide_hot, hot_table_ref, 4096)
    bottom = jnp.maximum(jnp.dot(dense_ref[...], weight_ref[...], preferred_element_type=F32), 0.0)
    bottom_ref[...] = bottom.astype(BF16)
    held[...] = bottom

    @pl.loop(0, 32)
    def _(g):
        near_ref[g, 0:16, :] = jnp.concatenate(
            [held[pl.ds(pl.multiple_of(g * 8, 8), 8), :]]
            + [wide_hot[pl.ds(index_ref[0, g * 8 + k], 1), :] for k in range(8)], axis=0
        ).astype(BF16)
        for f in range(1, 13, 2):
            rows = [wide_hot[pl.ds(index_ref[f + k // 8, g * 8 + k % 8], 1), :] for k in range(16)]
            near_ref[g, 8 + f * 8 : 24 + f * 8, :] = jnp.concatenate(rows, axis=0).astype(BF16)

    pass_on(order[0])
    collect(order[2])
    pass_on(order[1])
    collect(order[3])
    tall[464:512, :] = jnp.zeros((48, 1024), BF16)
    tall[0:479, :] = top_ref[...]

    @pl.loop(0, 7)
    def _(b):
        i = 4 * b + (iota((128, 512), 0) >> 5)
        j = iota((128, 512), 0) & 31
        high, low = jnp.maximum(i, j), jnp.minimum(i, j)
        source = 128 + ((high * (high - 1)) >> 1) + low
        source = jnp.where((high == low) | (high > 26), -1, source)
        pick = jnp.where(source == iota((128, 512), 1), 1.0, 0.0).astype(BF16)
        square_ref[pl.ds(pl.multiple_of(b * 128, 128), 128), :] = jnp.dot(
            pick, tall[...], preferred_element_type=F32
        ).astype(BF16)

    pass_on(order[2])
    pass_on(order[3])
    for copy in copies:
        copy.wait_recv()
    for copy in started:
        copy.wait_send()


def front_part(query, table, hot_index, hot_table, dense, weight, top):
    vmem = pl.BlockSpec(memory_space=pltpu.VMEM)
    return pl.pallas_call(
        front_kernel,
        out_shape=(
            jax.ShapeDtypeStruct((16, 8, 128), jnp.int32),
            jax.ShapeDtypeStruct((16, 8, 64, 128), BF16),
            jax.ShapeDtypeStruct((32, 112, 128), BF16),
            jax.ShapeDtypeStruct((256, 128), BF16),
            jax.ShapeDtypeStruct((896, 1024), BF16),
        ),
        in_specs=[vmem] + [pl.BlockSpec(memory_space=pl.ANY)] * 6,
        out_specs=(vmem,) * 5,
        scratch_shapes=[
            pltpu.VMEM((4096, 128), BF16),
            pltpu.SMEM((13, 256), jnp.int32),
            pltpu.VMEM((4096, 128), BF16),
            pltpu.VMEM((256, 256), BF16),
            pltpu.VMEM((256, 128), BF16),
            pltpu.VMEM((479, 1024), BF16),
            pltpu.VMEM((512, 1024), BF16),
            pltpu.VMEM((8, 16, 128), jnp.int32),
            pltpu.VMEM((16, 8, 128), jnp.int32),
            pltpu.SMEM((16, 8, 128), jnp.int32),
            pltpu.VMEM((4096, 128), F32),
            pltpu.VMEM((4096, 128), F32),
            pltpu.VMEM((256, 128), F32),
            pltpu.VMEM((4, 8, 208, 128), BF16),
            pltpu.VMEM((4, 8, 208, 128), BF16),
            pltpu.SemaphoreType.DMA((80,)),
            pltpu.SemaphoreType.DMA((80,)),
            pltpu.SemaphoreType.DMA((7,)),
        ],
        compiler_params=pltpu.CompilerParams(collective_id=2, has_side_effects=True, vmem_limit_bytes=60 * 1024 * 1024),
        name="front_part",
    )(query, table, hot_index, hot_table, dense, weight, top)


def main_kernel(
    slot_ref, place_ref, got_ref, near_ref, bottom_ref, weight0_ref, weight_ref, out_weight_ref, click_ref,
    sent_ref, hot_ref, low_ref, grad_ref,
    wide, stack, far, pairs, hidden, slope, terms,
):
    widen(wide, got_ref, 8192)
    for e in range(UNROLL):
        far[e, 104:144, :] = jnp.zeros((40, 128), F32)
    same = (iota((256, 256), 0) & 7) == (iota((256, 256), 1) & 7)
    fold = jnp.where((iota((256, 128), 0) >> 3) == (iota((256, 128), 1) & 31), 1.0, 0.0).astype(BF16)
    unfold = jnp.where((iota((128, 256), 1) >> 3) == (iota((128, 256), 0) & 31), 1.0, 0.0).astype(BF16)
    quarter = iota((8, 128), 1) >> 5
    zero8 = jnp.zeros((8, 128), F32)

    @pl.loop(0, 32 // UNROLL)
    def _(step):
        groups = [step * UNROLL + e for e in range(UNROLL)]
        for e, g in enumerate(groups):
            for f in range(13):
                for k in range(8):
                    far[e, f * 8 + k : f * 8 + k + 1, :] = wide[pl.ds(place_ref[f, g * 8 + k], 1), :]
        values = [jnp.concatenate([near_ref[g], far[e].astype(BF16)], axis=0) for e, g in enumerate(groups)]
        dots = [
            lax.dot_general(value, value, (((1,), (1,)), ((), ())), preferred_element_type=F32) for value in values
        ]
        dots = [jnp.where(same, dot, 0.0).astype(BF16) for dot in dots]
        folds = [jnp.dot(dot, fold, preferred_element_type=F32) for dot in dots]
        for e, g in enumerate(groups):
            stack[g] = values[e]
            for b in range(7):
                block = zero8
                for q in range(4):
                    i = 4 * b + q
                    block = jnp.where(quarter == q, folds[e][i * 8 : i * 8 + 8, :], block)
                pairs[pl.ds(pl.multiple_of(g * 8, 8), 8), b * 128 : b * 128 + 128] = block

    for b in range(7):
        i = 4 * b + (iota((256, 128), 1) >> 5)
        j = iota((256, 128), 1) & 31
        low_ref[:, b * 128 : b * 128 + 128] = jnp.where(i > j, pairs[:, b * 128 : b * 128 + 128], 0.0).astype(BF16)

    total = jnp.zeros((256, 128), F32)
    for n in range(4):
        here = slice(n * 256, n * 256 + 256)
        hidden[:, here] = jnp.dot(bottom_ref[...], weight0_ref[0:128, here], preferred_element_type=F32) + jnp.dot(
            low_ref[...], weight_ref[:, here], preferred_element_type=F32
        )
    for n in range(8):
        here = slice(n * 128, n * 128 + 128)
        v = hidden[:, here]
        c = 0.7978845608028654
        square = v * v
        t = jnp.tanh(c * v * (1.0 + 0.044715 * square))
        weight = out_weight_ref[:, here].astype(F32)
        act = (0.5 * v * (1.0 + t)).astype(BF16).astype(F32)
        total = total + act * weight
        slope[:, here] = weight * (0.5 * (1.0 + t) + 0.5 * c * v * (1.0 - t * t) * (1.0 + 0.134145 * square))
    logits = jnp.sum(total, axis=1, keepdims=True)
    clicks = jnp.broadcast_to(click_ref[...].astype(F32), (128, 256)).T[:, 0:1]
    errors = 1.0 / (1.0 + jnp.exp(-logits)) - clicks
    grad_ref[...] = (slope[...] * errors).astype(BF16)
    for b in range(7):
        here = slice(b * 128, b * 128 + 128)
        pairs[:, here] = lax.dot_general(
            grad_ref[...], weight_ref[here, :], (((1,), (1,)), ((), ())), preferred_element_type=F32
        )

    @pl.loop(0, 13)
    def _(step):
        wide[pl.ds(pl.multiple_of(step * 512, 512), 512), :] = jnp.zeros((512, 128), F32)

    @pl.loop(0, 32 // UNROLL)
    def _(step):
        groups = [step * UNROLL + e for e in range(UNROLL)]
        spreads = []
        for g in groups:
            rows = []
            for b in range(7):
                block = pairs[pl.ds(pl.multiple_of(g * 8, 8), 8), b * 128 : b * 128 + 128]
                for q in range(4):
                    rows.append(jnp.where(quarter == q, block, 0.0))
            rows += [zero8] * 4
            spreads.append(jnp.concatenate(rows, axis=0).astype(BF16))
        spreads = [jnp.dot(spread, unfold, preferred_element_type=F32) for spread in spreads]
        spreads = [jnp.where(same, spread, 0.0).astype(BF16) for spread in spreads]
        results = [jnp.dot(spread, stack[g], preferred_element_type=F32) for spread, g in zip(spreads, groups)]
        for e, g in enumerate(groups):
            for f in range(13):
                hot_ref[f, pl.ds(pl.multiple_of(g * 8, 8), 8), :] = results[e][8 + f * 8 : 16 + f * 8, :]
            terms[e] = results[e][112:216, :]
        for e, g in enumerate(groups):
            for f in range(13):
                for k in range(8):
                    row = f * 8 + k
                    wide[pl.ds(slot_ref[f, g * 8 + k], 1), :] = terms[e, row : row + 1, :]

    @pl.loop(0, 26)
    def _(step):
        here = pl.ds(pl.multiple_of(step * 256, 256), 256)
        sent_ref[here, :] = wide[here, :].astype(BF16)


def main_part(slot, places, got, near, bottom, weight0, weight, out_weight, clicks):
    vmem = pl.BlockSpec(memory_space=pltpu.VMEM)
    return pl.pallas_call(
        main_kernel,
        out_shape=(
            jax.ShapeDtypeStruct((6656, 128), BF16),
            jax.ShapeDtypeStruct((13, 256, 128), F32),
            jax.ShapeDtypeStruct((256, 896), BF16),
            jax.ShapeDtypeStruct((256, 1024), BF16),
        ),
        in_specs=[pl.BlockSpec(memory_space=pltpu.SMEM)] * 2 + [vmem] * 7,
        out_specs=(vmem,) * 4,
        scratch_shapes=[
            pltpu.VMEM((8192, 128), F32),
            pltpu.VMEM((32, 256, 128), BF16),
            pltpu.VMEM((UNROLL, 144, 128), F32),
            pltpu.VMEM((256, 896), F32),
            pltpu.VMEM((256, 1024), F32),
            pltpu.VMEM((256, 1024), F32),
            pltpu.VMEM((UNROLL, 104, 128), F32),
        ],
        compiler_params=params(),
        name="main_part",
    )(slot, places, got, near, bottom, weight0, weight, out_weight, clicks)


def hot_kernel(row_ref, value_ref, bottom_ref, low_ref, grad_ref, out_ref, halves, top):
    columns = jnp.concatenate([(row_ref[...] >> 11).astype(F32), jnp.zeros((115, 256), F32)], axis=0).T
    for f in range(13):
        high = columns[:, f : f + 1]
        value = value_ref[f]
        halves[f * 256 : f * 256 + 256, 0:128] = jnp.where(high == 0.0, value, 0.0).astype(BF16)
        halves[f * 256 : f * 256 + 256, 128:256] = jnp.where(high == 0.0, 0.0, value).astype(BF16)

    @pl.loop(0, 8)
    def _(m):
        start = pl.multiple_of(m * 256, 256)
        wanted = iota((256, 256), 0) + m * 256
        hits = [
            jnp.where((jnp.broadcast_to(row_ref[f : f + 1, :], (256, 256)) & 2047) == wanted, 1.0, 0.0).astype(BF16)
            for f in range(13)
        ]
        total = jnp.dot(jnp.concatenate(hits, axis=1), halves[...], preferred_element_type=F32)
        out_ref[pl.ds(start, 256), :] = total[:, 0:128].astype(BF16)
        out_ref[pl.ds(start + 2048, 256), :] = total[:, 128:256].astype(BF16)

    top[472:480, :] = jnp.zeros((8, 1024), F32)
    top[0:128, :] = lax.dot_general(
        bottom_ref[...], grad_ref[...], (((0,), (0,)), ((), ())), preferred_element_type=F32
    )
    for b in range(7):
        part = lax.dot_general(
            low_ref[:, b * 128 : b * 128 + 128], grad_ref[...], (((0,), (0,)), ((), ())), preferred_element_type=F32
        )
        for q in range(4):
            i = 4 * b + q
            if 0 < i < 27:
                at = 128 + i * (i - 1) // 2
                top[at : at + i, :] = part[q * 32 : q * 32 + i, :]
    for n in range(8):
        out_ref[4096 + n * 480 : 4576 + n * 480, :] = top[:, n * 128 : n * 128 + 128].astype(BF16)
    out_ref[7936:8192, :] = jnp.zeros((256, 128), BF16)


def back_kernel(
    sent_ref, want_ref, hot_row_ref, hot_value_ref, bottom_ref, low_ref, grad_ref,
    out_ref, part_ref, other_ref,
    in_ref, hot_halves, top, passing, got, halves, joined,
    core_buf, half, buf1, sum1, buf2, sum2, buf3, send_sem, recv_sem,
):
    x, y, z, core = place()
    plane = [(dx, dy) for dy in range(4) for dx in range(4)]
    partner = peer(x, y, z, 1 - core)
    zs = [peer(x, y, lax.rem(z + d, NZ), core) for d in range(1, NZ)]
    xys = [peer(lax.rem(x + dx, NX), lax.rem(y + dy, NY), z, core) for dx, dy in plane[1:]]
    xs = [xys[d - 1] for d in range(1, 4)]
    ys = [xys[4 * d - 1] for d in range(1, 4)]
    barrier = pltpu.get_barrier_semaphore()
    everyone = [partner] + zs + xys
    for other in everyone:
        pl.semaphore_signal(barrier, inc=1, device_id=other, device_id_type=MESH)
    pl.semaphore_wait(barrier, len(everyone))

    started = []

    def send(src, dst, device):
        index = len(started)
        copy = pltpu.make_async_remote_copy(
            src_ref=src, dst_ref=dst, send_sem=send_sem.at[index], recv_sem=recv_sem.at[index],
            device_id=device, device_id_type=MESH,
        )
        copy.start()
        started.append(copy)
        return copy

    along, flat = {}, []

    def set_out(dy):
        for d in range(1, 8):
            along[dy, d] = send(sent_ref.at[dy, d], passing.at[dy, d], zs[d - 1])
        passing[dy, 0] = sent_ref[dy, 0]

    def pass_on(dy):
        for d in range(1, 8):
            along[dy, d].wait_recv()
        for dx in range(4):
            early = passing.at[dy, :, pl.ds(dx * EARLY, EARLY)]
            late = passing.at[dy, :, pl.ds(4 * EARLY, 16)]
            k = dy * 4 + dx
            if k:
                flat.append(send(early, got.at[k, :, pl.ds(0, EARLY)], xys[k - 1]))
                flat.append(send(late, got.at[k, :, pl.ds(EARLY, 16)], xys[k - 1]))
            else:
                got[0, :, 0:EARLY, :] = passing[0, :, 0:EARLY, :]
                got[0, :, EARLY:64, :] = passing[0, :, 4 * EARLY : 4 * EARLY + 16, :]

    set_out(2)
    set_out(1)
    hot_kernel(hot_row_ref, hot_value_ref, bottom_ref, low_ref, grad_ref, in_ref, hot_halves, top)

    mine, other = core * 4096, (1 - core) * 4096
    own = (x, y)
    plan = [(which, d) for d in (1, 2, 3, 0) for which in (0, 1)]
    starts = [which * 2048 + lax.rem(own[which] + d, 4) * 512 for which, d in plan]
    over = [send(in_ref.at[rows_at(other + start, 512)], core_buf.at[rows_at(start, 512)], partner) for start in starts]
    pass_on(2)
    set_out(3)
    first = {}
    for (which, d), start, copy in zip(plan, starts, over):
        copy.wait_recv()
        if d:

            @pl.loop(0, 2)
            def _(step):
                here = rows_at(start + step * 256, 256)
                value = in_ref[rows_at(mine + start + step * 256, 256), :].astype(F32)
                half[here, :] = (value + core_buf[here, :].astype(F32)).astype(BF16)

            first[which, d] = send(
                half.at[rows_at(start, 512)], buf1.at[which, d - 1], (xs, ys)[which][d - 1]
            )
    pass_on(1)
    set_out(0)
    second = {}
    for which in range(2):
        for d in range(1, 4):
            first[which, d].wait_recv()
        for d in (1, 2, 3, 0):
            piece = lax.rem(own[1 - which] + d, 4) * 128
            here = rows_at(piece, 128)
            start = which * 2048 + own[which] * 512 + piece
            total = in_ref[rows_at(mine + start, 128), :].astype(F32) + core_buf[rows_at(start, 128), :].astype(F32)
            for e in range(3):
                total += buf1[which, e, here, :].astype(F32)
            if d:
                sum1[which, here, :] = total.astype(BF16)
                second[which, d] = send(sum1.at[which, here], buf2.at[which, d - 1], (ys, xs)[which][d - 1])
            else:
                sum2[:, which] = total.reshape(8, 16, 128)
    for which in range(2):
        for d in range(1, 4):
            second[which, d].wait_recv()
        sum2[:, which] = sum2[:, which] + (
            buf2[which, 0].astype(F32) + buf2[which, 1].astype(F32) + buf2[which, 2].astype(F32)
        ).reshape(8, 16, 128)
    third = [send(sum2.at[lax.rem(z + d, 8)], buf3.at[d - 1], zs[d - 1]) for d in range(1, 8)]
    pass_on(3)
    for copy in third:
        copy.wait_recv()
    total = sum2[z]
    for d in range(7):
        total += buf3[d]
    base = (mine + x * 512 + y * 128, mine + 2048 + y * 512 + x * 128)
    back = {}
    for which in range(2):
        block = out_ref.at[rows_at(base[which] + z * 16, 16)]
        out_ref[rows_at(base[which] + z * 16, 16), :] = total[which].astype(BF16)
        for d in range(1, 8):
            back[which, d] = send(block, block, zs[d - 1])
    pass_on(0)
    wide = {}
    for which in range(2):
        for d in range(1, 8):
            back[which, d].wait_recv()
        block = out_ref.at[rows_at(base[which], 128)]
        for d in range(1, 4):
            wide[which, d] = send(block, block, (ys, xs)[which][d - 1])
    for copy in flat:
        copy.wait_recv()
    cold_start(want_ref, got, halves, joined)
    last, across = {}, []
    for which in range(2):
        for d in range(1, 4):
            wide[which, d].wait_recv()
        block = out_ref.at[rows_at(mine + which * 2048 + own[which] * 512, 512)]
        for d in range(1, 4):
            last[which, d] = send(block, block, (xs, ys)[which][d - 1])
        across.append(send(block, block, partner))
    for n in range(4):
        cold_step(n, part_ref, halves, joined)
        for low_row in (n * 512, n * 512 + 2048):
            block = pl.ds(low_row, 512)
            across.append(send(part_ref.at[block], other_ref.at[block], partner))
        if n == 2:
            for d in range(1, 4):
                for which in range(2):
                    last[which, d].wait_recv()
                    block = out_ref.at[rows_at(mine + which * 2048 + lax.rem(own[which] + 4 - d, 4) * 512, 512)]
                    across.append(send(block, block, partner))
    for copy in across:
        copy.wait_recv()
    for copy in started:
        copy.wait_send()


def cold_start(want_ref, got, halves, joined):
    even, odd = want_ref[pl.ds(0, 64, stride=2), :], want_ref[pl.ds(1, 64, stride=2), :]
    both = jnp.where(iota((64, 128), 1) < 64, even, pltpu.roll(odd, 64, 1))
    joined[...] = jnp.where(both < 0, -1, both & 2047)
    columns = (want_ref[...] >> 11).astype(F32).T
    for r in range(128):
        high = columns[0:64, r : r + 1]
        value = got[r // 8, r % 8].astype(F32)
        halves[r * 64 : r * 64 + 64, 0:128] = jnp.where(high == 0.0, value, 0.0).astype(BF16)
        halves[r * 64 : r * 64 + 64, 128:256] = jnp.where(high == 0.0, 0.0, value).astype(BF16)


def cold_step(part, out_ref, halves, joined):
    @pl.loop(part * 2, part * 2 + 2)
    def _(m):
        start = pl.multiple_of(m * 256, 256)
        wanted = iota((256, 128), 0) + m * 256
        total = jnp.zeros((256, 256), F32)
        for n in range(4):
            hits = [
                jnp.where(jnp.broadcast_to(joined[t : t + 1, :], (256, 128)) == wanted, 1.0, 0.0).astype(BF16)
                for t in range(n * 16, n * 16 + 16)
            ]
            total = total + jnp.dot(
                jnp.concatenate(hits, axis=1), halves[n * 2048 : n * 2048 + 2048, :], preferred_element_type=F32
            )
        out_ref[pl.ds(start, 256), :] = total[:, 0:128].astype(BF16)
        out_ref[pl.ds(start + 2048, 256), :] = total[:, 128:256].astype(BF16)


def back_part(sent, want, hot_row, hot_value, bottom, low, grad):
    vmem = pl.BlockSpec(memory_space=pltpu.VMEM)
    return pl.pallas_call(
        back_kernel,
        out_shape=(
            jax.ShapeDtypeStruct((8192, 128), BF16),
            jax.ShapeDtypeStruct((4096, 128), BF16),
            jax.ShapeDtypeStruct((4096, 128), BF16),
        ),
        in_specs=[vmem] * 7,
        out_specs=(vmem,) * 3,
        scratch_shapes=[
            pltpu.VMEM((8192, 128), BF16),
            pltpu.VMEM((3328, 256), BF16),
            pltpu.VMEM((480, 1024), F32),
            pltpu.VMEM((4, 8, 208, 128), BF16),
            pltpu.VMEM((16, 8, 64, 128), BF16),
            pltpu.VMEM((8192, 256), BF16),
            pltpu.VMEM((64, 128), jnp.int32),
            pltpu.VMEM((4096, 128), BF16),
            pltpu.VMEM((4096, 128), BF16),
            pltpu.VMEM((2, 3, 512, 128), BF16),
            pltpu.VMEM((2, 512, 128), BF16),
            pltpu.VMEM((2, 3, 128, 128), BF16),
            pltpu.VMEM((8, 2, 16, 128), F32),
            pltpu.VMEM((7, 2, 16, 128), F32),
            pltpu.SemaphoreType.DMA((127,)),
            pltpu.SemaphoreType.DMA((127,)),
        ],
        compiler_params=pltpu.CompilerParams(collective_id=0, has_side_effects=True, vmem_limit_bytes=VMEM_LIMIT),
        name="back_part",
    )(sent, want, hot_row, hot_value, bottom, low, grad)


def format_kernel(in_ref, part_ref, other_ref, hot_ref, cold_ref, top_ref):
    hot_ref[...] = in_ref[0:4096, :].astype(F32)
    cold_ref[...] = part_ref[...].astype(F32) + other_ref[...].astype(F32)
    for n in range(8):
        top_ref[:, n * 128 : n * 128 + 128] = in_ref[4096 + n * 480 : 4576 + n * 480, :].astype(F32)[0:479, :]


def format_sums(values, part, other):
    return pl.pallas_call(
        format_kernel,
        out_shape=(
            jax.ShapeDtypeStruct((4096, 128), F32),
            jax.ShapeDtypeStruct((4096, 128), F32),
            jax.ShapeDtypeStruct((479, 1024), F32),
        ),
        compiler_params=params(),
        name="format_sums",
    )(values, part, other)


def body(
    dense_feats,
    bottom_weight,
    top_weight,
    out_weight,
    hot_table,
    cold_table,
    hot_index,
    cold_owner,
    cold_row,
    clicks,
):
    query, slot, places = build_requests(cold_owner.T, cold_row.T)
    hot_fields = hot_index.T
    wanted, got, near, bottom, weight = front_part(
        query, cold_table, hot_fields, hot_table, dense_feats, bottom_weight, top_weight
    )
    wanted = wanted.reshape(128, 128)
    outgoing, hot_terms, low, grad = main_part(
        slot, places, got.reshape(8192, 128), near, bottom, top_weight, weight, out_weight.reshape(1, 1024), clicks.reshape(1, 256)
    )
    sums, part, other = back_part(
        outgoing.reshape(4, 8, 208, 128), wanted, hot_fields, hot_terms, bottom, low, grad
    )
    return format_sums(sums, part, other)


def solution(mesh):
    return jax.shard_map(
        body,
        mesh=mesh,
        in_specs=(
            P(("dp", "rep"), None),
            P(),
            P(),
            P(),
            P(),
            P("dp", None),
            P(("dp", "rep"), None),
            P(("dp", "rep"), None),
            P(("dp", "rep"), None),
            P(("dp", "rep")),
        ),
        out_specs=(P(), P("dp", None), P()),
        check_vma=False,
    )
```

```python
import jax
import jax.numpy as jnp
from jax import lax
from jax.experimental import pallas as pl
from jax.experimental.pallas import tpu as pltpu
from jax.sharding import PartitionSpec as P

MESH = pl.DeviceIdType.MESH
NX, NY, NZ = 4, 4, 8
VMEM_LIMIT = 48 * 1024 * 1024
F32 = jnp.float32
BF16 = jnp.bfloat16
CAP = 52
EARLY = 48
UNROLL = 4


def place():
    me = lax.axis_index("dp")
    core = lax.axis_index("rep")
    z = lax.rem(me, NZ)
    x = lax.rem(lax.div(me, NZ), NX)
    y = lax.div(me, NZ * NX)
    return x, y, z, core


def peer(x, y, z, core):
    return (y * (NX * NZ) + x * NZ + z, core)


def rows_at(start, size):
    return pl.ds(pl.multiple_of(start, 16), size)


def params():
    return pltpu.CompilerParams(vmem_limit_bytes=VMEM_LIMIT)


def iota(shape, dimension):
    return lax.broadcasted_iota(jnp.int32, shape, dimension)


def build_kernel(owner_ref, row_ref, query_ref, slot_ref, place_ref, rank, rows, table):
    x, y, z, _ = place()
    fill = jnp.zeros((115, 256), F32)
    owner = jnp.concatenate([owner_ref[...].astype(F32), fill], axis=0).T.astype(jnp.int32)
    row = jnp.concatenate([row_ref[...].astype(F32), fill], axis=0).T
    dz = (lax.bitwise_and(owner, 7) - z + 8) & 7
    dx = (lax.bitwise_and(lax.shift_right_logical(owner, 3), 3) - x + 4) & 3
    dy = (lax.shift_right_logical(owner, 5) - y + 4) & 3
    relative = dz * 16 + dy * 4 + dx
    lane = iota((256, 128), 1)
    named = jnp.zeros((256, 128), F32)
    wanted = jnp.zeros((256, 128), F32)
    for f in range(13):
        here = relative[:, f : f + 1] == lane
        named = jnp.where(here, 1.0, named)
        wanted = jnp.where(here, row[:, f : f + 1], wanted)
    before = jnp.where(iota((256, 256), 1) < iota((256, 256), 0), 1.0, 0.0).astype(BF16)
    count = jnp.dot(before, named.astype(BF16), preferred_element_type=F32)
    back_x = (4 - dx) & 3
    block = ((((4 - dy) & 3) * 4 + back_x) * 8 + ((8 - dz) & 7)) * 64
    block, late = block.astype(F32), (4 * back_x).astype(F32)
    base = ((dy * 8 + dz) * 208).astype(F32)
    ahead = dx.astype(F32)
    slots = jnp.zeros((256, 128), F32)
    places = jnp.zeros((256, 128), F32)
    for f in range(13):
        here = relative[:, f : f + 1] == lane
        mine = jnp.sum(jnp.where(here, count, 0.0), axis=1, keepdims=True)
        past = mine - float(EARLY)
        over = ahead[:, f : f + 1]
        spot = jnp.where(past < 0.0, over * float(EARLY) + mine, 4.0 * EARLY + 4.0 * over + past)
        slots = jnp.where(lane == f, base[:, f : f + 1] + spot, slots)
        inside = jnp.where(mine < float(EARLY), mine, mine + late[:, f : f + 1])
        places = jnp.where(lane == f, block[:, f : f + 1] + inside, places)
    slot_ref[...] = slots.T[0:16, :].astype(jnp.int32)
    place_ref[...] = places.T[0:16, :].astype(jnp.int32)
    rank[...] = jnp.where(named > 0.0, count, -1.0)
    rows[...] = wanted
    table[...] = jnp.zeros((128, 128), F32)

    for p in range(CAP):
        chosen = jnp.sum(jnp.where(rank[...] == float(p), rows[...], 0.0), axis=0, keepdims=True)
        if p < EARLY:
            table[p : p + 1, :] = chosen
        else:
            for e in range(4):
                at = EARLY + e * 4 + p - EARLY
                table[at : at + 1, :] = jnp.where((iota((1, 128), 1) & 3) == e, chosen, -1.0)

    query_ref[...] = table[...].T.astype(jnp.int32).reshape(8, 16, 128)


def build_requests(cold_owner, cold_row):
    return pl.pallas_call(
        build_kernel,
        out_shape=(
            jax.ShapeDtypeStruct((8, 16, 128), jnp.int32),
            jax.ShapeDtypeStruct((16, 256), jnp.int32),
            jax.ShapeDtypeStruct((16, 256), jnp.int32),
        ),
        scratch_shapes=[pltpu.VMEM((256, 128), F32), pltpu.VMEM((256, 128), F32), pltpu.VMEM((128, 128), F32)],
        compiler_params=params(),
        name="build_requests",
    )(cold_owner, cold_row)


def widen(wide, ref, rows):
    @pl.loop(0, rows // 256)
    def _(step):
        here = pl.ds(pl.multiple_of(step * 256, 256), 256)
        wide[here, :] = ref[here, :].astype(F32)


def front_kernel(
    query_ref, table_far, index_far, hot_table_far, dense_far, weight_far, top_far,
    want_ref, got_ref, near_ref, bottom_ref, square_ref,
    table_ref, index_ref, hot_table_ref, dense_ref, weight_ref, top_ref, tall, middle, turned, wanted, wide, wide_hot, held, chosen, passing, send_sem, recv_sem, local_sem,
):
    x, y, z, core = place()
    plane = [(dx, dy) for dy in range(4) for dx in range(4)]
    zs = [peer(x, y, lax.rem(z + d, NZ), core) for d in range(1, NZ)]
    xys = [peer(lax.rem(x + dx, NX), lax.rem(y + dy, NY), z, core) for dx, dy in plane[1:]]
    barrier = pltpu.get_barrier_semaphore()
    for other in zs + xys:
        pl.semaphore_signal(barrier, inc=1, device_id=other, device_id_type=MESH)
    fetched = (
        (table_far, table_ref), (index_far, index_ref), (hot_table_far, hot_table_ref),
        (dense_far, dense_ref), (weight_far, weight_ref), (top_far, top_ref),
    )
    fetches = [pltpu.make_async_copy(src, dst, local_sem.at[1 + n]) for n, (src, dst) in enumerate(fetched)]
    for fetch in fetches:
        fetch.start()
    pl.semaphore_wait(barrier, len(zs) + len(xys))

    started = []

    def send(src, dst, device):
        index = len(started)
        copy = pltpu.make_async_remote_copy(
            src_ref=src, dst_ref=dst, send_sem=send_sem.at[index], recv_sem=recv_sem.at[index],
            device_id=device, device_id_type=MESH,
        )
        copy.start()
        started.append(copy)
        return copy

    copies = [send(query_ref.at[d], middle.at[d], zs[d - 1]) for d in range(1, 8)]
    middle[0] = query_ref[0]
    fetches[0].wait()
    widen(wide, table_ref, 4096)
    for copy in copies:
        copy.wait_recv()
    for d in range(8):
        for k in range(16):
            turned[k, d : d + 1, :] = middle[d, k : k + 1, :]
    copies = [send(turned.at[k], want_ref.at[k], xys[k - 1]) for k in range(1, 16)]
    want_ref[0] = turned[0]
    for copy in copies:
        copy.wait_recv()
    copy = pltpu.make_async_copy(want_ref, wanted, local_sem.at[0])
    copy.start()
    copy.wait()

    order = (2, 1, 3, 0)
    along = {}
    copies = []

    def collect(dy):
        @pl.loop(0, 8)
        def _(d):
            back = lax.rem(8 - d, 8)
            for tile in range(13):
                rows = []
                for e in range(16):
                    dx, p = (tile // 3, tile % 3 * 16 + e) if tile < 12 else (e // 4, EARLY + (4 - e // 4) % 4 * 4 + e % 4)
                    k = (4 - dy) % 4 * 4 + (4 - dx) % 4
                    rows.append(wide[pl.ds(wanted[k, back, p], 1), :])
                chosen[dy, d, tile * 16 : tile * 16 + 16, :] = jnp.concatenate(rows, axis=0).astype(BF16)

        for d in range(1, 8):
            along[dy, d] = send(chosen.at[dy, d], passing.at[dy, d], zs[d - 1])
        passing[dy, 0] = chosen[dy, 0]

    def pass_on(dy):
        for d in range(1, 8):
            along[dy, d].wait_recv()
        for dx in range(4):
            early = passing.at[dy, :, pl.ds(dx * EARLY, EARLY)]
            late = passing.at[dy, :, pl.ds(4 * EARLY, 16)]
            k = dy * 4 + dx
            if k:
                copies.append(send(early, got_ref.at[k, :, pl.ds(0, EARLY)], xys[k - 1]))
                copies.append(send(late, got_ref.at[k, :, pl.ds(EARLY, 16)], xys[k - 1]))
            else:
                got_ref[0, :, 0:EARLY, :] = passing[0, :, 0:EARLY, :]
                got_ref[0, :, EARLY:64, :] = passing[0, :, 4 * EARLY : 4 * EARLY + 16, :]

    for dy in order:
        collect(dy)
    for fetch in fetches[1:]:
        fetch.wait()
    widen(wide_hot, hot_table_ref, 4096)
    bottom = jnp.maximum(jnp.dot(dense_ref[...], weight_ref[...], preferred_element_type=F32), 0.0)
    bottom_ref[...] = bottom.astype(BF16)
    held[...] = bottom

    @pl.loop(0, 32)
    def _(g):
        near_ref[g, 0:16, :] = jnp.concatenate(
            [held[pl.ds(pl.multiple_of(g * 8, 8), 8), :]]
            + [wide_hot[pl.ds(index_ref[0, g * 8 + k], 1), :] for k in range(8)], axis=0
        ).astype(BF16)
        for f in range(1, 13, 2):
            rows = [wide_hot[pl.ds(index_ref[f + k // 8, g * 8 + k % 8], 1), :] for k in range(16)]
            near_ref[g, 8 + f * 8 : 24 + f * 8, :] = jnp.concatenate(rows, axis=0).astype(BF16)

    pass_on(order[0])
    pass_on(order[1])
    tall[464:512, :] = jnp.zeros((48, 1024), BF16)
    tall[0:479, :] = top_ref[...]

    @pl.loop(0, 7)
    def _(b):
        i = 4 * b + (iota((128, 512), 0) >> 5)
        j = iota((128, 512), 0) & 31
        high, low = jnp.maximum(i, j), jnp.minimum(i, j)
        source = 128 + ((high * (high - 1)) >> 1) + low
        source = jnp.where((high == low) | (high > 26), -1, source)
        pick = jnp.where(source == iota((128, 512), 1), 1.0, 0.0).astype(BF16)
        square_ref[pl.ds(pl.multiple_of(b * 128, 128), 128), :] = jnp.dot(
            pick, tall[...], preferred_element_type=F32
        ).astype(BF16)

    pass_on(order[2])
    pass_on(order[3])
    for copy in copies:
        copy.wait_recv()
    for copy in started:
        copy.wait_send()


def front_part(query, table, hot_index, hot_table, dense, weight, top):
    vmem = pl.BlockSpec(memory_space=pltpu.VMEM)
    return pl.pallas_call(
        front_kernel,
        out_shape=(
            jax.ShapeDtypeStruct((16, 8, 128), jnp.int32),
            jax.ShapeDtypeStruct((16, 8, 64, 128), BF16),
            jax.ShapeDtypeStruct((32, 112, 128), BF16),
            jax.ShapeDtypeStruct((256, 128), BF16),
            jax.ShapeDtypeStruct((896, 1024), BF16),
        ),
        in_specs=[vmem] + [pl.BlockSpec(memory_space=pl.ANY)] * 6,
        out_specs=(vmem,) * 5,
        scratch_shapes=[
            pltpu.VMEM((4096, 128), BF16),
            pltpu.SMEM((13, 256), jnp.int32),
            pltpu.VMEM((4096, 128), BF16),
            pltpu.VMEM((256, 256), BF16),
            pltpu.VMEM((256, 128), BF16),
            pltpu.VMEM((479, 1024), BF16),
            pltpu.VMEM((512, 1024), BF16),
            pltpu.VMEM((8, 16, 128), jnp.int32),
            pltpu.VMEM((16, 8, 128), jnp.int32),
            pltpu.SMEM((16, 8, 128), jnp.int32),
            pltpu.VMEM((4096, 128), F32),
            pltpu.VMEM((4096, 128), F32),
            pltpu.VMEM((256, 128), F32),
            pltpu.VMEM((4, 8, 208, 128), BF16),
            pltpu.VMEM((4, 8, 208, 128), BF16),
            pltpu.SemaphoreType.DMA((80,)),
            pltpu.SemaphoreType.DMA((80,)),
            pltpu.SemaphoreType.DMA((7,)),
        ],
        compiler_params=pltpu.CompilerParams(collective_id=2, has_side_effects=True, vmem_limit_bytes=60 * 1024 * 1024),
        name="front_part",
    )(query, table, hot_index, hot_table, dense, weight, top)


def main_kernel(
    slot_ref, place_ref, got_ref, near_ref, bottom_ref, weight0_ref, weight_ref, out_weight_ref, click_ref,
    sent_ref, hot_ref, low_ref, grad_ref,
    wide, stack, far, pairs, hidden, slope, terms,
):
    widen(wide, got_ref, 8192)
    for e in range(UNROLL):
        far[e, 104:144, :] = jnp.zeros((40, 128), F32)
    same = (iota((256, 256), 0) & 7) == (iota((256, 256), 1) & 7)
    fold = jnp.where((iota((256, 128), 0) >> 3) == (iota((256, 128), 1) & 31), 1.0, 0.0).astype(BF16)
    unfold = jnp.where((iota((128, 256), 1) >> 3) == (iota((128, 256), 0) & 31), 1.0, 0.0).astype(BF16)
    quarter = iota((8, 128), 1) >> 5
    zero8 = jnp.zeros((8, 128), F32)

    @pl.loop(0, 32 // UNROLL)
    def _(step):
        groups = [step * UNROLL + e for e in range(UNROLL)]
        for e, g in enumerate(groups):
            for f in range(13):
                for k in range(8):
                    far[e, f * 8 + k : f * 8 + k + 1, :] = wide[pl.ds(place_ref[f, g * 8 + k], 1), :]
        values = [jnp.concatenate([near_ref[g], far[e].astype(BF16)], axis=0) for e, g in enumerate(groups)]
        dots = [
            lax.dot_general(value, value, (((1,), (1,)), ((), ())), preferred_element_type=F32) for value in values
        ]
        dots = [jnp.where(same, dot, 0.0).astype(BF16) for dot in dots]
        folds = [jnp.dot(dot, fold, preferred_element_type=F32) for dot in dots]
        for e, g in enumerate(groups):
            stack[g] = values[e]
            for b in range(7):
                block = zero8
                for q in range(4):
                    i = 4 * b + q
                    block = jnp.where(quarter == q, folds[e][i * 8 : i * 8 + 8, :], block)
                pairs[pl.ds(pl.multiple_of(g * 8, 8), 8), b * 128 : b * 128 + 128] = block

    for b in range(7):
        i = 4 * b + (iota((256, 128), 1) >> 5)
        j = iota((256, 128), 1) & 31
        low_ref[:, b * 128 : b * 128 + 128] = jnp.where(i > j, pairs[:, b * 128 : b * 128 + 128], 0.0).astype(BF16)

    total = jnp.zeros((256, 128), F32)
    for n in range(4):
        here = slice(n * 256, n * 256 + 256)
        hidden[:, here] = jnp.dot(bottom_ref[...], weight0_ref[0:128, here], preferred_element_type=F32) + jnp.dot(
            low_ref[...], weight_ref[:, here], preferred_element_type=F32
        )
    for n in range(8):
        here = slice(n * 128, n * 128 + 128)
        v = hidden[:, here]
        c = 0.7978845608028654
        square = v * v
        t = jnp.tanh(c * v * (1.0 + 0.044715 * square))
        weight = out_weight_ref[:, here].astype(F32)
        act = (0.5 * v * (1.0 + t)).astype(BF16).astype(F32)
        total = total + act * weight
        slope[:, here] = weight * (0.5 * (1.0 + t) + 0.5 * c * v * (1.0 - t * t) * (1.0 + 0.134145 * square))
    logits = jnp.sum(total, axis=1, keepdims=True)
    clicks = jnp.broadcast_to(click_ref[...].astype(F32), (128, 256)).T[:, 0:1]
    errors = 1.0 / (1.0 + jnp.exp(-logits)) - clicks
    grad_ref[...] = (slope[...] * errors).astype(BF16)
    for b in range(7):
        here = slice(b * 128, b * 128 + 128)
        pairs[:, here] = lax.dot_general(
            grad_ref[...], weight_ref[here, :], (((1,), (1,)), ((), ())), preferred_element_type=F32
        )

    @pl.loop(0, 13)
    def _(step):
        wide[pl.ds(pl.multiple_of(step * 512, 512), 512), :] = jnp.zeros((512, 128), F32)

    @pl.loop(0, 32 // UNROLL)
    def _(step):
        groups = [step * UNROLL + e for e in range(UNROLL)]
        spreads = []
        for g in groups:
            rows = []
            for b in range(7):
                block = pairs[pl.ds(pl.multiple_of(g * 8, 8), 8), b * 128 : b * 128 + 128]
                for q in range(4):
                    rows.append(jnp.where(quarter == q, block, 0.0))
            rows += [zero8] * 4
            spreads.append(jnp.concatenate(rows, axis=0).astype(BF16))
        spreads = [jnp.dot(spread, unfold, preferred_element_type=F32) for spread in spreads]
        spreads = [jnp.where(same, spread, 0.0).astype(BF16) for spread in spreads]
        results = [jnp.dot(spread, stack[g], preferred_element_type=F32) for spread, g in zip(spreads, groups)]
        for e, g in enumerate(groups):
            for f in range(13):
                hot_ref[f, pl.ds(pl.multiple_of(g * 8, 8), 8), :] = results[e][8 + f * 8 : 16 + f * 8, :]
            terms[e] = results[e][112:216, :]
        for e, g in enumerate(groups):
            for f in range(13):
                for k in range(8):
                    row = f * 8 + k
                    wide[pl.ds(slot_ref[f, g * 8 + k], 1), :] = terms[e, row : row + 1, :]

    @pl.loop(0, 26)
    def _(step):
        here = pl.ds(pl.multiple_of(step * 256, 256), 256)
        sent_ref[here, :] = wide[here, :].astype(BF16)


def main_part(slot, places, got, near, bottom, weight0, weight, out_weight, clicks):
    vmem = pl.BlockSpec(memory_space=pltpu.VMEM)
    return pl.pallas_call(
        main_kernel,
        out_shape=(
            jax.ShapeDtypeStruct((6656, 128), BF16),
            jax.ShapeDtypeStruct((13, 256, 128), F32),
            jax.ShapeDtypeStruct((256, 896), BF16),
            jax.ShapeDtypeStruct((256, 1024), BF16),
        ),
        in_specs=[pl.BlockSpec(memory_space=pltpu.SMEM)] * 2 + [vmem] * 7,
        out_specs=(vmem,) * 4,
        scratch_shapes=[
            pltpu.VMEM((8192, 128), F32),
            pltpu.VMEM((32, 256, 128), BF16),
            pltpu.VMEM((UNROLL, 144, 128), F32),
            pltpu.VMEM((256, 896), F32),
            pltpu.VMEM((256, 1024), F32),
            pltpu.VMEM((256, 1024), F32),
            pltpu.VMEM((UNROLL, 104, 128), F32),
        ],
        compiler_params=params(),
        name="main_part",
    )(slot, places, got, near, bottom, weight0, weight, out_weight, clicks)


def hot_kernel(row_ref, value_ref, bottom_ref, low_ref, grad_ref, out_ref, halves, top):
    columns = jnp.concatenate([(row_ref[...] >> 11).astype(F32), jnp.zeros((115, 256), F32)], axis=0).T
    for f in range(13):
        high = columns[:, f : f + 1]
        value = value_ref[f]
        halves[f * 256 : f * 256 + 256, 0:128] = jnp.where(high == 0.0, value, 0.0).astype(BF16)
        halves[f * 256 : f * 256 + 256, 128:256] = jnp.where(high == 0.0, 0.0, value).astype(BF16)

    @pl.loop(0, 8)
    def _(m):
        start = pl.multiple_of(m * 256, 256)
        wanted = iota((256, 256), 0) + m * 256
        hits = [
            jnp.where((jnp.broadcast_to(row_ref[f : f + 1, :], (256, 256)) & 2047) == wanted, 1.0, 0.0).astype(BF16)
            for f in range(13)
        ]
        total = jnp.dot(jnp.concatenate(hits, axis=1), halves[...], preferred_element_type=F32)
        out_ref[pl.ds(start, 256), :] = total[:, 0:128].astype(BF16)
        out_ref[pl.ds(start + 2048, 256), :] = total[:, 128:256].astype(BF16)

    top[472:480, :] = jnp.zeros((8, 1024), F32)
    top[0:128, :] = lax.dot_general(
        bottom_ref[...], grad_ref[...], (((0,), (0,)), ((), ())), preferred_element_type=F32
    )
    for b in range(7):
        part = lax.dot_general(
            low_ref[:, b * 128 : b * 128 + 128], grad_ref[...], (((0,), (0,)), ((), ())), preferred_element_type=F32
        )
        for q in range(4):
            i = 4 * b + q
            if 0 < i < 27:
                at = 128 + i * (i - 1) // 2
                top[at : at + i, :] = part[q * 32 : q * 32 + i, :]
    for n in range(8):
        out_ref[4096 + n * 480 : 4576 + n * 480, :] = top[:, n * 128 : n * 128 + 128].astype(BF16)
    out_ref[7936:8192, :] = jnp.zeros((256, 128), BF16)


def back_kernel(
    sent_ref, want_ref, hot_row_ref, hot_value_ref, bottom_ref, low_ref, grad_ref,
    out_ref, part_ref, other_ref,
    in_ref, hot_halves, top, passing, got, halves, joined,
    core_buf, half, buf1, sum1, buf2, sum2, buf3, send_sem, recv_sem,
):
    x, y, z, core = place()
    plane = [(dx, dy) for dy in range(4) for dx in range(4)]
    partner = peer(x, y, z, 1 - core)
    zs = [peer(x, y, lax.rem(z + d, NZ), core) for d in range(1, NZ)]
    xys = [peer(lax.rem(x + dx, NX), lax.rem(y + dy, NY), z, core) for dx, dy in plane[1:]]
    xs = [xys[d - 1] for d in range(1, 4)]
    ys = [xys[4 * d - 1] for d in range(1, 4)]
    barrier = pltpu.get_barrier_semaphore()
    everyone = [partner] + zs + xys
    for other in everyone:
        pl.semaphore_signal(barrier, inc=1, device_id=other, device_id_type=MESH)
    pl.semaphore_wait(barrier, len(everyone))

    started = []

    def send(src, dst, device):
        index = len(started)
        copy = pltpu.make_async_remote_copy(
            src_ref=src, dst_ref=dst, send_sem=send_sem.at[index], recv_sem=recv_sem.at[index],
            device_id=device, device_id_type=MESH,
        )
        copy.start()
        started.append(copy)
        return copy

    along, flat = {}, []

    def set_out(dy):
        for d in range(1, 8):
            along[dy, d] = send(sent_ref.at[dy, d], passing.at[dy, d], zs[d - 1])
        passing[dy, 0] = sent_ref[dy, 0]

    def pass_on(dy):
        for d in range(1, 8):
            along[dy, d].wait_recv()
        for dx in range(4):
            early = passing.at[dy, :, pl.ds(dx * EARLY, EARLY)]
            late = passing.at[dy, :, pl.ds(4 * EARLY, 16)]
            k = dy * 4 + dx
            if k:
                flat.append(send(early, got.at[k, :, pl.ds(0, EARLY)], xys[k - 1]))
                flat.append(send(late, got.at[k, :, pl.ds(EARLY, 16)], xys[k - 1]))
            else:
                got[0, :, 0:EARLY, :] = passing[0, :, 0:EARLY, :]
                got[0, :, EARLY:64, :] = passing[0, :, 4 * EARLY : 4 * EARLY + 16, :]

    set_out(2)
    set_out(1)
    hot_kernel(hot_row_ref, hot_value_ref, bottom_ref, low_ref, grad_ref, in_ref, hot_halves, top)

    mine, other = core * 4096, (1 - core) * 4096
    own = (x, y)
    plan = [(which, d) for d in (1, 2, 3, 0) for which in (0, 1)]
    starts = [which * 2048 + lax.rem(own[which] + d, 4) * 512 for which, d in plan]
    over = [send(in_ref.at[rows_at(other + start, 512)], core_buf.at[rows_at(start, 512)], partner) for start in starts]
    pass_on(2)
    set_out(3)
    first = {}
    for (which, d), start, copy in zip(plan, starts, over):
        copy.wait_recv()
        if d:

            @pl.loop(0, 2)
            def _(step):
                here = rows_at(start + step * 256, 256)
                value = in_ref[rows_at(mine + start + step * 256, 256), :].astype(F32)
                half[here, :] = (value + core_buf[here, :].astype(F32)).astype(BF16)

            first[which, d] = send(
                half.at[rows_at(start, 512)], buf1.at[which, d - 1], (xs, ys)[which][d - 1]
            )
    pass_on(1)
    set_out(0)
    second = {}
    for which in range(2):
        for d in range(1, 4):
            first[which, d].wait_recv()
        for d in (1, 2, 3, 0):
            piece = lax.rem(own[1 - which] + d, 4) * 128
            here = rows_at(piece, 128)
            start = which * 2048 + own[which] * 512 + piece
            total = in_ref[rows_at(mine + start, 128), :].astype(F32) + core_buf[rows_at(start, 128), :].astype(F32)
            for e in range(3):
                total += buf1[which, e, here, :].astype(F32)
            if d:
                sum1[which, here, :] = total.astype(BF16)
                second[which, d] = send(sum1.at[which, here], buf2.at[which, d - 1], (ys, xs)[which][d - 1])
            else:
                sum2[:, which] = total.reshape(8, 16, 128)
    for which in range(2):
        for d in range(1, 4):
            second[which, d].wait_recv()
        sum2[:, which] = sum2[:, which] + (
            buf2[which, 0].astype(F32) + buf2[which, 1].astype(F32) + buf2[which, 2].astype(F32)
        ).reshape(8, 16, 128)
    third = [send(sum2.at[lax.rem(z + d, 8)], buf3.at[d - 1], zs[d - 1]) for d in range(1, 8)]
    pass_on(3)
    for copy in third:
        copy.wait_recv()
    total = sum2[z]
    for d in range(7):
        total += buf3[d]
    base = (mine + x * 512 + y * 128, mine + 2048 + y * 512 + x * 128)
    back = {}
    for which in range(2):
        block = out_ref.at[rows_at(base[which] + z * 16, 16)]
        out_ref[rows_at(base[which] + z * 16, 16), :] = total[which].astype(BF16)
        for d in range(1, 8):
            back[which, d] = send(block, block, zs[d - 1])
    pass_on(0)
    wide = {}
    for which in range(2):
        for d in range(1, 8):
            back[which, d].wait_recv()
        block = out_ref.at[rows_at(base[which], 128)]
        for d in range(1, 4):
            wide[which, d] = send(block, block, (ys, xs)[which][d - 1])
    for copy in flat:
        copy.wait_recv()
    cold_start(want_ref, got, halves, joined)
    last, across = {}, []
    for which in range(2):
        for d in range(1, 4):
            wide[which, d].wait_recv()
        block = out_ref.at[rows_at(mine + which * 2048 + own[which] * 512, 512)]
        for d in range(1, 4):
            last[which, d] = send(block, block, (xs, ys)[which][d - 1])
        across.append(send(block, block, partner))
    for n in range(4):
        cold_step(n, part_ref, halves, joined)
        for low_row in (n * 512, n * 512 + 2048):
            block = pl.ds(low_row, 512)
            across.append(send(part_ref.at[block], other_ref.at[block], partner))
        if n == 2:
            for d in range(1, 4):
                for which in range(2):
                    last[which, d].wait_recv()
                    block = out_ref.at[rows_at(mine + which * 2048 + lax.rem(own[which] + 4 - d, 4) * 512, 512)]
                    across.append(send(block, block, partner))
    for copy in across:
        copy.wait_recv()
    for copy in started:
        copy.wait_send()


def cold_start(want_ref, got, halves, joined):
    even, odd = want_ref[pl.ds(0, 64, stride=2), :], want_ref[pl.ds(1, 64, stride=2), :]
    both = jnp.where(iota((64, 128), 1) < 64, even, pltpu.roll(odd, 64, 1))
    joined[...] = jnp.where(both < 0, -1, both & 2047)
    columns = (want_ref[...] >> 11).astype(F32).T
    for r in range(128):
        high = columns[0:64, r : r + 1]
        value = got[r // 8, r % 8].astype(F32)
        halves[r * 64 : r * 64 + 64, 0:128] = jnp.where(high == 0.0, value, 0.0).astype(BF16)
        halves[r * 64 : r * 64 + 64, 128:256] = jnp.where(high == 0.0, 0.0, value).astype(BF16)


def cold_step(part, out_ref, halves, joined):
    @pl.loop(part * 2, part * 2 + 2)
    def _(m):
        start = pl.multiple_of(m * 256, 256)
        wanted = iota((256, 128), 0) + m * 256
        total = jnp.zeros((256, 256), F32)
        for n in range(4):
            hits = [
                jnp.where(jnp.broadcast_to(joined[t : t + 1, :], (256, 128)) == wanted, 1.0, 0.0).astype(BF16)
                for t in range(n * 16, n * 16 + 16)
            ]
            total = total + jnp.dot(
                jnp.concatenate(hits, axis=1), halves[n * 2048 : n * 2048 + 2048, :], preferred_element_type=F32
            )
        out_ref[pl.ds(start, 256), :] = total[:, 0:128].astype(BF16)
        out_ref[pl.ds(start + 2048, 256), :] = total[:, 128:256].astype(BF16)


def back_part(sent, want, hot_row, hot_value, bottom, low, grad):
    vmem = pl.BlockSpec(memory_space=pltpu.VMEM)
    return pl.pallas_call(
        back_kernel,
        out_shape=(
            jax.ShapeDtypeStruct((8192, 128), BF16),
            jax.ShapeDtypeStruct((4096, 128), BF16),
            jax.ShapeDtypeStruct((4096, 128), BF16),
        ),
        in_specs=[vmem] * 7,
        out_specs=(vmem,) * 3,
        scratch_shapes=[
            pltpu.VMEM((8192, 128), BF16),
            pltpu.VMEM((3328, 256), BF16),
            pltpu.VMEM((480, 1024), F32),
            pltpu.VMEM((4, 8, 208, 128), BF16),
            pltpu.VMEM((16, 8, 64, 128), BF16),
            pltpu.VMEM((8192, 256), BF16),
            pltpu.VMEM((64, 128), jnp.int32),
            pltpu.VMEM((4096, 128), BF16),
            pltpu.VMEM((4096, 128), BF16),
            pltpu.VMEM((2, 3, 512, 128), BF16),
            pltpu.VMEM((2, 512, 128), BF16),
            pltpu.VMEM((2, 3, 128, 128), BF16),
            pltpu.VMEM((8, 2, 16, 128), F32),
            pltpu.VMEM((7, 2, 16, 128), F32),
            pltpu.SemaphoreType.DMA((127,)),
            pltpu.SemaphoreType.DMA((127,)),
        ],
        compiler_params=pltpu.CompilerParams(collective_id=0, has_side_effects=True, vmem_limit_bytes=VMEM_LIMIT),
        name="back_part",
    )(sent, want, hot_row, hot_value, bottom, low, grad)


def format_kernel(in_ref, part_ref, other_ref, hot_ref, cold_ref, top_ref):
    hot_ref[...] = in_ref[0:4096, :].astype(F32)
    cold_ref[...] = part_ref[...].astype(F32) + other_ref[...].astype(F32)
    for n in range(8):
        top_ref[:, n * 128 : n * 128 + 128] = in_ref[4096 + n * 480 : 4576 + n * 480, :].astype(F32)[0:479, :]


def format_sums(values, part, other):
    return pl.pallas_call(
        format_kernel,
        out_shape=(
            jax.ShapeDtypeStruct((4096, 128), F32),
            jax.ShapeDtypeStruct((4096, 128), F32),
            jax.ShapeDtypeStruct((479, 1024), F32),
        ),
        compiler_params=params(),
        name="format_sums",
    )(values, part, other)


def body(
    dense_feats,
    bottom_weight,
    top_weight,
    out_weight,
    hot_table,
    cold_table,
    hot_index,
    cold_owner,
    cold_row,
    clicks,
):
    query, slot, places = build_requests(cold_owner.T, cold_row.T)
    hot_fields = hot_index.T
    wanted, got, near, bottom, weight = front_part(
        query, cold_table, hot_fields, hot_table, dense_feats, bottom_weight, top_weight
    )
    wanted = wanted.reshape(128, 128)
    outgoing, hot_terms, low, grad = main_part(
        slot, places, got.reshape(8192, 128), near, bottom, top_weight, weight, out_weight.reshape(1, 1024), clicks.reshape(1, 256)
    )
    sums, part, other = back_part(
        outgoing.reshape(4, 8, 208, 128), wanted, hot_fields, hot_terms, bottom, low, grad
    )
    return format_sums(sums, part, other)


def solution(mesh):
    return jax.shard_map(
        body,
        mesh=mesh,
        in_specs=(
            P(("dp", "rep"), None),
            P(),
            P(),
            P(),
            P(),
            P("dp", None),
            P(("dp", "rep"), None),
            P(("dp", "rep"), None),
            P(("dp", "rep"), None),
            P(("dp", "rep")),
        ),
        out_specs=(P(), P("dp", None), P()),
        check_vma=False,
    )
```

```python
import jax
import jax.numpy as jnp
from jax import lax
from jax.experimental import pallas as pl
from jax.experimental.pallas import tpu as pltpu
from jax.sharding import PartitionSpec as P

MESH = pl.DeviceIdType.MESH
NX, NY, NZ = 4, 4, 8
VMEM_LIMIT = 60 * 1024 * 1024
F32 = jnp.float32
BF16 = jnp.bfloat16
CAP = 52
EARLY = 48
UNROLL = 4


def place():
    me = lax.axis_index("dp")
    core = lax.axis_index("rep")
    z = lax.rem(me, NZ)
    x = lax.rem(lax.div(me, NZ), NX)
    y = lax.div(me, NZ * NX)
    return x, y, z, core


def peer(x, y, z, core):
    return (y * (NX * NZ) + x * NZ + z, core)


def rows_at(start, size):
    return pl.ds(pl.multiple_of(start, 16), size)


def params():
    return pltpu.CompilerParams(vmem_limit_bytes=VMEM_LIMIT)


def iota(shape, dimension):
    return lax.broadcasted_iota(jnp.int32, shape, dimension)


def build_tables(x, y, z, owner_ref, row_ref, query_ref, term_ref, place_ref, rank, rows, table):
    fill = jnp.zeros((115, 256), F32)
    owner = jnp.concatenate([owner_ref[...].astype(F32), fill], axis=0).T.astype(jnp.int32)
    row = jnp.concatenate([row_ref[...].astype(F32), fill], axis=0).T
    dz = (lax.bitwise_and(owner, 7) - z + 8) & 7
    dx = (lax.bitwise_and(lax.shift_right_logical(owner, 3), 3) - x + 4) & 3
    dy = (lax.shift_right_logical(owner, 5) - y + 4) & 3
    relative = dz * 16 + dy * 4 + dx
    lane = iota((256, 128), 1)
    named = jnp.zeros((256, 128), F32)
    wanted = jnp.zeros((256, 128), F32)
    number = jnp.zeros((256, 128), F32)
    sample = (iota((256, 128), 0) + 8).astype(F32)
    for f in range(13):
        here = relative[:, f : f + 1] == lane
        named = jnp.where(here, 1.0, named)
        wanted = jnp.where(here, row[:, f : f + 1], wanted)
        number = jnp.where(here, sample + float(f * 256), number)
    before = jnp.where(iota((256, 256), 1) < iota((256, 256), 0), 1.0, 0.0).astype(BF16)
    count = jnp.dot(before, named.astype(BF16), preferred_element_type=F32)
    back_x = (4 - dx) & 3
    block = ((((4 - dy) & 3) * 4 + back_x) * 8 + ((8 - dz) & 7)) * 64
    block, late = block.astype(F32), (4 * back_x).astype(F32)
    places = jnp.zeros((256, 128), F32)
    for f in range(13):
        here = relative[:, f : f + 1] == lane
        mine = jnp.minimum(jnp.sum(jnp.where(here, count, 0.0), axis=1, keepdims=True), float(CAP - 1))
        inside = jnp.where(mine < float(EARLY), mine, mine + late[:, f : f + 1])
        places = jnp.where(lane == f, block[:, f : f + 1] + inside, places)
    place_ref[...] = jnp.clip(places.T[0:16, :].astype(jnp.int32), 0, 8191)
    rank[...] = jnp.where(named > 0.0, count, -1.0)
    rows[...] = wanted
    table[...] = jnp.zeros((128, 128), F32)

    for p in range(CAP):
        chosen = jnp.sum(jnp.where(rank[...] == float(p), rows[...], 0.0), axis=0, keepdims=True)
        if p < EARLY:
            table[p : p + 1, :] = chosen
        else:
            for e in range(4):
                at = EARLY + e * 4 + p - EARLY
                table[at : at + 1, :] = jnp.where((iota((1, 128), 1) & 3) == e, chosen, -1.0)

    query_ref[...] = table[...].T.astype(jnp.int32).reshape(8, 16, 128)
    rows[...] = number
    for p in range(CAP):
        table[p : p + 1, :] = jnp.sum(jnp.where(rank[...] == float(p), rows[...], 0.0), axis=0, keepdims=True)
    term_ref[...] = jnp.clip(table[...].T.astype(jnp.int32), 0, 3335).reshape(8, 16, 128)


def widen(wide, ref, rows):
    @pl.loop(0, rows // 256)
    def _(step):
        here = pl.ds(pl.multiple_of(step * 256, 256), 256)
        wide[here, :] = ref[here, :].astype(F32)


def main_kernel(
    place_ref, got_ref, near_ref, bottom_ref, weight0_ref, weight_ref, out_weight_ref, click_ref,
    hot_ref, low_ref, grad_ref, terms,
    wide, stack, far, pairs, hidden, slope,
):
    for k in range(16):
        for d in range(8):
            at = (k * 8 + d) * 64
            wide[at : at + 64, :] = got_ref[k, d].astype(F32)
    for e in range(UNROLL):
        far[e, 104:144, :] = jnp.zeros((40, 128), F32)
    same = (iota((256, 256), 0) & 7) == (iota((256, 256), 1) & 7)
    fold = jnp.where((iota((256, 128), 0) >> 3) == (iota((256, 128), 1) & 31), 1.0, 0.0).astype(BF16)
    unfold = jnp.where((iota((128, 256), 1) >> 3) == (iota((128, 256), 0) & 31), 1.0, 0.0).astype(BF16)
    quarter = iota((8, 128), 1) >> 5
    zero8 = jnp.zeros((8, 128), F32)

    @pl.loop(0, 32 // UNROLL)
    def _(step):
        groups = [step * UNROLL + e for e in range(UNROLL)]
        for e, g in enumerate(groups):
            for f in range(13):
                for k in range(8):
                    far[e, f * 8 + k : f * 8 + k + 1, :] = wide[pl.ds(place_ref[f, g * 8 + k], 1), :]
        values = [jnp.concatenate([near_ref[g], far[e].astype(BF16)], axis=0) for e, g in enumerate(groups)]
        dots = [
            lax.dot_general(value, value, (((1,), (1,)), ((), ())), preferred_element_type=F32) for value in values
        ]
        dots = [jnp.where(same, dot, 0.0).astype(BF16) for dot in dots]
        folds = [jnp.dot(dot, fold, preferred_element_type=F32) for dot in dots]
        for e, g in enumerate(groups):
            stack[g] = values[e]
            for b in range(7):
                block = zero8
                for q in range(4):
                    i = 4 * b + q
                    block = jnp.where(quarter == q, folds[e][i * 8 : i * 8 + 8, :], block)
                pairs[pl.ds(pl.multiple_of(g * 8, 8), 8), b * 128 : b * 128 + 128] = block

    for b in range(7):
        i = 4 * b + (iota((256, 128), 1) >> 5)
        j = iota((256, 128), 1) & 31
        low_ref[:, b * 128 : b * 128 + 128] = jnp.where(i > j, pairs[:, b * 128 : b * 128 + 128], 0.0).astype(BF16)

    total = jnp.zeros((256, 128), F32)
    for n in range(4):
        here = slice(n * 256, n * 256 + 256)
        hidden[:, here] = jnp.dot(bottom_ref[...], weight0_ref[0:128, here], preferred_element_type=F32) + jnp.dot(
            low_ref[...], weight_ref[:, here], preferred_element_type=F32
        )
    for n in range(8):
        here = slice(n * 128, n * 128 + 128)
        v = hidden[:, here]
        c = 0.7978845608028654
        square = v * v
        t = jnp.tanh(c * v * (1.0 + 0.044715 * square))
        weight = out_weight_ref[:, here].astype(F32)
        act = (0.5 * v * (1.0 + t)).astype(BF16).astype(F32)
        total = total + act * weight
        slope[:, here] = weight * (0.5 * (1.0 + t) + 0.5 * c * v * (1.0 - t * t) * (1.0 + 0.134145 * square))
    logits = jnp.sum(total, axis=1, keepdims=True)
    clicks = jnp.broadcast_to(click_ref[...].astype(F32), (128, 256)).T[:, 0:1]
    errors = 1.0 / (1.0 + jnp.exp(-logits)) - clicks
    grad_ref[...] = (slope[...] * errors).astype(BF16)
    for b in range(7):
        here = slice(b * 128, b * 128 + 128)
        pairs[:, here] = lax.dot_general(
            grad_ref[...], weight_ref[here, :], (((1,), (1,)), ((), ())), preferred_element_type=F32
        )

    terms[0:8, :] = zero8

    @pl.loop(0, 32 // UNROLL)
    def _(step):
        groups = [step * UNROLL + e for e in range(UNROLL)]
        spreads = []
        for g in groups:
            rows = []
            for b in range(7):
                block = pairs[pl.ds(pl.multiple_of(g * 8, 8), 8), b * 128 : b * 128 + 128]
                for q in range(4):
                    rows.append(jnp.where(quarter == q, block, 0.0))
            rows += [zero8] * 4
            spreads.append(jnp.concatenate(rows, axis=0).astype(BF16))
        spreads = [jnp.dot(spread, unfold, preferred_element_type=F32) for spread in spreads]
        spreads = [jnp.where(same, spread, 0.0).astype(BF16) for spread in spreads]
        results = [jnp.dot(spread, stack[g], preferred_element_type=F32) for spread, g in zip(spreads, groups)]
        for e, g in enumerate(groups):
            for f in range(13):
                hot_ref[f, pl.ds(pl.multiple_of(g * 8, 8), 8), :] = results[e][8 + f * 8 : 16 + f * 8, :]
                terms[pl.ds(pl.multiple_of(8 + f * 256 + g * 8, 8), 8), :] = results[e][112 + f * 8 : 120 + f * 8, :]


def hot_kernel(row_ref, value_ref, bottom_ref, low_ref, grad_ref, out_ref, halves, top):
    columns = jnp.concatenate([(row_ref[...] >> 11).astype(F32), jnp.zeros((115, 256), F32)], axis=0).T
    for f in range(13):
        high = columns[:, f : f + 1]
        value = value_ref[f]
        halves[f * 256 : f * 256 + 256, 0:128] = jnp.where(high == 0.0, value, 0.0).astype(BF16)
        halves[f * 256 : f * 256 + 256, 128:256] = jnp.where(high == 0.0, 0.0, value).astype(BF16)

    @pl.loop(0, 8)
    def _(m):
        start = pl.multiple_of(m * 256, 256)
        wanted = iota((256, 256), 0) + m * 256
        hits = [
            jnp.where((jnp.broadcast_to(row_ref[f : f + 1, :], (256, 256)) & 2047) == wanted, 1.0, 0.0).astype(BF16)
            for f in range(13)
        ]
        total = jnp.dot(jnp.concatenate(hits, axis=1), halves[...], preferred_element_type=F32)
        out_ref[pl.ds(start, 256), :] = total[:, 0:128].astype(BF16)
        out_ref[pl.ds(start + 2048, 256), :] = total[:, 128:256].astype(BF16)

    top[472:480, :] = jnp.zeros((8, 1024), F32)
    top[0:128, :] = lax.dot_general(
        bottom_ref[...], grad_ref[...], (((0,), (0,)), ((), ())), preferred_element_type=F32
    )
    for b in range(7):
        part = lax.dot_general(
            low_ref[:, b * 128 : b * 128 + 128], grad_ref[...], (((0,), (0,)), ((), ())), preferred_element_type=F32
        )
        for q in range(4):
            i = 4 * b + q
            if 0 < i < 27:
                at = 128 + i * (i - 1) // 2
                top[at : at + i, :] = part[q * 32 : q * 32 + i, :]
    for n in range(8):
        out_ref[4096 + n * 480 : 4576 + n * 480, :] = top[:, n * 128 : n * 128 + 128].astype(BF16)
    out_ref[7936:8192, :] = jnp.zeros((256, 128), BF16)


def cold_start(want_ref, got, halves, joined):
    even, odd = want_ref[pl.ds(0, 64, stride=2), :], want_ref[pl.ds(1, 64, stride=2), :]
    both = jnp.where(iota((64, 128), 1) < 64, even, pltpu.roll(odd, 64, 1))
    joined[...] = jnp.where(both < 0, -1, both & 2047)
    columns = (want_ref[...] >> 11).astype(F32).T
    for r in range(128):
        high = columns[0:64, r : r + 1]
        value = got[r // 8, r % 8].astype(F32)
        halves[r * 64 : r * 64 + 64, 0:128] = jnp.where(high == 0.0, value, 0.0).astype(BF16)
        halves[r * 64 : r * 64 + 64, 128:256] = jnp.where(high == 0.0, 0.0, value).astype(BF16)


def cold_step(part, out_ref, halves, joined):
    @pl.loop(part * 2, part * 2 + 2)
    def _(m):
        start = pl.multiple_of(m * 256, 256)
        wanted = iota((256, 128), 0) + m * 256
        total = jnp.zeros((256, 256), F32)
        for n in range(4):
            hits = [
                jnp.where(jnp.broadcast_to(joined[t : t + 1, :], (256, 128)) == wanted, 1.0, 0.0).astype(BF16)
                for t in range(n * 16, n * 16 + 16)
            ]
            total = total + jnp.dot(
                jnp.concatenate(hits, axis=1), halves[n * 2048 : n * 2048 + 2048, :], preferred_element_type=F32
            )
        out_ref[pl.ds(start, 256), :] = total[:, 0:128].astype(BF16)
        out_ref[pl.ds(start + 2048, 256), :] = total[:, 128:256].astype(BF16)


def whole_kernel(
    owner_far, row_far, table_far, index_far, hot_table_far, dense_far, weight_far, top_far, out_weight_ref,
    click_ref,
    out_ref, part_ref, other_ref,
    owner_ref, row_ref, table_ref, hot_row_ref, hot_table_ref, dense_ref, weight_ref, top_ref, tall, query_ref,
    term_turn, place_turn, rank, rows, table, want_ref, want_flat, middle, turned, safe, wide, wide_hot, held, chosen,
    passing, got_ref, near_ref, bottom_ref, square_ref, hot_value_ref, low_ref, grad_ref, terms, rows_in, stack,
    far, pairs, hidden, slope, in_ref, hot_halves, top, leaving, onward, come, halves, joined, core_buf, half,
    buf1, sum1, buf2, sum2, buf3, index_ref, wanted, term_at, place_at,
    send_sem, recv_sem, local_sem,
):
    x, y, z, core = place()
    plane = [(dx, dy) for dy in range(4) for dx in range(4)]
    partner = peer(x, y, z, 1 - core)
    zs = [peer(x, y, lax.rem(z + d, NZ), core) for d in range(1, NZ)]
    xys = [peer(lax.rem(x + dx, NX), lax.rem(y + dy, NY), z, core) for dx, dy in plane[1:]]
    xs = [xys[d - 1] for d in range(1, 4)]
    ys = [xys[4 * d - 1] for d in range(1, 4)]
    barrier = pltpu.get_barrier_semaphore()
    everyone = [partner] + zs + xys
    for device in everyone:
        pl.semaphore_signal(barrier, inc=1, device_id=device, device_id_type=MESH)
    fetched = (
        (owner_far, owner_ref), (row_far, row_ref), (table_far, table_ref), (index_far, index_ref),
        (index_far, hot_row_ref), (hot_table_far, hot_table_ref), (dense_far, dense_ref),
        (weight_far, weight_ref), (top_far, top_ref),
    )
    fetches = [pltpu.make_async_copy(src, dst, local_sem.at[3 + n]) for n, (src, dst) in enumerate(fetched)]
    for fetch in fetches:
        fetch.start()
    fetches[0].wait()
    fetches[1].wait()
    build_tables(x, y, z, owner_ref, row_ref, query_ref, term_turn, place_turn, rank, rows, table)
    staged = [
        pltpu.make_async_copy(term_turn, term_at, local_sem.at[1]),
        pltpu.make_async_copy(place_turn, place_at, local_sem.at[2]),
    ]
    for copy in staged:
        copy.start()
    pl.semaphore_wait(barrier, len(everyone))

    started = []

    def send(src, dst, device):
        index = len(started)
        copy = pltpu.make_async_remote_copy(
            src_ref=src, dst_ref=dst, send_sem=send_sem.at[index], recv_sem=recv_sem.at[index],
            device_id=device, device_id_type=MESH,
        )
        copy.start()
        started.append(copy)
        return copy

    copies = [send(query_ref.at[d], middle.at[d], zs[d - 1]) for d in range(1, 8)]
    middle[0] = query_ref[0]
    fetches[2].wait()
    widen(wide, table_ref, 4096)
    for copy in copies:
        copy.wait_recv()
    for d in range(8):
        for k in range(16):
            turned[k, d : d + 1, :] = middle[d, k : k + 1, :]
    copies = [send(turned.at[k], want_ref.at[k], xys[k - 1]) for k in range(1, 16)]
    want_ref[0] = turned[0]
    for copy in copies:
        copy.wait_recv()
    for k in range(16):
        safe[k] = jnp.clip(want_ref[k], 0, 4095)
    copy = pltpu.make_async_copy(safe, wanted, local_sem.at[0])
    copy.start()
    copy.wait()

    order = (2, 1, 3, 0)
    along = {}
    copies = []

    def collect(dy):
        @pl.loop(0, 8)
        def _(d):
            back = lax.rem(8 - d, 8)
            for tile in range(13):
                rows = []
                for e in range(16):
                    dx, p = (tile // 3, tile % 3 * 16 + e) if tile < 12 else (e // 4, EARLY + (4 - e // 4) % 4 * 4 + e % 4)
                    k = (4 - dy) % 4 * 4 + (4 - dx) % 4
                    rows.append(wide[pl.ds(wanted[k, back, p], 1), :])
                chosen[dy, d, tile * 16 : tile * 16 + 16, :] = jnp.concatenate(rows, axis=0).astype(BF16)

        for d in range(1, 8):
            along[dy, d] = send(chosen.at[dy, d], passing.at[dy, d], zs[d - 1])
        passing[dy, 0] = chosen[dy, 0]

    def pass_on(dy):
        for d in range(1, 8):
            along[dy, d].wait_recv()
        for dx in range(4):
            early = passing.at[dy, :, pl.ds(dx * EARLY, EARLY)]
            late = passing.at[dy, :, pl.ds(4 * EARLY, 16)]
            k = dy * 4 + dx
            if k:
                copies.append(send(early, got_ref.at[k, :, pl.ds(0, EARLY)], xys[k - 1]))
                copies.append(send(late, got_ref.at[k, :, pl.ds(EARLY, 16)], xys[k - 1]))
            else:
                got_ref[0, :, 0:EARLY, :] = passing[0, :, 0:EARLY, :]
                got_ref[0, :, EARLY:64, :] = passing[0, :, 4 * EARLY : 4 * EARLY + 16, :]

    for dy in order:
        collect(dy)
    for fetch in fetches[3:]:
        fetch.wait()
    widen(wide_hot, hot_table_ref, 4096)
    bottom = jnp.maximum(jnp.dot(dense_ref[...], weight_ref[...], preferred_element_type=F32), 0.0)
    bottom_ref[...] = bottom.astype(BF16)
    held[...] = bottom

    @pl.loop(0, 32)
    def _(g):
        near_ref[g, 0:16, :] = jnp.concatenate(
            [held[pl.ds(pl.multiple_of(g * 8, 8), 8), :]]
            + [wide_hot[pl.ds(index_ref[0, g * 8 + k], 1), :] for k in range(8)], axis=0
        ).astype(BF16)
        for f in range(1, 13, 2):
            rows = [wide_hot[pl.ds(index_ref[f + k // 8, g * 8 + k % 8], 1), :] for k in range(16)]
            near_ref[g, 8 + f * 8 : 24 + f * 8, :] = jnp.concatenate(rows, axis=0).astype(BF16)

    pass_on(order[0])
    pass_on(order[1])
    tall[464:512, :] = jnp.zeros((48, 1024), BF16)
    tall[0:479, :] = top_ref[...]

    @pl.loop(0, 7)
    def _(b):
        i = 4 * b + (iota((128, 512), 0) >> 5)
        j = iota((128, 512), 0) & 31
        high, low = jnp.maximum(i, j), jnp.minimum(i, j)
        source = 128 + ((high * (high - 1)) >> 1) + low
        source = jnp.where((high == low) | (high > 26), -1, source)
        pick = jnp.where(source == iota((128, 512), 1), 1.0, 0.0).astype(BF16)
        square_ref[pl.ds(pl.multiple_of(b * 128, 128), 128), :] = jnp.dot(
            pick, tall[...], preferred_element_type=F32
        ).astype(BF16)

    pass_on(order[2])
    pass_on(order[3])
    for copy in copies:
        copy.wait_recv()
    for copy in staged:
        copy.wait()
    main_kernel(
        place_at, got_ref, near_ref, bottom_ref, top_ref, square_ref, out_weight_ref, click_ref,
        hot_value_ref, low_ref, grad_ref, terms, rows_in, stack, far, pairs, hidden, slope,
    )
    for k in range(16):
        want_flat[k * 8 : k * 8 + 8, :] = want_ref[k]

    along, flat = {}, []

    def set_out(dy):
        @pl.loop(0, 8)
        def _(d):
            for tile in range(13):
                picked = []
                for e in range(16):
                    dx, p = (tile // 3, tile % 3 * 16 + e) if tile < 12 else (e // 4, EARLY + e % 4)
                    picked.append(terms[pl.ds(term_at[d, dy * 4 + dx, p], 1), :])
                leaving[dy, d, tile * 16 : tile * 16 + 16, :] = jnp.concatenate(picked, axis=0).astype(BF16)

        for d in range(1, 8):
            along[dy, d] = send(leaving.at[dy, d], onward.at[dy, d], zs[d - 1])
        onward[dy, 0] = leaving[dy, 0]

    def hand_on(dy):
        for d in range(1, 8):
            along[dy, d].wait_recv()
        for dx in range(4):
            early = onward.at[dy, :, pl.ds(dx * EARLY, EARLY)]
            late = onward.at[dy, :, pl.ds(4 * EARLY, 16)]
            k = dy * 4 + dx
            if k:
                flat.append(send(early, come.at[k, :, pl.ds(0, EARLY)], xys[k - 1]))
                flat.append(send(late, come.at[k, :, pl.ds(EARLY, 16)], xys[k - 1]))
            else:
                come[0, :, 0:EARLY, :] = onward[0, :, 0:EARLY, :]
                come[0, :, EARLY:64, :] = onward[0, :, 4 * EARLY : 4 * EARLY + 16, :]

    set_out(2)
    set_out(1)
    hot_kernel(hot_row_ref, hot_value_ref, bottom_ref, low_ref, grad_ref, in_ref, hot_halves, top)

    mine, other = core * 4096, (1 - core) * 4096
    own = (x, y)
    plan = [(which, d) for d in (1, 2, 3, 0) for which in (0, 1)]
    starts = [which * 2048 + lax.rem(own[which] + d, 4) * 512 for which, d in plan]
    over = [send(in_ref.at[rows_at(other + start, 512)], core_buf.at[rows_at(start, 512)], partner) for start in starts]
    hand_on(2)
    set_out(3)
    first = {}
    for (which, d), start, copy in zip(plan, starts, over):
        copy.wait_recv()
        if d:

            @pl.loop(0, 2)
            def _(step):
                here = rows_at(start + step * 256, 256)
                value = in_ref[rows_at(mine + start + step * 256, 256), :].astype(F32)
                half[here, :] = (value + core_buf[here, :].astype(F32)).astype(BF16)

            first[which, d] = send(
                half.at[rows_at(start, 512)], buf1.at[which, d - 1], (xs, ys)[which][d - 1]
            )
    hand_on(1)
    set_out(0)
    second = {}
    for which in range(2):
        for d in range(1, 4):
            first[which, d].wait_recv()
        for d in (1, 2, 3, 0):
            piece = lax.rem(own[1 - which] + d, 4) * 128
            here = rows_at(piece, 128)
            start = which * 2048 + own[which] * 512 + piece
            total = in_ref[rows_at(mine + start, 128), :].astype(F32) + core_buf[rows_at(start, 128), :].astype(F32)
            for e in range(3):
                total += buf1[which, e, here, :].astype(F32)
            if d:
                sum1[which, here, :] = total.astype(BF16)
                second[which, d] = send(sum1.at[which, here], buf2.at[which, d - 1], (ys, xs)[which][d - 1])
            else:
                sum2[:, which] = total.reshape(8, 16, 128)
    for which in range(2):
        for d in range(1, 4):
            second[which, d].wait_recv()
        sum2[:, which] = sum2[:, which] + (
            buf2[which, 0].astype(F32) + buf2[which, 1].astype(F32) + buf2[which, 2].astype(F32)
        ).reshape(8, 16, 128)
    third = [send(sum2.at[lax.rem(z + d, 8)], buf3.at[d - 1], zs[d - 1]) for d in range(1, 8)]
    hand_on(3)
    for copy in third:
        copy.wait_recv()
    total = sum2[z]
    for d in range(7):
        total += buf3[d]
    base = (mine + x * 512 + y * 128, mine + 2048 + y * 512 + x * 128)
    back = {}
    for which in range(2):
        block = out_ref.at[rows_at(base[which] + z * 16, 16)]
        out_ref[rows_at(base[which] + z * 16, 16), :] = total[which].astype(BF16)
        for d in range(1, 8):
            back[which, d] = send(block, block, zs[d - 1])
    hand_on(0)
    spread = {}
    for which in range(2):
        for d in range(1, 8):
            back[which, d].wait_recv()
        block = out_ref.at[rows_at(base[which], 128)]
        for d in range(1, 4):
            spread[which, d] = send(block, block, (ys, xs)[which][d - 1])
    for copy in flat:
        copy.wait_recv()
    cold_start(want_flat, come, halves, joined)
    last, across = {}, []
    for which in range(2):
        for d in range(1, 4):
            spread[which, d].wait_recv()
        block = out_ref.at[rows_at(mine + which * 2048 + own[which] * 512, 512)]
        for d in range(1, 4):
            last[which, d] = send(block, block, (xs, ys)[which][d - 1])
        across.append(send(block, block, partner))
    for n in range(4):
        cold_step(n, part_ref, halves, joined)
        for low_row in (n * 512, n * 512 + 2048):
            block = pl.ds(low_row, 512)
            across.append(send(part_ref.at[block], other_ref.at[block], partner))
        if n == 2:
            for d in range(1, 4):
                for which in range(2):
                    last[which, d].wait_recv()
                    block = out_ref.at[rows_at(mine + which * 2048 + lax.rem(own[which] + 4 - d, 4) * 512, 512)]
                    across.append(send(block, block, partner))
    for copy in across:
        copy.wait_recv()
    for copy in started:
        copy.wait_send()


def whole(owner, row, table, index, hot_table, dense, weight, top, out_weight, clicks):
    vmem = pl.BlockSpec(memory_space=pltpu.VMEM)
    return pl.pallas_call(
        whole_kernel,
        out_shape=(
            jax.ShapeDtypeStruct((8192, 128), BF16),
            jax.ShapeDtypeStruct((4096, 128), BF16),
            jax.ShapeDtypeStruct((4096, 128), BF16),
        ),
        in_specs=[pl.BlockSpec(memory_space=pl.ANY)] * 8 + [vmem] * 2,
        out_specs=(vmem,) * 3,
        scratch_shapes=[
            pltpu.VMEM((13, 256), jnp.int32),
            pltpu.VMEM((13, 256), jnp.int32),
            pltpu.VMEM((4096, 128), BF16),
            pltpu.VMEM((13, 256), jnp.int32),
            pltpu.VMEM((4096, 128), BF16),
            pltpu.VMEM((256, 256), BF16),
            pltpu.VMEM((256, 128), BF16),
            pltpu.VMEM((479, 1024), BF16),
            pltpu.VMEM((512, 1024), BF16),
            pltpu.VMEM((8, 16, 128), jnp.int32),
            pltpu.VMEM((8, 16, 128), jnp.int32),
            pltpu.VMEM((16, 256), jnp.int32),
            pltpu.VMEM((256, 128), F32),
            pltpu.VMEM((256, 128), F32),
            pltpu.VMEM((128, 128), F32),
            pltpu.VMEM((16, 8, 128), jnp.int32),
            pltpu.VMEM((128, 128), jnp.int32),
            pltpu.VMEM((8, 16, 128), jnp.int32),
            pltpu.VMEM((16, 8, 128), jnp.int32),
            pltpu.VMEM((16, 8, 128), jnp.int32),
            pltpu.VMEM((4096, 128), F32),
            pltpu.VMEM((4096, 128), F32),
            pltpu.VMEM((256, 128), F32),
            pltpu.VMEM((4, 8, 208, 128), BF16),
            pltpu.VMEM((4, 8, 208, 128), BF16),
            pltpu.VMEM((16, 8, 64, 128), BF16),
            pltpu.VMEM((32, 112, 128), BF16),
            pltpu.VMEM((256, 128), BF16),
            pltpu.VMEM((896, 1024), BF16),
            pltpu.VMEM((13, 256, 128), F32),
            pltpu.VMEM((256, 896), BF16),
            pltpu.VMEM((256, 1024), BF16),
            pltpu.VMEM((3336, 128), F32),
            pltpu.VMEM((8192, 128), F32),
            pltpu.VMEM((32, 256, 128), BF16),
            pltpu.VMEM((4, 144, 128), F32),
            pltpu.VMEM((256, 896), F32),
            pltpu.VMEM((256, 1024), F32),
            pltpu.VMEM((256, 1024), F32),
            pltpu.VMEM((8192, 128), BF16),
            pltpu.VMEM((3328, 256), BF16),
            pltpu.VMEM((480, 1024), F32),
            pltpu.VMEM((4, 8, 208, 128), BF16),
            pltpu.VMEM((4, 8, 208, 128), BF16),
            pltpu.VMEM((16, 8, 64, 128), BF16),
            pltpu.VMEM((8192, 256), BF16),
            pltpu.VMEM((64, 128), jnp.int32),
            pltpu.VMEM((4096, 128), BF16),
            pltpu.VMEM((4096, 128), BF16),
            pltpu.VMEM((2, 3, 512, 128), BF16),
            pltpu.VMEM((2, 512, 128), BF16),
            pltpu.VMEM((2, 3, 128, 128), BF16),
            pltpu.VMEM((8, 2, 16, 128), F32),
            pltpu.VMEM((7, 2, 16, 128), F32),
            pltpu.SMEM((13, 256), jnp.int32),
            pltpu.SMEM((16, 8, 128), jnp.int32),
            pltpu.SMEM((8, 16, 128), jnp.int32),
            pltpu.SMEM((16, 256), jnp.int32),
            pltpu.SemaphoreType.DMA((207,)),
            pltpu.SemaphoreType.DMA((207,)),
            pltpu.SemaphoreType.DMA((12,)),
        ],
        compiler_params=pltpu.CompilerParams(collective_id=0, has_side_effects=True, vmem_limit_bytes=VMEM_LIMIT),
        name="whole",
    )(owner, row, table, index, hot_table, dense, weight, top, out_weight, clicks)


def format_kernel(in_ref, part_ref, other_ref, hot_ref, cold_ref, top_ref):
    hot_ref[...] = in_ref[0:4096, :].astype(F32)
    cold_ref[...] = part_ref[...].astype(F32) + other_ref[...].astype(F32)
    for n in range(8):
        top_ref[:, n * 128 : n * 128 + 128] = in_ref[4096 + n * 480 : 4576 + n * 480, :].astype(F32)[0:479, :]


def format_sums(values, part, other):
    return pl.pallas_call(
        format_kernel,
        out_shape=(
            jax.ShapeDtypeStruct((4096, 128), F32),
            jax.ShapeDtypeStruct((4096, 128), F32),
            jax.ShapeDtypeStruct((479, 1024), F32),
        ),
        compiler_params=params(),
        name="format_sums",
    )(values, part, other)


def body(
    dense_feats,
    bottom_weight,
    top_weight,
    out_weight,
    hot_table,
    cold_table,
    hot_index,
    cold_owner,
    cold_row,
    clicks,
):
    sums, part, other = whole(
        cold_owner.T, cold_row.T, cold_table, hot_index.T, hot_table, dense_feats, bottom_weight, top_weight,
        out_weight.reshape(1, 1024), clicks.reshape(1, 256),
    )
    return format_sums(sums, part, other)


def solution(mesh):
    return jax.shard_map(
        body,
        mesh=mesh,
        in_specs=(
            P(("dp", "rep"), None),
            P(),
            P(),
            P(),
            P(),
            P("dp", None),
            P(("dp", "rep"), None),
            P(("dp", "rep"), None),
            P(("dp", "rep"), None),
            P(("dp", "rep")),
        ),
        out_specs=(P(), P("dp", None), P()),
        check_vma=False,
    )
```

```python
import jax
import jax.numpy as jnp
from jax import lax
from jax.experimental import pallas as pl
from jax.experimental.pallas import tpu as pltpu
from jax.sharding import PartitionSpec as P

MESH = pl.DeviceIdType.MESH
NX, NY, NZ = 4, 4, 8
VMEM_LIMIT = 60 * 1024 * 1024
F32 = jnp.float32
BF16 = jnp.bfloat16
CAP = 52
EARLY = 48
UNROLL = 4


def place():
    me = lax.axis_index("dp")
    core = lax.axis_index("rep")
    z = lax.rem(me, NZ)
    x = lax.rem(lax.div(me, NZ), NX)
    y = lax.div(me, NZ * NX)
    return x, y, z, core


def peer(x, y, z, core):
    return (y * (NX * NZ) + x * NZ + z, core)


def rows_at(start, size):
    return pl.ds(pl.multiple_of(start, 16), size)


def params():
    return pltpu.CompilerParams(vmem_limit_bytes=VMEM_LIMIT)


def iota(shape, dimension):
    return lax.broadcasted_iota(jnp.int32, shape, dimension)


def build_tables(x, y, z, owner_ref, row_ref, query_ref, term_ref, place_ref, rank, rows, table):
    fill = jnp.zeros((115, 256), F32)
    owner = jnp.concatenate([owner_ref[...].astype(F32), fill], axis=0).T.astype(jnp.int32)
    row = jnp.concatenate([row_ref[...].astype(F32), fill], axis=0).T
    dz = (lax.bitwise_and(owner, 7) - z + 8) & 7
    dx = (lax.bitwise_and(lax.shift_right_logical(owner, 3), 3) - x + 4) & 3
    dy = (lax.shift_right_logical(owner, 5) - y + 4) & 3
    relative = dz * 16 + dy * 4 + dx
    lane = iota((256, 128), 1)
    named = jnp.zeros((256, 128), F32)
    wanted = jnp.zeros((256, 128), F32)
    number = jnp.zeros((256, 128), F32)
    sample = (iota((256, 128), 0) + 8).astype(F32)
    for f in range(13):
        here = relative[:, f : f + 1] == lane
        named = jnp.where(here, 1.0, named)
        wanted = jnp.where(here, row[:, f : f + 1], wanted)
        number = jnp.where(here, sample + float(f * 256), number)
    before = jnp.where(iota((256, 256), 1) < iota((256, 256), 0), 1.0, 0.0).astype(BF16)
    count = jnp.dot(before, named.astype(BF16), preferred_element_type=F32)
    back_x = (4 - dx) & 3
    block = ((((4 - dy) & 3) * 4 + back_x) * 8 + ((8 - dz) & 7)) * 64
    block, late = block.astype(F32), (4 * back_x).astype(F32)
    places = jnp.zeros((256, 128), F32)
    for f in range(13):
        here = relative[:, f : f + 1] == lane
        mine = jnp.minimum(jnp.sum(jnp.where(here, count, 0.0), axis=1, keepdims=True), float(CAP - 1))
        inside = jnp.where(mine < float(EARLY), mine, mine + late[:, f : f + 1])
        places = jnp.where(lane == f, block[:, f : f + 1] + inside, places)
    place_ref[...] = jnp.clip(places.T[0:16, :].astype(jnp.int32), 0, 8191)
    rank[...] = jnp.where(named > 0.0, count, -1.0)
    rows[...] = wanted
    table[...] = jnp.zeros((128, 128), F32)

    for p in range(CAP):
        chosen = jnp.sum(jnp.where(rank[...] == float(p), rows[...], 0.0), axis=0, keepdims=True)
        if p < EARLY:
            table[p : p + 1, :] = chosen
        else:
            for e in range(4):
                at = EARLY + e * 4 + p - EARLY
                table[at : at + 1, :] = jnp.where((iota((1, 128), 1) & 3) == e, chosen, -1.0)

    query_ref[...] = table[...].T.astype(jnp.int32).reshape(8, 16, 128)
    rows[...] = number
    for p in range(CAP):
        table[p : p + 1, :] = jnp.sum(jnp.where(rank[...] == float(p), rows[...], 0.0), axis=0, keepdims=True)
    term_ref[...] = jnp.clip(table[...].T.astype(jnp.int32), 0, 3335).reshape(8, 16, 128)


def widen(wide, ref, rows):
    @pl.loop(0, rows // 256)
    def _(step):
        here = pl.ds(pl.multiple_of(step * 256, 256), 256)
        wide[here, :] = ref[here, :].astype(F32)


def main_kernel(
    place_ref, got_ref, near_ref, bottom_ref, weight0_ref, weight_ref, out_weight_ref, click_ref,
    hot_ref, low_ref, grad_ref, terms,
    wide, stack, far, pairs, hidden, slope,
):
    for k in range(16):
        for d in range(8):
            at = (k * 8 + d) * 64
            wide[at : at + 64, :] = got_ref[k, d].astype(F32)
    for e in range(UNROLL):
        far[e, 104:144, :] = jnp.zeros((40, 128), F32)
    same = (iota((256, 256), 0) & 7) == (iota((256, 256), 1) & 7)
    fold = jnp.where((iota((256, 128), 0) >> 3) == (iota((256, 128), 1) & 31), 1.0, 0.0).astype(BF16)
    unfold = jnp.where((iota((128, 256), 1) >> 3) == (iota((128, 256), 0) & 31), 1.0, 0.0).astype(BF16)
    quarter = iota((8, 128), 1) >> 5
    zero8 = jnp.zeros((8, 128), F32)

    @pl.loop(0, 32 // UNROLL)
    def _(step):
        groups = [step * UNROLL + e for e in range(UNROLL)]
        for e, g in enumerate(groups):
            for f in range(13):
                for k in range(8):
                    far[e, f * 8 + k : f * 8 + k + 1, :] = wide[pl.ds(place_ref[f, g * 8 + k], 1), :]
        values = [jnp.concatenate([near_ref[g], far[e].astype(BF16)], axis=0) for e, g in enumerate(groups)]
        dots = [
            lax.dot_general(value, value, (((1,), (1,)), ((), ())), preferred_element_type=F32) for value in values
        ]
        dots = [jnp.where(same, dot, 0.0).astype(BF16) for dot in dots]
        folds = [jnp.dot(dot, fold, preferred_element_type=F32) for dot in dots]
        for e, g in enumerate(groups):
            stack[g] = values[e]
            for b in range(7):
                block = zero8
                for q in range(4):
                    i = 4 * b + q
                    block = jnp.where(quarter == q, folds[e][i * 8 : i * 8 + 8, :], block)
                pairs[pl.ds(pl.multiple_of(g * 8, 8), 8), b * 128 : b * 128 + 128] = block

    for b in range(7):
        i = 4 * b + (iota((256, 128), 1) >> 5)
        j = iota((256, 128), 1) & 31
        low_ref[:, b * 128 : b * 128 + 128] = jnp.where(i > j, pairs[:, b * 128 : b * 128 + 128], 0.0).astype(BF16)

    total = jnp.zeros((256, 128), F32)
    for n in range(4):
        here = slice(n * 256, n * 256 + 256)
        hidden[:, here] = jnp.dot(bottom_ref[...], weight0_ref[0:128, here], preferred_element_type=F32) + jnp.dot(
            low_ref[...], weight_ref[:, here], preferred_element_type=F32
        )
    for n in range(8):
        here = slice(n * 128, n * 128 + 128)
        v = hidden[:, here]
        c = 0.7978845608028654
        square = v * v
        t = jnp.tanh(c * v * (1.0 + 0.044715 * square))
        weight = out_weight_ref[:, here].astype(F32)
        act = (0.5 * v * (1.0 + t)).astype(BF16).astype(F32)
        total = total + act * weight
        slope[:, here] = weight * (0.5 * (1.0 + t) + 0.5 * c * v * (1.0 - t * t) * (1.0 + 0.134145 * square))
    logits = jnp.sum(total, axis=1, keepdims=True)
    clicks = jnp.broadcast_to(click_ref[...].astype(F32), (128, 256)).T[:, 0:1]
    errors = 1.0 / (1.0 + jnp.exp(-logits)) - clicks
    grad_ref[...] = (slope[...] * errors).astype(BF16)
    for b in range(7):
        here = slice(b * 128, b * 128 + 128)
        pairs[:, here] = lax.dot_general(
            grad_ref[...], weight_ref[here, :], (((1,), (1,)), ((), ())), preferred_element_type=F32
        )

    terms[0:8, :] = zero8

    @pl.loop(0, 32 // UNROLL)
    def _(step):
        groups = [step * UNROLL + e for e in range(UNROLL)]
        spreads = []
        for g in groups:
            rows = []
            for b in range(7):
                block = pairs[pl.ds(pl.multiple_of(g * 8, 8), 8), b * 128 : b * 128 + 128]
                for q in range(4):
                    rows.append(jnp.where(quarter == q, block, 0.0))
            rows += [zero8] * 4
            spreads.append(jnp.concatenate(rows, axis=0).astype(BF16))
        spreads = [jnp.dot(spread, unfold, preferred_element_type=F32) for spread in spreads]
        spreads = [jnp.where(same, spread, 0.0).astype(BF16) for spread in spreads]
        results = [jnp.dot(spread, stack[g], preferred_element_type=F32) for spread, g in zip(spreads, groups)]
        for e, g in enumerate(groups):
            for f in range(13):
                hot_ref[f, pl.ds(pl.multiple_of(g * 8, 8), 8), :] = results[e][8 + f * 8 : 16 + f * 8, :]
                terms[pl.ds(pl.multiple_of(8 + f * 256 + g * 8, 8), 8), :] = results[e][112 + f * 8 : 120 + f * 8, :]


def hot_kernel(row_ref, value_ref, bottom_ref, low_ref, grad_ref, out_ref, halves, top):
    columns = jnp.concatenate([(row_ref[...] >> 11).astype(F32), jnp.zeros((115, 256), F32)], axis=0).T
    for f in range(13):
        high = columns[:, f : f + 1]
        value = value_ref[f]
        halves[f * 256 : f * 256 + 256, 0:128] = jnp.where(high == 0.0, value, 0.0).astype(BF16)
        halves[f * 256 : f * 256 + 256, 128:256] = jnp.where(high == 0.0, 0.0, value).astype(BF16)

    @pl.loop(0, 8)
    def _(m):
        start = pl.multiple_of(m * 256, 256)
        wanted = iota((256, 256), 0) + m * 256
        hits = [
            jnp.where((jnp.broadcast_to(row_ref[f : f + 1, :], (256, 256)) & 2047) == wanted, 1.0, 0.0).astype(BF16)
            for f in range(13)
        ]
        total = jnp.dot(jnp.concatenate(hits, axis=1), halves[...], preferred_element_type=F32)
        out_ref[pl.ds(start, 256), :] = total[:, 0:128].astype(BF16)
        out_ref[pl.ds(start + 2048, 256), :] = total[:, 128:256].astype(BF16)

    top[472:480, :] = jnp.zeros((8, 1024), F32)
    top[0:128, :] = lax.dot_general(
        bottom_ref[...], grad_ref[...], (((0,), (0,)), ((), ())), preferred_element_type=F32
    )
    for b in range(7):
        part = lax.dot_general(
            low_ref[:, b * 128 : b * 128 + 128], grad_ref[...], (((0,), (0,)), ((), ())), preferred_element_type=F32
        )
        for q in range(4):
            i = 4 * b + q
            if 0 < i < 27:
                at = 128 + i * (i - 1) // 2
                top[at : at + i, :] = part[q * 32 : q * 32 + i, :]
    for n in range(8):
        out_ref[4096 + n * 480 : 4576 + n * 480, :] = top[:, n * 128 : n * 128 + 128].astype(BF16)
    out_ref[7936:8192, :] = jnp.zeros((256, 128), BF16)


def cold_start(want_ref, got, halves, joined):
    even, odd = want_ref[pl.ds(0, 64, stride=2), :], want_ref[pl.ds(1, 64, stride=2), :]
    both = jnp.where(iota((64, 128), 1) < 64, even, pltpu.roll(odd, 64, 1))
    joined[...] = jnp.where(both < 0, -1, both & 2047)
    columns = (want_ref[...] >> 11).astype(F32).T
    for r in range(128):
        high = columns[0:64, r : r + 1]
        value = got[r // 8, r % 8].astype(F32)
        halves[r * 64 : r * 64 + 64, 0:128] = jnp.where(high == 0.0, value, 0.0).astype(BF16)
        halves[r * 64 : r * 64 + 64, 128:256] = jnp.where(high == 0.0, 0.0, value).astype(BF16)


def cold_step(part, out_ref, halves, joined):
    @pl.loop(part * 2, part * 2 + 2)
    def _(m):
        start = pl.multiple_of(m * 256, 256)
        wanted = iota((256, 128), 0) + m * 256
        total = jnp.zeros((256, 256), F32)
        for n in range(4):
            hits = [
                jnp.where(jnp.broadcast_to(joined[t : t + 1, :], (256, 128)) == wanted, 1.0, 0.0).astype(BF16)
                for t in range(n * 16, n * 16 + 16)
            ]
            total = total + jnp.dot(
                jnp.concatenate(hits, axis=1), halves[n * 2048 : n * 2048 + 2048, :], preferred_element_type=F32
            )
        out_ref[pl.ds(start, 256), :] = total[:, 0:128].astype(BF16)
        out_ref[pl.ds(start + 2048, 256), :] = total[:, 128:256].astype(BF16)


def whole_kernel(
    owner_far, row_far, table_far, index_far, hot_table_far, dense_far, weight_far, top_far, out_weight_ref,
    click_ref,
    out_ref, part_ref, other_ref,
    owner_ref, row_ref, table_ref, hot_row_ref, hot_table_ref, dense_ref, weight_ref, top_ref, tall, query_ref,
    term_turn, place_turn, rank, rows, table, want_ref, want_flat, middle, turned, safe, wide, wide_hot, held, chosen,
    passing, got_ref, near_ref, bottom_ref, square_ref, hot_value_ref, low_ref, grad_ref, terms, rows_in, stack,
    far, pairs, hidden, slope, in_ref, hot_halves, top, leaving, onward, come, halves, joined, core_buf, half,
    buf1, sum1, buf2, sum2, buf3, index_ref, wanted, term_at, place_at,
    send_sem, recv_sem, local_sem,
):
    x, y, z, core = place()
    plane = [(dx, dy) for dy in range(4) for dx in range(4)]
    partner = peer(x, y, z, 1 - core)
    zs = [peer(x, y, lax.rem(z + d, NZ), core) for d in range(1, NZ)]
    xys = [peer(lax.rem(x + dx, NX), lax.rem(y + dy, NY), z, core) for dx, dy in plane[1:]]
    xs = [xys[d - 1] for d in range(1, 4)]
    ys = [xys[4 * d - 1] for d in range(1, 4)]
    barrier = pltpu.get_barrier_semaphore()
    everyone = [partner] + zs + xys
    for device in everyone:
        pl.semaphore_signal(barrier, inc=1, device_id=device, device_id_type=MESH)
    fetched = (
        (owner_far, owner_ref), (row_far, row_ref), (table_far, table_ref), (index_far, index_ref),
        (index_far, hot_row_ref), (hot_table_far, hot_table_ref), (dense_far, dense_ref),
        (weight_far, weight_ref), (top_far, top_ref),
    )
    fetches = [pltpu.make_async_copy(src, dst, local_sem.at[3 + n]) for n, (src, dst) in enumerate(fetched)]
    for fetch in fetches:
        fetch.start()
    fetches[0].wait()
    fetches[1].wait()
    build_tables(x, y, z, owner_ref, row_ref, query_ref, term_turn, place_turn, rank, rows, table)
    staged = [
        pltpu.make_async_copy(term_turn, term_at, local_sem.at[1]),
        pltpu.make_async_copy(place_turn, place_at, local_sem.at[2]),
    ]
    for copy in staged:
        copy.start()
    pl.semaphore_wait(barrier, len(everyone))

    started = []

    def send(src, dst, device):
        index = len(started)
        copy = pltpu.make_async_remote_copy(
            src_ref=src, dst_ref=dst, send_sem=send_sem.at[index], recv_sem=recv_sem.at[index],
            device_id=device, device_id_type=MESH,
        )
        copy.start()
        started.append(copy)
        return copy

    copies = [send(query_ref.at[d], middle.at[d], zs[d - 1]) for d in range(1, 8)]
    middle[0] = query_ref[0]
    fetches[2].wait()
    widen(wide, table_ref, 4096)
    for copy in copies:
        copy.wait_recv()
    for d in range(8):
        for k in range(16):
            turned[k, d : d + 1, :] = middle[d, k : k + 1, :]
    copies = [send(turned.at[k], want_ref.at[k], xys[k - 1]) for k in range(1, 16)]
    want_ref[0] = turned[0]
    for copy in copies:
        copy.wait_recv()
    for k in range(16):
        safe[k] = jnp.clip(want_ref[k], 0, 4095)
    copy = pltpu.make_async_copy(safe, wanted, local_sem.at[0])
    copy.start()
    copy.wait()

    order = (2, 1, 3, 0)
    along = {}
    copies = []

    def collect(dy):
        @pl.loop(0, 8)
        def _(d):
            back = lax.rem(8 - d, 8)
            for tile in range(13):
                rows = []
                for e in range(16):
                    dx, p = (tile // 3, tile % 3 * 16 + e) if tile < 12 else (e // 4, EARLY + (4 - e // 4) % 4 * 4 + e % 4)
                    k = (4 - dy) % 4 * 4 + (4 - dx) % 4
                    rows.append(wide[pl.ds(wanted[k, back, p], 1), :])
                chosen[dy, d, tile * 16 : tile * 16 + 16, :] = jnp.concatenate(rows, axis=0).astype(BF16)

        for d in range(1, 8):
            along[dy, d] = send(chosen.at[dy, d], passing.at[dy, d], zs[d - 1])
        passing[dy, 0] = chosen[dy, 0]

    def pass_on(dy):
        for d in range(1, 8):
            along[dy, d].wait_recv()
        for dx in range(4):
            early = passing.at[dy, :, pl.ds(dx * EARLY, EARLY)]
            late = passing.at[dy, :, pl.ds(4 * EARLY, 16)]
            k = dy * 4 + dx
            if k:
                copies.append(send(early, got_ref.at[k, :, pl.ds(0, EARLY)], xys[k - 1]))
                copies.append(send(late, got_ref.at[k, :, pl.ds(EARLY, 16)], xys[k - 1]))
            else:
                got_ref[0, :, 0:EARLY, :] = passing[0, :, 0:EARLY, :]
                got_ref[0, :, EARLY:64, :] = passing[0, :, 4 * EARLY : 4 * EARLY + 16, :]

    for dy in order:
        collect(dy)
    for fetch in fetches[3:]:
        fetch.wait()
    widen(wide_hot, hot_table_ref, 4096)
    bottom = jnp.maximum(jnp.dot(dense_ref[...], weight_ref[...], preferred_element_type=F32), 0.0)
    bottom_ref[...] = bottom.astype(BF16)
    held[...] = bottom

    @pl.loop(0, 32)
    def _(g):
        near_ref[g, 0:16, :] = jnp.concatenate(
            [held[pl.ds(pl.multiple_of(g * 8, 8), 8), :]]
            + [wide_hot[pl.ds(index_ref[0, g * 8 + k], 1), :] for k in range(8)], axis=0
        ).astype(BF16)
        for f in range(1, 13, 2):
            rows = [wide_hot[pl.ds(index_ref[f + k // 8, g * 8 + k % 8], 1), :] for k in range(16)]
            near_ref[g, 8 + f * 8 : 24 + f * 8, :] = jnp.concatenate(rows, axis=0).astype(BF16)

    pass_on(order[0])
    pass_on(order[1])
    tall[464:512, :] = jnp.zeros((48, 1024), BF16)
    tall[0:479, :] = top_ref[...]

    @pl.loop(0, 7)
    def _(b):
        i = 4 * b + (iota((128, 512), 0) >> 5)
        j = iota((128, 512), 0) & 31
        high, low = jnp.maximum(i, j), jnp.minimum(i, j)
        source = 128 + ((high * (high - 1)) >> 1) + low
        source = jnp.where((high == low) | (high > 26), -1, source)
        pick = jnp.where(source == iota((128, 512), 1), 1.0, 0.0).astype(BF16)
        square_ref[pl.ds(pl.multiple_of(b * 128, 128), 128), :] = jnp.dot(
            pick, tall[...], preferred_element_type=F32
        ).astype(BF16)

    pass_on(order[2])
    pass_on(order[3])
    for copy in copies:
        copy.wait_recv()
    for copy in staged:
        copy.wait()
    main_kernel(
        place_at, got_ref, near_ref, bottom_ref, top_ref, square_ref, out_weight_ref, click_ref,
        hot_value_ref, low_ref, grad_ref, terms, rows_in, stack, far, pairs, hidden, slope,
    )
    for k in range(16):
        want_flat[k * 8 : k * 8 + 8, :] = want_ref[k]

    along, flat = {}, []

    def set_out(dy):
        @pl.loop(0, 8)
        def _(d):
            for tile in range(13):
                picked = []
                for e in range(16):
                    dx, p = (tile // 3, tile % 3 * 16 + e) if tile < 12 else (e // 4, EARLY + e % 4)
                    picked.append(terms[pl.ds(term_at[d, dy * 4 + dx, p], 1), :])
                leaving[dy, d, tile * 16 : tile * 16 + 16, :] = jnp.concatenate(picked, axis=0).astype(BF16)

        for d in range(1, 8):
            along[dy, d] = send(leaving.at[dy, d], onward.at[dy, d], zs[d - 1])
        onward[dy, 0] = leaving[dy, 0]

    def hand_on(dy):
        for d in range(1, 8):
            along[dy, d].wait_recv()
        for dx in range(4):
            early = onward.at[dy, :, pl.ds(dx * EARLY, EARLY)]
            late = onward.at[dy, :, pl.ds(4 * EARLY, 16)]
            k = dy * 4 + dx
            if k:
                flat.append(send(early, come.at[k, :, pl.ds(0, EARLY)], xys[k - 1]))
                flat.append(send(late, come.at[k, :, pl.ds(EARLY, 16)], xys[k - 1]))
            else:
                come[0, :, 0:EARLY, :] = onward[0, :, 0:EARLY, :]
                come[0, :, EARLY:64, :] = onward[0, :, 4 * EARLY : 4 * EARLY + 16, :]

    set_out(2)
    hot_kernel(hot_row_ref, hot_value_ref, bottom_ref, low_ref, grad_ref, in_ref, hot_halves, top)

    mine, other = core * 4096, (1 - core) * 4096
    own = (x, y)
    plan = [(which, d) for d in (1, 2, 3, 0) for which in (0, 1)]
    starts = [which * 2048 + lax.rem(own[which] + d, 4) * 512 for which, d in plan]
    over = [send(in_ref.at[rows_at(other + start, 512)], core_buf.at[rows_at(start, 512)], partner) for start in starts]
    set_out(1)
    first = {}
    for (which, d), start, copy in zip(plan, starts, over):
        copy.wait_recv()
        if d:

            @pl.loop(0, 2)
            def _(step):
                here = rows_at(start + step * 256, 256)
                value = in_ref[rows_at(mine + start + step * 256, 256), :].astype(F32)
                half[here, :] = (value + core_buf[here, :].astype(F32)).astype(BF16)

            first[which, d] = send(
                half.at[rows_at(start, 512)], buf1.at[which, d - 1], (xs, ys)[which][d - 1]
            )
    hand_on(2)
    set_out(3)
    second = {}
    for which in range(2):
        for d in range(1, 4):
            first[which, d].wait_recv()
        for d in (1, 2, 3, 0):
            piece = lax.rem(own[1 - which] + d, 4) * 128
            here = rows_at(piece, 128)
            start = which * 2048 + own[which] * 512 + piece
            total = in_ref[rows_at(mine + start, 128), :].astype(F32) + core_buf[rows_at(start, 128), :].astype(F32)
            for e in range(3):
                total += buf1[which, e, here, :].astype(F32)
            if d:
                sum1[which, here, :] = total.astype(BF16)
                second[which, d] = send(sum1.at[which, here], buf2.at[which, d - 1], (ys, xs)[which][d - 1])
            else:
                sum2[:, which] = total.reshape(8, 16, 128)
    hand_on(1)
    set_out(0)
    for which in range(2):
        for d in range(1, 4):
            second[which, d].wait_recv()
        sum2[:, which] = sum2[:, which] + (
            buf2[which, 0].astype(F32) + buf2[which, 1].astype(F32) + buf2[which, 2].astype(F32)
        ).reshape(8, 16, 128)
    third = [send(sum2.at[lax.rem(z + d, 8)], buf3.at[d - 1], zs[d - 1]) for d in range(1, 8)]
    hand_on(3)
    for copy in third:
        copy.wait_recv()
    total = sum2[z]
    for d in range(7):
        total += buf3[d]
    base = (mine + x * 512 + y * 128, mine + 2048 + y * 512 + x * 128)
    back = {}
    for which in range(2):
        block = out_ref.at[rows_at(base[which] + z * 16, 16)]
        out_ref[rows_at(base[which] + z * 16, 16), :] = total[which].astype(BF16)
        for d in range(1, 8):
            back[which, d] = send(block, block, zs[d - 1])
    hand_on(0)
    spread = {}
    for which in range(2):
        for d in range(1, 8):
            back[which, d].wait_recv()
        block = out_ref.at[rows_at(base[which], 128)]
        for d in range(1, 4):
            spread[which, d] = send(block, block, (ys, xs)[which][d - 1])
    for copy in flat:
        copy.wait_recv()
    cold_start(want_flat, come, halves, joined)
    last, across = {}, []
    for which in range(2):
        for d in range(1, 4):
            spread[which, d].wait_recv()
        block = out_ref.at[rows_at(mine + which * 2048 + own[which] * 512, 512)]
        for d in range(1, 4):
            last[which, d] = send(block, block, (xs, ys)[which][d - 1])
        across.append(send(block, block, partner))
    for n in range(4):
        cold_step(n, part_ref, halves, joined)
        for low_row in (n * 512, n * 512 + 2048):
            block = pl.ds(low_row, 512)
            across.append(send(part_ref.at[block], other_ref.at[block], partner))
        if n == 2:
            for d in range(1, 4):
                for which in range(2):
                    last[which, d].wait_recv()
                    block = out_ref.at[rows_at(mine + which * 2048 + lax.rem(own[which] + 4 - d, 4) * 512, 512)]
                    across.append(send(block, block, partner))
    for copy in across:
        copy.wait_recv()
    for copy in started:
        copy.wait_send()


def whole(owner, row, table, index, hot_table, dense, weight, top, out_weight, clicks):
    vmem = pl.BlockSpec(memory_space=pltpu.VMEM)
    return pl.pallas_call(
        whole_kernel,
        out_shape=(
            jax.ShapeDtypeStruct((8192, 128), BF16),
            jax.ShapeDtypeStruct((4096, 128), BF16),
            jax.ShapeDtypeStruct((4096, 128), BF16),
        ),
        in_specs=[pl.BlockSpec(memory_space=pl.ANY)] * 8 + [vmem] * 2,
        out_specs=(vmem,) * 3,
        scratch_shapes=[
            pltpu.VMEM((13, 256), jnp.int32),
            pltpu.VMEM((13, 256), jnp.int32),
            pltpu.VMEM((4096, 128), BF16),
            pltpu.VMEM((13, 256), jnp.int32),
            pltpu.VMEM((4096, 128), BF16),
            pltpu.VMEM((256, 256), BF16),
            pltpu.VMEM((256, 128), BF16),
            pltpu.VMEM((479, 1024), BF16),
            pltpu.VMEM((512, 1024), BF16),
            pltpu.VMEM((8, 16, 128), jnp.int32),
            pltpu.VMEM((8, 16, 128), jnp.int32),
            pltpu.VMEM((16, 256), jnp.int32),
            pltpu.VMEM((256, 128), F32),
            pltpu.VMEM((256, 128), F32),
            pltpu.VMEM((128, 128), F32),
            pltpu.VMEM((16, 8, 128), jnp.int32),
            pltpu.VMEM((128, 128), jnp.int32),
            pltpu.VMEM((8, 16, 128), jnp.int32),
            pltpu.VMEM((16, 8, 128), jnp.int32),
            pltpu.VMEM((16, 8, 128), jnp.int32),
            pltpu.VMEM((4096, 128), F32),
            pltpu.VMEM((4096, 128), F32),
            pltpu.VMEM((256, 128), F32),
            pltpu.VMEM((4, 8, 208, 128), BF16),
            pltpu.VMEM((4, 8, 208, 128), BF16),
            pltpu.VMEM((16, 8, 64, 128), BF16),
            pltpu.VMEM((32, 112, 128), BF16),
            pltpu.VMEM((256, 128), BF16),
            pltpu.VMEM((896, 1024), BF16),
            pltpu.VMEM((13, 256, 128), F32),
            pltpu.VMEM((256, 896), BF16),
            pltpu.VMEM((256, 1024), BF16),
            pltpu.VMEM((3336, 128), F32),
            pltpu.VMEM((8192, 128), F32),
            pltpu.VMEM((32, 256, 128), BF16),
            pltpu.VMEM((4, 144, 128), F32),
            pltpu.VMEM((256, 896), F32),
            pltpu.VMEM((256, 1024), F32),
            pltpu.VMEM((256, 1024), F32),
            pltpu.VMEM((8192, 128), BF16),
            pltpu.VMEM((3328, 256), BF16),
            pltpu.VMEM((480, 1024), F32),
            pltpu.VMEM((4, 8, 208, 128), BF16),
            pltpu.VMEM((4, 8, 208, 128), BF16),
            pltpu.VMEM((16, 8, 64, 128), BF16),
            pltpu.VMEM((8192, 256), BF16),
            pltpu.VMEM((64, 128), jnp.int32),
            pltpu.VMEM((4096, 128), BF16),
            pltpu.VMEM((4096, 128), BF16),
            pltpu.VMEM((2, 3, 512, 128), BF16),
            pltpu.VMEM((2, 512, 128), BF16),
            pltpu.VMEM((2, 3, 128, 128), BF16),
            pltpu.VMEM((8, 2, 16, 128), F32),
            pltpu.VMEM((7, 2, 16, 128), F32),
            pltpu.SMEM((13, 256), jnp.int32),
            pltpu.SMEM((16, 8, 128), jnp.int32),
            pltpu.SMEM((8, 16, 128), jnp.int32),
            pltpu.SMEM((16, 256), jnp.int32),
            pltpu.SemaphoreType.DMA((207,)),
            pltpu.SemaphoreType.DMA((207,)),
            pltpu.SemaphoreType.DMA((12,)),
        ],
        compiler_params=pltpu.CompilerParams(collective_id=0, has_side_effects=True, vmem_limit_bytes=VMEM_LIMIT),
        name="whole",
    )(owner, row, table, index, hot_table, dense, weight, top, out_weight, clicks)


def format_kernel(in_ref, part_ref, other_ref, hot_ref, cold_ref, top_ref):
    hot_ref[...] = in_ref[0:4096, :].astype(F32)
    cold_ref[...] = part_ref[...].astype(F32) + other_ref[...].astype(F32)
    for n in range(8):
        top_ref[:, n * 128 : n * 128 + 128] = in_ref[4096 + n * 480 : 4576 + n * 480, :].astype(F32)[0:479, :]


def format_sums(values, part, other):
    return pl.pallas_call(
        format_kernel,
        out_shape=(
            jax.ShapeDtypeStruct((4096, 128), F32),
            jax.ShapeDtypeStruct((4096, 128), F32),
            jax.ShapeDtypeStruct((479, 1024), F32),
        ),
        compiler_params=params(),
        name="format_sums",
    )(values, part, other)


def body(
    dense_feats,
    bottom_weight,
    top_weight,
    out_weight,
    hot_table,
    cold_table,
    hot_index,
    cold_owner,
    cold_row,
    clicks,
):
    sums, part, other = whole(
        cold_owner.T, cold_row.T, cold_table, hot_index.T, hot_table, dense_feats, bottom_weight, top_weight,
        out_weight.reshape(1, 1024), clicks.reshape(1, 256),
    )
    return format_sums(sums, part, other)


def solution(mesh):
    return jax.shard_map(
        body,
        mesh=mesh,
        in_specs=(
            P(("dp", "rep"), None),
            P(),
            P(),
            P(),
            P(),
            P("dp", None),
            P(("dp", "rep"), None),
            P(("dp", "rep"), None),
            P(("dp", "rep"), None),
            P(("dp", "rep")),
        ),
        out_specs=(P(), P("dp", None), P()),
        check_vma=False,
    )
```
